32 devices in a mesh: gz: 4 (over y, core), gy: 8 (over z, x).
Axes of the slice: x: 2, y: 2, z: 4, core: 2. Of those that a mesh axis runs over, the one named last changes fastest.
Arguments:
- right_side: float32 [32, 64, 1024], P('gz', 'gy'), may hold values from -5 to 5
- coefficient: float32 [32, 64, 1024], P('gz', 'gy'), may hold values from 0.5 to 4
Outputs:
- correction: float32 [32, 64, 1024], P('gz', 'gy')
- residual: float32 [32, 64, 1024], P('gz', 'gy')
The draws below stay inside these ranges and needn't reach their ends.
All inputs are finite; a program needn't handle non-finite values.
Results may differ from the reference program's by a relative error of at most 0.0003.
Values sent between devices are 32-bit elements; how exact they have to be, the bound alone decides.
No kernel may reach another device: no remote copies, remote signals or barrier semaphores. Data moves between devices by JAX's collectives and lax.ppermute only.
A program may use at most 64 MiB of HBM per device.

```python
import math
import jax
import jax.numpy as jnp
from jax import lax

NX = 1024
LEVELS = 4
NZ = 32
NY = 64


def draw_right_side(key, part):
    key = jax.random.fold_in(key, 11)
    phase_key, rough_key = jax.random.split(key)
    shape = (NZ, NY, NX)
    phases = jax.random.uniform(phase_key, (2,), jnp.float32, 0.0, 6.283185307179586)
    zpos = (jnp.arange(NZ, dtype=jnp.float32)[:, None, None] + 0.5) / NZ
    ypos = (jnp.arange(NY, dtype=jnp.float32)[None, :, None] + 0.5) / NY
    xpos = (jnp.arange(NX, dtype=jnp.float32)[None, None, :] + 0.5) / NX
    profile = 0.6 + 0.4 * jnp.sin(6.283185307179586 * ypos + phases[0])
    profile = profile * (0.8 + 0.2 * jnp.cos(6.283185307179586 * xpos + phases[1]))
    profile = profile * (0.7 + 0.3 * jnp.sin(3.141592653589793 * zpos))
    rough = jnp.clip(jax.random.normal(rough_key, shape, jnp.float32), -3.5, 3.5)
    return jnp.clip(rough + 1.5 * profile, -5.0, 5.0)


def block_scale(rng, dims, pieces, least, largest):
    factor_of, own = 1.0, jax.random.fold_in(rng, 6)
    for position, shards_of in pieces:
        draws = jnp.exp(jax.random.uniform(jax.random.fold_in(own, position), (shards_of,), jnp.float32, least / len(pieces), largest / len(pieces)))
        factor_of = factor_of * jnp.repeat(draws, dims[position] // shards_of).reshape([-1 if axis == position else 1 for axis in range(len(dims))])
    return factor_of


def setup_inputs(seed: int = 0) -> dict:
    seeds = jax.random.split(jax.random.key(seed), 3)
    right_side = draw_right_side(jax.random.fold_in(seeds[2], 71), 0)
    coefficient = jnp.clip(jnp.exp(math.log(4.0) - 2.0794415 * jax.random.uniform(seeds[1], (NZ, NY, NX), jnp.float32) ** block_scale(seeds[1], (NZ, NY, NX), ((0, 4), (1, 8)), -0.2, 0.2)), 0.5, 4.0)
    return {"right_side": right_side, "coefficient": coefficient}


def coarsen(field):
    total = field[0::2, 0::2, 0::2] + field[0::2, 0::2, 1::2]
    total = total + field[0::2, 1::2, 0::2] + field[0::2, 1::2, 1::2]
    total = total + field[1::2, 0::2, 0::2] + field[1::2, 0::2, 1::2]
    total = total + field[1::2, 1::2, 0::2] + field[1::2, 1::2, 1::2]
    return total * 0.125


def prolong(field):
    return jnp.repeat(jnp.repeat(jnp.repeat(field, 2, axis=0), 2, axis=1), 2, axis=2)


def face_terms(kpad):
    center = kpad[1:-1, 1:-1, 1:-1]
    z_minus = 0.5 * (center + kpad[:-2, 1:-1, 1:-1])
    z_plus = 0.5 * (center + kpad[2:, 1:-1, 1:-1])
    y_minus = 0.5 * (center + kpad[1:-1, :-2, 1:-1])
    y_plus = 0.5 * (center + kpad[1:-1, 2:, 1:-1])
    x_minus = 0.5 * (center + kpad[1:-1, 1:-1, :-2])
    x_plus = 0.5 * (center + kpad[1:-1, 1:-1, 2:])
    total = z_minus + z_plus + y_minus + y_plus + x_minus + x_plus
    return (z_minus, z_plus, y_minus, y_plus, x_minus, x_plus), total


def neighbour_sum(weights, upad):
    z_minus, z_plus, y_minus, y_plus, x_minus, x_plus = weights
    acc = z_minus * upad[:-2, 1:-1, 1:-1] + z_plus * upad[2:, 1:-1, 1:-1]
    acc = acc + y_minus * upad[1:-1, :-2, 1:-1] + y_plus * upad[1:-1, 2:, 1:-1]
    acc = acc + x_minus * upad[1:-1, 1:-1, :-2] + x_plus * upad[1:-1, 1:-1, 2:]
    return acc


def cycle(rhs, conduct, level):
    scale = 4.0 ** level
    weights, diag = face_terms(jnp.pad(conduct, 1))
    shape = rhs.shape
    parity = (lax.broadcasted_iota(jnp.int32, shape, 0) + lax.broadcasted_iota(jnp.int32, shape, 1)
              + lax.broadcasted_iota(jnp.int32, shape, 2) + 4) % 2

    def smooth(field, sweeps):
        for sweep in range(sweeps):
            for colour in (0, 1):
                fresh = (scale * rhs + neighbour_sum(weights, jnp.pad(field, 1))) / diag
                field = jnp.where(parity == colour, fresh, field)
        return field

    def remainder(field):
        return rhs - (diag * field - neighbour_sum(weights, jnp.pad(field, 1))) / scale

    field = jnp.zeros(shape, jnp.float32)
    if level == LEVELS - 1:
        return smooth(field, 12), None
    field = smooth(field, 2)
    error, unused = cycle(coarsen(remainder(field)), coarsen(conduct), level + 1)
    field = field + prolong(error)
    field = smooth(field, 2)
    return field, remainder(field)


def reference(right_side, coefficient):
    correction, residual = cycle(right_side, coefficient, 0)
    return correction, residual
```

```python
import jax
import jax.numpy as jnp
from jax import lax
from jax.experimental import pallas as pl
from jax.experimental.pallas import tpu as pltpu
from jax.sharding import PartitionSpec as P

LANES = 128
LINES = 18
LEVELS = 4
PAD = 5
F32 = jnp.float32
WHOLE_COARSE_CELLS = 1 << 19


def call(body, micros, outs, scratch, *args, specs=None):
    vmem = pl.BlockSpec(memory_space=pltpu.VMEM)
    return pl.pallas_call(
        body,
        out_shape=[jax.ShapeDtypeStruct(s, F32) for s in outs],
        in_specs=specs or [vmem] * len(args),
        out_specs=[vmem] * len(outs),
        scratch_shapes=[pltpu.VMEM(s, F32) for s in scratch],
        cost_estimate=pl.CostEstimate(flops=0, transcendentals=0, bytes_accessed=micros * 3_000_000),
        compiler_params=pltpu.CompilerParams(vmem_limit_bytes=56 << 20),
    )(*args)


def iota(axis, rows=8):
    return lax.broadcasted_iota(jnp.int32, (rows, LANES), axis)


def barrel(arrays, block):
    for bit in (1, 2, 4):
        high = (block & bit) != 0
        arrays = [jnp.where(high, arrays[(j + bit) % 8], arrays[j]) for j in range(8)]
    return arrays


def lane_gather(array, index):
    return jnp.take_along_axis(array, index, axis=1, mode="promise_in_bounds")


def split_lanes(tiles):
    lane = iota(1)
    block = lane // 16
    parts = [lane_gather(tiles[t], 8 * (lane % 16) + (block - t) % 8) for t in range(8)]
    mixed = barrel(parts, block)
    return [pltpu.roll(mixed[-s % 8], (-16 * s) % LANES, axis=1) for s in range(8)]


def join_lanes(arrays):
    lane = iota(1)
    block = lane // 16
    moved = [pltpu.roll(arrays[s], (16 * s) % LANES, axis=1) for s in range(8)]
    mixed = barrel(moved, block)
    return [lane_gather(mixed[-t % 8], 16 * ((lane % 8 + t) % 8) + lane // 8) for t in range(8)]


def put_coarse(message, row, s, value):
    for z in range(4):
        e, c = z % 2, (s + z + row) % 2
        message[(c * 2 + e) * 2 + s // 2, 2 * row + z // 2, :] = value[z]


REACH = ((0, 0, 4), (0, 1, 3), (1, 0, 4), (1, 1, 5))
YFACE = [(a, c, y, n) for a, c, n in REACH for y in range(n)]
ZFACE = sorted(((a, c, d) for a, c, n in REACH for d in range(1, n + 1)), key=lambda r: r[2] - REACH[2 * r[0] + r[1]][2])
CORNER = {1: (12, 0, 12), 2: (8, 16, 8), 3: (4, 12, 4), 4: (1, 24, 4)}
CORNER_ROWS = 28


def own_sides():
    return [lax.rem(lax.axis_index(axis), 2) == 0 for axis in ("gz", "gy")]


def halo_cell(side, distance):
    z = 7 + distance if side == 0 else -distance
    return z % 2, (z // 2) % 8


def pick(flag, a, b):
    return jnp.where(flag, a, b), jnp.where(flag, b, a)


def pack_kernel(f_ref, k_ref, local, ya, yb, za, zb, coarse, natural):
    zup, yup = own_sides()
    for a, ref in enumerate((f_ref, k_ref)):
        for z in range(8):
            arrays = split_lanes([ref[z, :, t * LANES : (t + 1) * LANES] for t in range(8)])
            for s in range(8):
                natural[a, s, 8 * z : 8 * z + 8, :] = arrays[s]
    for a in range(2):
        for c in range(2):
            for y in range(8):
                for e in range(2):
                    q = (e + y + c) % 2
                    for s in range(4):
                        local[a, c, y, e, s] = natural[a, 2 * s + q, pl.ds(y + 8 * e, 4, stride=16), :]
    for i, (a, c, y, n) in enumerate(YFACE):
        first, second = pick(yup, y + 8 - n, y)
        ya[i] = local[a, c, first]
        yb[i] = local[a, c, second]

    def faces(y, carry):
        for i, (a, c, d) in enumerate(ZFACE):
            high, low = 8 - d, d - 1
            for s in range(4):
                up = local[a, c, y, high % 2, s, high // 2 : high // 2 + 1]
                down = local[a, c, y, low % 2, s, low // 2 : low // 2 + 1]
                za[y, s, i : i + 1], zb[y, s, i : i + 1] = pick(zup, up, down)
        return carry

    lax.fori_loop(0, 8, faces, 0)
    for row in range(4):
        for s in range(4):
            total = None
            for c in range(2):
                for y in (2 * row, 2 * row + 1):
                    pair = local[1, c, y, 0, s] + local[1, c, y, 1, s]
                    total = pair if total is None else total + pair
            put_coarse(coarse, row, s, total * 0.125)


def relay_kernel(za, zb, ca, cb):
    zabove, yup = own_sides()
    for target, up in ((ca, yup), (cb, jnp.logical_not(yup))):
        for d, (_, at, rows) in CORNER.items():
            y = jnp.where(up, 8 - d, d - 1)
            for s in range(4):
                parts = pick(zabove, za[y, s, 0:rows], zb[y, s, 0:rows])
                for side in range(2):
                    base = (4 * side + s) * CORNER_ROWS + at
                    target[base : base + rows, :] = parts[side]


def neighbours(ref, line, e, s, q, groups, edge=None, first=None, last=None):
    rows = ref.shape[-2]
    lane = iota(1, rows)
    same = ref[line, e, s]
    if q == 0 and s == 0:
        other = jnp.where(lane == 0, 0.0, pltpu.roll(ref[line, e, groups - 1], 1, axis=1))
    elif q == 1 and s == groups - 1:
        other = jnp.where(lane == LANES - 1, 0.0, pltpu.roll(ref[line, e, 0], LANES - 1, axis=1))
    else:
        other = ref[line, e, s + (1 if q else -1)]
    zsame = ref[line, 1 - e, s]
    zother = pltpu.roll(zsame, 1 if e == 0 else rows - 1, axis=0)
    if edge is not None:
        zother = edge(zother, line, e, s)
    return (same + other) + (zsame + zother) + (ref[line - 1, e, s] + ref[line + 1, e, s])


def closed(zother, line, e, s):
    rows = zother.shape[0]
    return jnp.where(iota(0, rows) == (0 if e == 0 else rows - 1), 0.0, zother)


def over_lines(low, high, offset, visit, lines=4):
    steps, rest = divmod(high - low + 1, lines)

    def step(i, carry):
        for j in range(lines):
            visit(low + offset + j + lines * i, (low + j) % 2)
        return carry

    lax.fori_loop(0, steps, step, 0)
    for y in range(high + 1 - rest, high + 1):
        visit(y + offset, y % 2)


def diagonal(k, kother, line, e, s, q, groups, edge=None):
    centre = k[line, e, s]
    return centre, 6.0 * centre + neighbours(kother, line, e, s, q, groups, edge)


def down_kernel(
    local, ya, yb, za, zb, ca, cb,
    k, g, fs, half, ub, kx, zc, zd, coarse,
    f, ur, vr, vb,
):
    zabove, yabove = own_sides()
    zup = zabove
    blank = jnp.zeros((8, LANES), F32)
    for c in range(2):
        for line in (*range(PAD), *range(PAD + 8, LINES)):
            for e in range(2):
                for s in range(4):
                    k[c, line, e, s] = blank
                    f[c, line, e, s] = blank
    both = (f, k)

    def assemble(y, carry):
        for e in range(2):
            for s in range(4):
                f[1, PAD + y, e, s] = blank
                for a in range(2):
                    for c in range(2):
                        both[a][c, PAD + y, e, s, 0:4] = local[a, c, y, e, s]
        for s in range(4):
            for side, part in enumerate(pick(zabove, za[y, s], zb[y, s])):
                for i, (a, c, d) in enumerate(ZFACE):
                    e, row = halo_cell(side, d)
                    if d == 5:
                        kx[side, y, s : s + 1] = part[i : i + 1]
                    else:
                        both[a][c, PAD + y, e, s, row : row + 1] = part[i : i + 1]
        return carry

    lax.fori_loop(0, 8, assemble, 0)
    for i, (a, c, y, n) in enumerate(YFACE):
        first, second = pick(yabove, PAD + y + 8, PAD + y - n)
        for e in range(2):
            for s in range(4):
                both[a][c, first, e, s, 0:4] = ya[i, e, s]
                both[a][c, second, e, s, 0:4] = yb[i, e, s]
    for d, (count, at, _) in CORNER.items():
        for message, line in zip((ca, cb), pick(yabove, PAD + 7 + d, PAD - d)):
            for side in range(2):
                for i, (a, c, dz) in enumerate(ZFACE[:count]):
                    e, row = halo_cell(side, dz)
                    for s in range(4):
                        base = (4 * side + s) * CORNER_ROWS + at + i
                        both[a][c, line, e, s, row : row + 1] = message[base : base + 1, :]

    rows = iota(0)

    def far(zother, line, e, s):
        beyond = kx[1 - e, line - PAD, s : s + 1]
        return jnp.where(rows == (6 if e == 0 else 5), jnp.broadcast_to(beyond, (8, LANES)), zother)

    def prepare(c, line, parity, edge, keep):
        for e in range(2):
            q = (e + parity + c) % 2
            for s in range(4):
                centre, total = diagonal(k.at[c], k.at[1 - c], line, e, s, q, 4, edge)
                inside = centre != 0.0
                scale = jnp.where(inside, 1.0 / jnp.where(inside, total, 1.0), 0.0)
                start = 2.0 * f[c, line, e, s] * scale
                g[c, line, e, s] = scale
                fs[c, line, e, s] = start
                if keep:
                    half[line - PAD, e, s] = 0.5 * total
                if c == 0:
                    ur[line, e, s] = start
                    vr[line, e, s] = centre * start

    over_lines(-4, -1, PAD, lambda line, parity: prepare(0, line, parity, None, False))
    over_lines(8, 11, PAD, lambda line, parity: prepare(0, line, parity, None, False))
    over_lines(0, 7, PAD, lambda line, parity: prepare(0, line, parity, far, True))
    over_lines(-3, 10, PAD, lambda line, parity: prepare(1, line, parity, None, False))

    def relax(c, low, high):
        sweep(c, low, high, k, g, fs, (ur, ub), (vr, vb))

    relax(1, -3, 10)
    relax(0, -2, 9)
    relax(1, -1, 8)

    for row in range(4):
        for s in range(4):
            total = None
            for y in (2 * row, 2 * row + 1):
                for e in range(2):
                    line = PAD + y
                    value = red_residual(line, y % 2, e, s, k, g, fs, half, ur, ub, vb)
                    total = value if total is None else total + value
            put_coarse(coarse, row, s, total * 0.125)

    for y in range(8):
        for s in range(4):
            for d in range(1, 6):
                at, high, low = (4 * y + s) * 5 + d - 1, 8 - d, d - 1
                up = ub[PAD + y, high % 2, s, high // 2 : high // 2 + 1]
                down = ub[PAD + y, low % 2, s, low // 2 : low // 2 + 1]
                zc[at : at + 1, :], zd[at : at + 1, :] = pick(zup, up, down)


def widen_kernel(ub, zc, zd, wide, yc, yd):
    zabove, yup = own_sides()
    for y in range(8):
        for s in range(4):
            at = (4 * y + s) * 5
            for e in range(2):
                wide[y, e, s, 0:4] = ub[PAD + y, e, s, 0:4]
            for side, part in enumerate(pick(zabove, zc[at : at + 4, :], zd[at : at + 4, :])):
                for d in range(1, 5):
                    e, row = halo_cell(side, d)
                    wide[y, e, s, row : row + 1] = part[d - 1 : d]
    first, second = pick(yup, 3, 0)
    for i in range(5):
        yc[i] = wide[first + i]
        yd[i] = wide[second + i]


def sweep(c, low, high, k, g, fs, u, v, edges=(None, None)):
    def visit(line, parity):
        for e in range(2):
            q = (e + parity + c) % 2
            for s in range(4):
                near = neighbours(u[1 - c], line, e, s, q, 4, edges[0])
                flow = neighbours(v[1 - c], line, e, s, q, 4, edges[1])
                centre = k[c, line, e, s]
                value = fs[c, line, e, s] + g[c, line, e, s] * (centre * near + flow)
                u[c][line, e, s] = value
                v[c][line, e, s] = centre * value

    over_lines(low, high, PAD, visit)


def red_residual(line, parity, e, s, k, g, fs, half, ur, ub, vb):
    q = (e + parity) % 2
    near = neighbours(ub, line, e, s, q, 4)
    flow = neighbours(vb, line, e, s, q, 4)
    fresh = fs[0, line, e, s] + g[0, line, e, s] * (k[0, line, e, s] * near + flow)
    return half[line - PAD, e, s] * (fresh - ur[line, e, s])


def up_kernel(
    k, g, fs, half, wide, kx, yc, yd, zc, zd, error, errorx,
    correction, residual,
    ub, ur, vb, vr, ux, vx, natural,
):
    zabove, yabove = own_sides()
    ub[PAD : PAD + 8] = wide[...]
    first, second = pick(yabove, PAD + 8, 0)
    for i in range(5):
        ub[first + i] = yc[i]
        ub[second + i] = yd[i]
    for y in range(8):
        for s in range(4):
            at = (4 * y + s) * 5 + 4
            for side, part in enumerate(pick(zabove, zc[at : at + 1, :], zd[at : at + 1, :])):
                beyond = kx[side, y, s : s + 1]
                value = part + errorx[side, y // 2, s : s + 1]
                value = jnp.where(beyond != 0.0, value, 0.0)
                ux[side, y, s : s + 1] = value
                vx[side, y, s : s + 1] = beyond * value

    def add(line, parity):
        for e in range(2):
            for s in range(4):
                centre = k[1, line, e, s]
                value = ub[line, e, s] + error[(line + 1) // 2, s]
                value = jnp.where(centre != 0.0, value, 0.0)
                ub[line, e, s] = value
                vb[line, e, s] = centre * value

    over_lines(-5, 12, PAD, add)

    rows = iota(0)

    def far(ref):
        def edge(zother, line, e, s):
            beyond = ref[1 - e, line - PAD, s : s + 1]
            return jnp.where(rows == (6 if e == 0 else 5), jnp.broadcast_to(beyond, (8, LANES)), zother)

        return edge

    u, v = (ur, ub), (vr, vb)
    sweep(0, -4, -1, k, g, fs, u, v)
    sweep(0, 8, 11, k, g, fs, u, v)
    sweep(0, 0, 7, k, g, fs, u, v, (far(ux), far(vx)))
    sweep(1, -3, 10, k, g, fs, u, v)
    sweep(0, -2, 9, k, g, fs, u, v)
    sweep(1, -1, 8, k, g, fs, u, v)

    quiet = jnp.zeros((4, LANES), F32)
    for y in range(8):
        for e in range(2):
            at = pl.ds(y + 8 * e, 4, stride=16)
            q = (e + y) % 2
            for s in range(4):
                value = red_residual(PAD + y, y % 2, e, s, k, g, fs, half, ur, ub, vb)
                natural[1, 2 * s + q, at, :] = value[0:4]
                natural[1, 2 * s + 1 - q, at, :] = quiet
                natural[0, 2 * s + q, at, :] = ur[PAD + y, e, s, 0:4]
                natural[0, 2 * s + 1 - q, at, :] = ub[PAD + y, e, s, 0:4]
    for a, out in enumerate((correction, residual)):
        for z in range(8):
            tiles = join_lanes([natural[a, s, 8 * z : 8 * z + 8, :] for s in range(8)])
            for t in range(8):
                out[z, :, t * LANES : (t + 1) * LANES] = tiles[t]


def shifted(value, step, axis):
    size = value.shape[axis]
    where = iota(axis, value.shape[0])
    moved = pltpu.roll(value, -step % size, axis=axis)
    return jnp.where((where >= size - step) if step > 0 else (where < -step), 0.0, moved)


def coarse_kernel(nz, ny):
    height, depth = 4 * ny, 2 * nz
    height2, height3 = height // 2, height // 4

    def body(
        fmine, ftheirs, kmine, ktheirs, error, errorx,
        f, k, g, fs, half, ur, ub, vr, vb, f2, k2, fc, kc, gc, sc, uc, vc, hc, w3, f3,
    ):
        u, v = (ur, ub), (vr, vb)
        zplace, yplace = lax.axis_index("gz"), lax.axis_index("gy")
        swaps = swap_steps(nz, ny)[:-1]

        def slot(i, j):
            apart = (zplace * ny + yplace) ^ (i * ny + j)
            return sum(((apart >> step) & 1) << bit for bit, step in enumerate(swaps))

        def spread(odd):
            def visit(j, carry):
                order = [slot(i, j) for i in range(nz)]
                for sources, target in (((fmine, ftheirs), f), ((kmine, ktheirs), k)):
                    for m in range(8):
                        pieces = [sources[(i + odd) % 2][order[i], m] for i in range(nz)]
                        for row in range(4):
                            whole = jnp.concatenate([p[2 * row : 2 * row + 2] for p in pieces], axis=0)
                            target[m // 4, 1 + 4 * j + row, m // 2 % 2, m % 2] = whole
                return carry

            lax.fori_loop(0, ny, visit, 0)

        for odd in range(2):
            pl.when(lax.rem(zplace, 2) == odd)(lambda odd=odd: spread(odd))
        blank = jnp.zeros((depth, LANES), F32)
        for line in (0, height + 1):
            for e in range(2):
                for s in range(2):
                    for c in range(2):
                        k[c, line, e, s] = blank
                        u[c][line, e, s] = blank
                        v[c][line, e, s] = blank

        def prepare(c):
            def visit(line, parity):
                for e in range(2):
                    for s in range(2):
                        centre, total = diagonal(k.at[c], k.at[1 - c], line, e, s, (e + parity + c) % 2, 2, closed)
                        scale = 1.0 / total
                        start = 8.0 * f[c, line, e, s] * scale
                        g[c, line, e, s] = scale
                        fs[c, line, e, s] = start
                        if c == 0:
                            half[line, e, s] = 0.125 * total
                            ur[line, e, s] = start
                            vr[line, e, s] = centre * start

            over_lines(0, height - 1, 1, visit, 8)

        def fresh(c, line, parity, e, s):
            q = (e + parity + c) % 2
            near = neighbours(u[1 - c], line, e, s, q, 2, closed)
            flow = neighbours(v[1 - c], line, e, s, q, 2, closed)
            return fs[c, line, e, s] + g[c, line, e, s] * (k[c, line, e, s] * near + flow)

        def relax(c):
            def visit(line, parity):
                for e in range(2):
                    for s in range(2):
                        value = fresh(c, line, parity, e, s)
                        u[c][line, e, s] = value
                        v[c][line, e, s] = k[c, line, e, s] * value

            over_lines(0, height - 1, 1, visit, 8)

        prepare(0)
        prepare(1)
        relax(1)
        relax(0)
        relax(1)

        def restrict(i, carry):
            for s in range(2):
                value, conduct = None, None
                for j in range(2):
                    line = 1 + 2 * i + j
                    for e in range(2):
                        part = half[line, e, s] * (fresh(0, line, j, e, s) - ur[line, e, s])
                        value = part if value is None else value + part
                        part = k[0, line, e, s] + k[1, line, e, s]
                        conduct = part if conduct is None else conduct + part
                f2[s, i] = value * 0.125
                k2[s, i] = conduct * 0.125
            return carry

        lax.fori_loop(0, height2, restrict, 0)

        even = iota(0, depth) % 2 == 0

        def q_is_zero(c, y):
            return even if (y + c) % 2 == 0 else jnp.logical_not(even)

        def coloured(pair, c, y):
            return jnp.where(q_is_zero(c, y), pair[0], pair[1])

        def around(ref, c, y):
            mid = ref[1 + y]
            other = jnp.where(q_is_zero(c, y), shifted(mid, -1, 1), shifted(mid, 1, 1))
            return (mid + other) + (shifted(mid, -1, 0) + shifted(mid, 1, 0)) + (ref[y] + ref[y + 2])

        for c in range(2):
            for line in (0, height2 + 1):
                kc[c, line] = blank
                uc[c, line] = blank
                vc[c, line] = blank
            for y in range(height2):
                kc[c, 1 + y] = coloured((k2[0, y], k2[1, y]), c, y)
                fc[c, y] = coloured((f2[0, y], f2[1, y]), c, y)
        for c in range(2):
            for y in range(height2):
                centre = kc[c, 1 + y]
                total = 6.0 * centre + around(kc.at[1 - c], c, y)
                scale = 1.0 / total
                start = 32.0 * fc[c, y] * scale
                gc[c, y] = scale
                sc[c, y] = start
                if c == 0:
                    hc[y] = total * (0.5 / 16.0)
                    uc[0, 1 + y] = start
                    vc[0, 1 + y] = centre * start

        def fresh2(c, y):
            flow = kc[c, 1 + y] * around(uc.at[1 - c], c, y) + around(vc.at[1 - c], c, y)
            return sc[c, y] + gc[c, y] * flow

        def relax2(c):
            for y in range(height2):
                value = fresh2(c, y)
                uc[c, 1 + y] = value
                vc[c, 1 + y] = kc[c, 1 + y] * value

        relax2(1)
        relax2(0)
        relax2(1)

        def paired(a, b):
            total = (a + b) * 0.125
            return jnp.where(even, total + pltpu.roll(total, depth - 1, axis=0), 0.0)

        conduct = []
        right = []
        for y in range(height3):
            parts = [hc[2 * y + j] * (fresh2(0, 2 * y + j) - uc[0, 1 + 2 * y + j]) for j in range(2)]
            right.append(paired(*parts))
            parts = [kc[0, 1 + 2 * y + j] + kc[1, 1 + 2 * y + j] for j in range(2)]
            conduct.append(paired(*parts))
        moves = ((-2, 0), (2, 0), (-1, 1), (1, 1))
        for y in range(height3):
            centre = conduct[y]
            beside = [shifted(centre, step, axis) for step, axis in moves]
            beside.append(conduct[y - 1] if y else jnp.zeros_like(centre))
            beside.append(conduct[y + 1] if y + 1 < height3 else jnp.zeros_like(centre))
            total = 6.0 * centre
            for part in beside:
                total = total + part
            scale = jnp.where(even, 1.0 / jnp.where(even, total, 1.0), 0.0)
            f3[y] = 128.0 * right[y] * scale
            lane, row = iota(1, depth), iota(0, depth)
            open_faces = (row >= 2, row < depth - 2, lane >= 1, lane < LANES - 1)
            for i in range(6):
                weight = (centre + beside[i]) * scale
                w3[y, i] = jnp.where(open_faces[i], weight, 0.0) if i < 4 else weight
        mixed = (iota(0, depth) // 2 + iota(1, depth)) % 2

        def relax3(c, field):
            result = []
            for y in range(height3):
                mid = field[y]
                value = f3[y]
                for i, (step, axis) in enumerate(moves):
                    value = value + w3[y, i] * pltpu.roll(mid, -step % mid.shape[axis], axis=axis)
                if y:
                    value = value + w3[y, 4] * field[y - 1]
                if y + 1 < height3:
                    value = value + w3[y, 5] * field[y + 1]
                result.append(jnp.where(mixed == (y + c) % 2, value, mid))
            return result

        def two_colours(_, field):
            return tuple(relax3(1, relax3(0, list(field))))

        field = lax.fori_loop(0, 12, two_colours, (blank,) * height3)

        for y in range(height2):
            coarse = field[y // 2]
            value = uc[1, 1 + y] + (coarse + pltpu.roll(coarse, 1, axis=0))
            uc[1, 1 + y] = value
            vc[1, 1 + y] = kc[1, 1 + y] * value
        for c in (0, 1, 0, 1):
            relax2(c)

        for y in range(height2):
            zero = q_is_zero(0, y)
            red, black = uc[0, 1 + y], uc[1, 1 + y]
            f2[0, y] = jnp.where(zero, red, black)
            f2[1, y] = jnp.where(zero, black, red)

        def add(line, parity):
            for e in range(2):
                for s in range(2):
                    value = ub[line, e, s] + f2[s, (line - 1) // 2]
                    ub[line, e, s] = value
                    vb[line, e, s] = k[1, line, e, s] * value

        over_lines(0, height - 1, 1, add, 8)
        for c in (0, 1, 0, 1):
            relax(c)

        for j in range(-3, 7):
            line = 1 + jnp.clip(4 * yplace + j, 0, height - 1)
            for t in range(-3, 7):
                e = t % 2
                at = pl.ds(jnp.clip(2 * zplace + t // 2, 0, depth - 1), 1)
                for s in range(4):
                    row = u[(s + e + j) % 2][line, e, s // 2, at, :]
                    if -2 <= t <= 5:
                        error[j + 3, s, t % 8 : t % 8 + 1, :] = row
                    elif 0 <= j < 8 // 2:
                        errorx[1 if t < 0 else 0, j, s : s + 1, :] = row

    lines, lines2 = (height + 2, 2, 2, depth, LANES), (height2 + 2, depth, LANES)
    flat2 = (2, height2, depth, LANES)
    scratch = [(2, *lines)] * 4 + [lines] * 5 + [flat2, flat2, flat2, (2, *lines2), flat2, flat2]
    scratch += [(2, *lines2), (2, *lines2), flat2[1:], (height3, 6, depth, LANES), (height3, depth, LANES)]
    return body, scratch


def swap_steps(nz, ny):
    ybits, zbits = ny.bit_length() - 1, nz.bit_length() - 1
    return [*range(ybits - 1, -1, -1), *range(ybits + zbits - 1, ybits - 1, -1)]


def swap(block, step, nz, ny):
    return lax.ppermute(block, ("gz", "gy"), [(i, i ^ (1 << step)) for i in range(nz * ny)])


def swapped(block, step, nz, ny):
    return jnp.concatenate([block, swap(block, step, nz, ny)])


def solve_coarse(fmine, ftheirs, kmine, ktheirs, nz, ny):
    body, scratch = coarse_kernel(nz, ny)
    outs = ((10, 4, 8, LANES), (2, 4, 4, LANES))
    return call(body, 11, outs, scratch, fmine, ftheirs, kmine, ktheirs)


def extended(array, sides, width):
    for axis, dim in sides:
        size, length = (lax.axis_size(axis), array.shape[dim])
        up = [(i, (i + 1) % size) for i in range(size - 1)]
        down = [(j, i) for i, j in up]
        last = lax.slice_in_dim(array, length - width, length, axis=dim)
        initial = lax.slice_in_dim(array, 0, width, axis=dim)
        before = lax.ppermute(last, axis, up)
        after = lax.ppermute(initial, axis, down)
        array = jnp.concatenate([before, array, after], axis=dim)
    return array


def coarsen(field):
    total = field[0::2, 0::2, 0::2] + field[0::2, 0::2, 1::2]
    total = total + field[0::2, 1::2, 0::2] + field[0::2, 1::2, 1::2]
    total = total + field[1::2, 0::2, 0::2] + field[1::2, 0::2, 1::2]
    total = total + field[1::2, 1::2, 0::2] + field[1::2, 1::2, 1::2]
    return total * 0.125


def prolong(field):
    return jnp.repeat(jnp.repeat(jnp.repeat(field, 2, axis=0), 2, axis=1), 2, axis=2)


def face_terms(kpad):
    center = kpad[1:-1, 1:-1, 1:-1]
    z_minus = 0.5 * (center + kpad[:-2, 1:-1, 1:-1])
    z_plus = 0.5 * (center + kpad[2:, 1:-1, 1:-1])
    y_minus = 0.5 * (center + kpad[1:-1, :-2, 1:-1])
    y_plus = 0.5 * (center + kpad[1:-1, 2:, 1:-1])
    x_minus = 0.5 * (center + kpad[1:-1, 1:-1, :-2])
    x_plus = 0.5 * (center + kpad[1:-1, 1:-1, 2:])
    total = z_minus + z_plus + y_minus + y_plus + x_minus + x_plus
    return ((z_minus, z_plus, y_minus, y_plus, x_minus, x_plus), total)


def neighbour_sum(weights, upad):
    z_minus, z_plus, y_minus, y_plus, x_minus, x_plus = weights
    acc = z_minus * upad[:-2, 1:-1, 1:-1] + z_plus * upad[2:, 1:-1, 1:-1]
    acc = acc + y_minus * upad[1:-1, :-2, 1:-1] + y_plus * upad[1:-1, 2:, 1:-1]
    acc = acc + x_minus * upad[1:-1, 1:-1, :-2] + x_plus * upad[1:-1, 1:-1, 2:]
    return acc


def extend(field, layout):
    if layout == "column":
        wider = extended(field, (("gy", 1),), 1)
        wider = jnp.pad(wider, ((1, 1), (0, 0), (0, 0)))
    else:
        wider = extended(field, (("gz", 0), ("gy", 1)), 1)
    return jnp.pad(wider, ((0, 0), (0, 0), (1, 1)))


def region_masks(shape, z_start, y_start):
    zpos = lax.broadcasted_iota(jnp.int32, shape, 0) + z_start
    ypos = lax.broadcasted_iota(jnp.int32, shape, 1) + y_start
    xpos = lax.broadcasted_iota(jnp.int32, shape, 2)
    return (zpos + ypos + xpos + 4) % 2


def cycle(rhs, conduct, level, layout, z_start, y_start, z_total, y_total):
    scale = 4.0**level
    weights, total = face_terms(extend(conduct, layout))
    parity = region_masks(rhs.shape, z_start, y_start)
    first = parity == 0
    second = parity == 1

    def relax(field, colour):
        fresh = (scale * rhs + neighbour_sum(weights, extend(field, layout))) / total
        return jnp.where(colour, fresh, field)

    def smooth(field, sweeps):
        for sweep in range(sweeps):
            for colour in (first, second):
                field = relax(field, colour)
        return field

    def remainder(field):
        return rhs - (total * field - neighbour_sum(weights, extend(field, layout))) / scale

    field = jnp.zeros(rhs.shape, jnp.float32)
    if level == LEVELS - 1:
        return (smooth(field, 12), None)
    field = smooth(field, 2)
    rhs_next = coarsen(remainder(field))
    conduct_next = coarsen(conduct)
    joined = layout == "split" and level == 1
    if joined:
        local_depth = rhs_next.shape[0]
        rhs_next, conduct_next = (
            lax.all_gather(rhs_next, "gz", axis=0, tiled=True),
            lax.all_gather(conduct_next, "gz", axis=0, tiled=True),
        )
        error, unused = cycle(
            rhs_next, conduct_next, level + 1, "column", 0, y_start // 2, z_total // 2, y_total // 2
        )
        error = lax.dynamic_slice_in_dim(error, lax.axis_index("gz") * local_depth, local_depth, 0)
    else:
        error, unused = cycle(
            rhs_next,
            conduct_next,
            level + 1,
            layout,
            z_start // 2,
            y_start // 2,
            z_total // 2,
            y_total // 2,
        )
    field = field + prolong(error)
    field = smooth(field, 2)
    return (field, remainder(field))


def natural_coarse(message):
    packed = message.reshape(2, 2, 2, 4, 2, LANES)
    parity = (jnp.arange(2)[:, None, None, None, None] + jnp.arange(4)[None, None, :, None, None]) % 2 == 0
    even = jnp.where(parity, packed[0], packed[1])
    odd = jnp.where(parity, packed[1], packed[0])
    both = jnp.stack([even, odd])
    return both.transpose(4, 1, 3, 5, 2, 0).reshape(4, 4, 4 * LANES)


def solve_coarse_spread(message, kmessage, nz, ny):
    z_start, y_start = 4 * lax.axis_index("gz"), 4 * lax.axis_index("gy")
    field, unused = cycle(
        natural_coarse(message), natural_coarse(kmessage), 1, "split", z_start, y_start, 4 * nz, 4 * ny
    )
    wide = extended(field, (("gz", 0), ("gy", 1)), 3).reshape(10, 10, LANES, 4).transpose(1, 3, 0, 2)
    error = jnp.concatenate([wide[:, :, 3:9], wide[:, :, 1:3]], axis=2)
    return error, jnp.stack([wide[3:7, :, 9], wide[3:7, :, 0]])


def exchange(first, second, axis):
    size = lax.axis_size(axis)
    results = []
    for message, start in ((first, 0), (second, 1)):
        pairs = [(i, i + 1) for i in range(start, size - 1, 2)]
        results.append(lax.ppermute(message, axis, pairs + [(j, i) for i, j in pairs]))
    return results


def on_device(right_side, coefficient):
    nz, ny = lax.axis_size("gz"), lax.axis_size("gy")
    assert right_side.shape == (8, 8, 8 * LANES)
    cells = (2, 2, 8, 2, 4, 4, LANES)
    yface, zface = (16, 2, 4, 4, LANES), (8, 4, 16, LANES)
    coarse = (8, 8, LANES)
    outs = (cells, yface, yface, zface, zface, coarse)
    packed = call(pack_kernel, 3, outs, [(2, 8, 64, LANES)], right_side, coefficient)
    local, ya, yb, za, zb, kmessage = packed
    coarse_cells = 8 * 8 * LANES
    whole = nz * ny * coarse_cells <= WHOLE_COARSE_CELLS and nz & (nz - 1) == 0 and ny & (ny - 1) == 0
    swaps = swap_steps(nz, ny)
    kall = kmessage[None]
    ya, yb = exchange(ya, yb, "gy")
    za, zb = exchange(za, zb, "gz")
    relayed = (8 * CORNER_ROWS, LANES)
    ca, cb = exchange(*call(relay_kernel, 2, (relayed, relayed), [], za, zb), "gy")
    if whole:
        kall = swapped(kall, swaps[0], nz, ny)
        kall = swapped(kall, swaps[1], nz, ny)
        ca, cb, kall = lax.optimization_barrier((ca, cb, kall))
        for step in swaps[2:-1]:
            kall = swapped(kall, step, nz, ny)
        ktheirs = swap(kall, swaps[-1], nz, ny)
    lines, zface = (LINES, 2, 4, 8, LANES), (160, LANES)
    outs = ((2, *lines), (2, *lines), (2, *lines), (8, *lines[1:]), lines, (2, 8, 4, LANES), zface, zface, coarse)
    scratch = [(2, *lines), lines, lines, lines]
    k, g, fs, half, ub, kx, zc, zd, message = call(down_kernel, 6, outs, scratch, local, ya, yb, za, zb, ca, cb)
    fall, half_way = message[None], len(swaps) // 2
    zc, zd = exchange(zc, zd, "gz")
    if whole:
        for step in swaps[:half_way]:
            fall = swapped(fall, step, nz, ny)
        fall, zc, zd = lax.optimization_barrier((fall, zc, zd))
    yface = (5, *lines[1:])
    wide, yc, yd = call(widen_kernel, 2, ((8, *lines[1:]), yface, yface), [], ub, zc, zd)
    if whole:
        fall = swapped(fall, swaps[half_way], nz, ny)
        fall, yc, yd = lax.optimization_barrier((fall, yc, yd))
    yc, yd = exchange(yc, yd, "gy")
    if whole:
        for step in swaps[half_way + 1 : -1]:
            fall = swapped(fall, step, nz, ny)
        fall, yc, yd = lax.optimization_barrier((fall, yc, yd))
        ftheirs = swap(fall, swaps[-1], nz, ny)
        error, errorx = solve_coarse(fall, ftheirs, kall, ktheirs, nz, ny)
    else:
        error, errorx = solve_coarse_spread(message, kmessage, nz, ny)
    block = (8, 8, 8 * LANES)
    scratch = [lines] * 4 + [(2, 8, 4, LANES)] * 2 + [(2, 8, 64, LANES)]
    return call(up_kernel, 6, (block, block), scratch, k, g, fs, half, wide, kx, yc, yd, zc, zd, error, errorx)


def solution(mesh):
    spec = P("gz", "gy", None)
    return jax.shard_map(
        on_device, mesh=mesh, in_specs=(spec, spec), out_specs=(spec, spec), check_vma=False
    )
```

```python
import jax
import jax.numpy as jnp
from jax import lax
from jax.experimental import pallas as pl
from jax.experimental.pallas import tpu as pltpu
from jax.sharding import PartitionSpec as P

LANES = 128
LINES = 18
LEVELS = 4
PAD = 5
F32 = jnp.float32
WHOLE_COARSE_CELLS = 1 << 19


def call(body, micros, outs, scratch, *args, specs=None):
    vmem = pl.BlockSpec(memory_space=pltpu.VMEM)
    return pl.pallas_call(
        body,
        out_shape=[jax.ShapeDtypeStruct(s, F32) for s in outs],
        in_specs=specs or [vmem] * len(args),
        out_specs=[vmem] * len(outs),
        scratch_shapes=[pltpu.VMEM(s, F32) if isinstance(s, tuple) else s for s in scratch],
        cost_estimate=pl.CostEstimate(flops=0, transcendentals=0, bytes_accessed=micros * 3_000_000),
        compiler_params=pltpu.CompilerParams(vmem_limit_bytes=56 << 20),
    )(*args)


def iota(axis, rows=8):
    return lax.broadcasted_iota(jnp.int32, (rows, LANES), axis)


def barrel(arrays, block):
    for bit in (1, 2, 4):
        high = (block & bit) != 0
        arrays = [jnp.where(high, arrays[(j + bit) % 8], arrays[j]) for j in range(8)]
    return arrays


def lane_gather(array, index):
    return jnp.take_along_axis(array, index, axis=1, mode="promise_in_bounds")


def split_lanes(tiles):
    lane = iota(1)
    block = lane // 16
    parts = [lane_gather(tiles[t], 8 * (lane % 16) + (block - t) % 8) for t in range(8)]
    mixed = barrel(parts, block)
    return [pltpu.roll(mixed[-s % 8], (-16 * s) % LANES, axis=1) for s in range(8)]


def join_lanes(arrays):
    lane = iota(1)
    block = lane // 16
    moved = [pltpu.roll(arrays[s], (16 * s) % LANES, axis=1) for s in range(8)]
    mixed = barrel(moved, block)
    return [lane_gather(mixed[-t % 8], 16 * ((lane % 8 + t) % 8) + lane // 8) for t in range(8)]


def put_coarse(message, row, s, value):
    for z in range(4):
        e, c = z % 2, (s + z + row) % 2
        message[(c * 2 + e) * 2 + s // 2, 2 * row + z // 2, :] = value[z]


REACH = ((0, 0, 4), (0, 1, 3), (1, 0, 4), (1, 1, 5))
YFACE = [(a, c, y, n) for a, c, n in REACH for y in range(n)]
ZFACE = sorted(((a, c, d) for a, c, n in REACH for d in range(1, n + 1)), key=lambda r: r[2] - REACH[2 * r[0] + r[1]][2])
CORNER = {1: (12, 0, 12), 2: (8, 16, 8), 3: (4, 12, 4), 4: (1, 24, 4)}
CORNER_ROWS = 28


def own_sides():
    return [lax.rem(lax.axis_index(axis), 2) == 0 for axis in ("gz", "gy")]


def halo_cell(side, distance):
    z = 7 + distance if side == 0 else -distance
    return z % 2, (z // 2) % 8


def pick(flag, a, b):
    return jnp.where(flag, a, b), jnp.where(flag, b, a)


def pack_kernel(f_ref, k_ref, local, ya, yb, natural):
    _, yup = own_sides()
    for a, ref in enumerate((f_ref, k_ref)):
        for z in range(8):
            arrays = split_lanes([ref[z, :, t * LANES : (t + 1) * LANES] for t in range(8)])
            for s in range(8):
                natural[a, s, 8 * z : 8 * z + 8, :] = arrays[s]
    for a in range(2):
        for c in range(2):
            for y in range(8):
                for e in range(2):
                    q = (e + y + c) % 2
                    for s in range(4):
                        local[a, c, y, e, s] = natural[a, 2 * s + q, pl.ds(y + 8 * e, 4, stride=16), :]
    for i, (a, c, y, n) in enumerate(YFACE):
        first, second = pick(yup, y + 8 - n, y)
        ya[i] = local[a, c, first]
        yb[i] = local[a, c, second]


def zpack_kernel(local, za, zb, coarse):
    zup, _ = own_sides()

    def faces(y, carry):
        for i, (a, c, d) in enumerate(ZFACE):
            high, low = 8 - d, d - 1
            for s in range(4):
                up = local[a, c, y, high % 2, s, high // 2 : high // 2 + 1]
                down = local[a, c, y, low % 2, s, low // 2 : low // 2 + 1]
                za[y, s, i : i + 1], zb[y, s, i : i + 1] = pick(zup, up, down)
        return carry

    lax.fori_loop(0, 8, faces, 0)
    for row in range(4):
        for s in range(4):
            total = None
            for c in range(2):
                for y in (2 * row, 2 * row + 1):
                    pair = local[1, c, y, 0, s] + local[1, c, y, 1, s]
                    total = pair if total is None else total + pair
            put_coarse(coarse, row, s, total * 0.125)


def relay_kernel(za_far, zb_far, ca, cb, za, zb, sem):
    zabove, yup = own_sides()
    copies = [pltpu.make_async_copy(*pair, sem.at[i]) for i, pair in enumerate(((za_far, za), (zb_far, zb)))]
    for copy in copies:
        copy.start()
    for copy in copies:
        copy.wait()
    for target, up in ((ca, yup), (cb, jnp.logical_not(yup))):
        for d, (_, at, rows) in CORNER.items():
            y = jnp.where(up, 8 - d, d - 1)
            for s in range(4):
                parts = pick(zabove, za[y, s, 0:rows], zb[y, s, 0:rows])
                for side in range(2):
                    base = (4 * side + s) * CORNER_ROWS + at
                    target[base : base + rows, :] = parts[side]


def neighbours(ref, line, e, s, q, groups, edge=None, first=None, last=None):
    rows = ref.shape[-2]
    lane = iota(1, rows)
    same = ref[line, e, s]
    if q == 0 and s == 0:
        other = jnp.where(lane == 0, 0.0, pltpu.roll(ref[line, e, groups - 1], 1, axis=1))
    elif q == 1 and s == groups - 1:
        other = jnp.where(lane == LANES - 1, 0.0, pltpu.roll(ref[line, e, 0], LANES - 1, axis=1))
    else:
        other = ref[line, e, s + (1 if q else -1)]
    zsame = ref[line, 1 - e, s]
    zother = pltpu.roll(zsame, 1 if e == 0 else rows - 1, axis=0)
    if edge is not None:
        zother = edge(zother, line, e, s)
    return (same + other) + (zsame + zother) + (ref[line - 1, e, s] + ref[line + 1, e, s])


def closed(zother, line, e, s):
    rows = zother.shape[0]
    return jnp.where(iota(0, rows) == (0 if e == 0 else rows - 1), 0.0, zother)


def over_lines(low, high, offset, visit, lines=4):
    steps, rest = divmod(high - low + 1, lines)

    def step(i, carry):
        for j in range(lines):
            visit(low + offset + j + lines * i, (low + j) % 2)
        return carry

    lax.fori_loop(0, steps, step, 0)
    for y in range(high + 1 - rest, high + 1):
        visit(y + offset, y % 2)


def diagonal(k, kother, line, e, s, q, groups, edge=None):
    centre = k[line, e, s]
    return centre, 6.0 * centre + neighbours(kother, line, e, s, q, groups, edge)


def down_kernel(
    local, ya, yb, za, zb, ca, cb,
    k, g, fs, half, ub, kx, zc, zd, coarse,
    f, ur, vr, vb,
):
    zabove, yabove = own_sides()
    zup = zabove
    blank = jnp.zeros((8, LANES), F32)
    for c in range(2):
        for line in (*range(PAD), *range(PAD + 8, LINES)):
            for e in range(2):
                for s in range(4):
                    k[c, line, e, s] = blank
                    f[c, line, e, s] = blank
    both = (f, k)

    def assemble(y, carry):
        for e in range(2):
            for s in range(4):
                f[1, PAD + y, e, s] = blank
                for a in range(2):
                    for c in range(2):
                        both[a][c, PAD + y, e, s, 0:4] = local[a, c, y, e, s]
        for s in range(4):
            for side, part in enumerate(pick(zabove, za[y, s], zb[y, s])):
                for i, (a, c, d) in enumerate(ZFACE):
                    e, row = halo_cell(side, d)
                    if d == 5:
                        kx[side, y, s : s + 1] = part[i : i + 1]
                    else:
                        both[a][c, PAD + y, e, s, row : row + 1] = part[i : i + 1]
        return carry

    lax.fori_loop(0, 8, assemble, 0)
    for i, (a, c, y, n) in enumerate(YFACE):
        first, second = pick(yabove, PAD + y + 8, PAD + y - n)
        for e in range(2):
            for s in range(4):
                both[a][c, first, e, s, 0:4] = ya[i, e, s]
                both[a][c, second, e, s, 0:4] = yb[i, e, s]
    for d, (count, at, _) in CORNER.items():
        for message, line in zip((ca, cb), pick(yabove, PAD + 7 + d, PAD - d)):
            for side in range(2):
                for i, (a, c, dz) in enumerate(ZFACE[:count]):
                    e, row = halo_cell(side, dz)
                    for s in range(4):
                        base = (4 * side + s) * CORNER_ROWS + at + i
                        both[a][c, line, e, s, row : row + 1] = message[base : base + 1, :]

    rows = iota(0)

    def far(zother, line, e, s):
        beyond = kx[1 - e, line - PAD, s : s + 1]
        return jnp.where(rows == (6 if e == 0 else 5), jnp.broadcast_to(beyond, (8, LANES)), zother)

    def prepare(c, line, parity, edge, keep):
        for e in range(2):
            q = (e + parity + c) % 2
            for s in range(4):
                centre, total = diagonal(k.at[c], k.at[1 - c], line, e, s, q, 4, edge)
                inside = centre != 0.0
                scale = jnp.where(inside, 1.0 / jnp.where(inside, total, 1.0), 0.0)
                start = 2.0 * f[c, line, e, s] * scale
                g[c, line, e, s] = scale
                fs[c, line, e, s] = start
                if keep:
                    half[line - PAD, e, s] = 0.5 * total
                if c == 0:
                    ur[line, e, s] = start
                    vr[line, e, s] = centre * start

    over_lines(-4, -1, PAD, lambda line, parity: prepare(0, line, parity, None, False))
    over_lines(8, 11, PAD, lambda line, parity: prepare(0, line, parity, None, False))
    over_lines(0, 7, PAD, lambda line, parity: prepare(0, line, parity, far, True))
    over_lines(-3, 10, PAD, lambda line, parity: prepare(1, line, parity, None, False))

    def relax(c, low, high):
        sweep(c, low, high, k, g, fs, (ur, ub), (vr, vb))

    relax(1, -3, 10)
    relax(0, -2, 9)
    relax(1, -1, 8)

    for row in range(4):
        for s in range(4):
            total = None
            for y in (2 * row, 2 * row + 1):
                for e in range(2):
                    line = PAD + y
                    value = red_residual(line, y % 2, e, s, k, g, fs, half, ur, ub, vb)
                    total = value if total is None else total + value
            put_coarse(coarse, row, s, total * 0.125)

    for y in range(8):
        for s in range(4):
            for d in range(1, 6):
                at, high, low = (4 * y + s) * 5 + d - 1, 8 - d, d - 1
                up = ub[PAD + y, high % 2, s, high // 2 : high // 2 + 1]
                down = ub[PAD + y, low % 2, s, low // 2 : low // 2 + 1]
                zc[at : at + 1, :], zd[at : at + 1, :] = pick(zup, up, down)


def widen_kernel(ub, zc, zd, wide, yc, yd):
    zabove, yup = own_sides()
    for y in range(8):
        for s in range(4):
            at = (4 * y + s) * 5
            for e in range(2):
                wide[y, e, s, 0:4] = ub[PAD + y, e, s, 0:4]
            for side, part in enumerate(pick(zabove, zc[at : at + 4, :], zd[at : at + 4, :])):
                for d in range(1, 5):
                    e, row = halo_cell(side, d)
                    wide[y, e, s, row : row + 1] = part[d - 1 : d]
    first, second = pick(yup, 3, 0)
    for i in range(5):
        yc[i] = wide[first + i]
        yd[i] = wide[second + i]


def sweep(c, low, high, k, g, fs, u, v, edges=(None, None)):
    def visit(line, parity):
        for e in range(2):
            q = (e + parity + c) % 2
            for s in range(4):
                near = neighbours(u[1 - c], line, e, s, q, 4, edges[0])
                flow = neighbours(v[1 - c], line, e, s, q, 4, edges[1])
                centre = k[c, line, e, s]
                value = fs[c, line, e, s] + g[c, line, e, s] * (centre * near + flow)
                u[c][line, e, s] = value
                v[c][line, e, s] = centre * value

    over_lines(low, high, PAD, visit)


def red_residual(line, parity, e, s, k, g, fs, half, ur, ub, vb):
    q = (e + parity) % 2
    near = neighbours(ub, line, e, s, q, 4)
    flow = neighbours(vb, line, e, s, q, 4)
    fresh = fs[0, line, e, s] + g[0, line, e, s] * (k[0, line, e, s] * near + flow)
    return half[line - PAD, e, s] * (fresh - ur[line, e, s])


def up_kernel(
    k, g, fs, half, wide, kx, yc, yd, zc, zd, error, errorx,
    correction, residual,
    ub, ur, vb, vr, ux, vx, natural,
):
    zabove, yabove = own_sides()
    ub[PAD : PAD + 8] = wide[...]
    first, second = pick(yabove, PAD + 8, 0)
    for i in range(5):
        ub[first + i] = yc[i]
        ub[second + i] = yd[i]
    for y in range(8):
        for s in range(4):
            at = (4 * y + s) * 5 + 4
            for side, part in enumerate(pick(zabove, zc[at : at + 1, :], zd[at : at + 1, :])):
                beyond = kx[side, y, s : s + 1]
                value = part + errorx[side, y // 2, s : s + 1]
                value = jnp.where(beyond != 0.0, value, 0.0)
                ux[side, y, s : s + 1] = value
                vx[side, y, s : s + 1] = beyond * value

    def add(line, parity):
        for e in range(2):
            for s in range(4):
                centre = k[1, line, e, s]
                value = ub[line, e, s] + error[(line + 1) // 2, s]
                value = jnp.where(centre != 0.0, value, 0.0)
                ub[line, e, s] = value
                vb[line, e, s] = centre * value

    over_lines(-5, 12, PAD, add)

    rows = iota(0)

    def far(ref):
        def edge(zother, line, e, s):
            beyond = ref[1 - e, line - PAD, s : s + 1]
            return jnp.where(rows == (6 if e == 0 else 5), jnp.broadcast_to(beyond, (8, LANES)), zother)

        return edge

    u, v = (ur, ub), (vr, vb)
    sweep(0, -4, -1, k, g, fs, u, v)
    sweep(0, 8, 11, k, g, fs, u, v)
    sweep(0, 0, 7, k, g, fs, u, v, (far(ux), far(vx)))
    sweep(1, -3, 10, k, g, fs, u, v)
    sweep(0, -2, 9, k, g, fs, u, v)
    sweep(1, -1, 8, k, g, fs, u, v)

    quiet = jnp.zeros((4, LANES), F32)
    for y in range(8):
        for e in range(2):
            at = pl.ds(y + 8 * e, 4, stride=16)
            q = (e + y) % 2
            for s in range(4):
                value = red_residual(PAD + y, y % 2, e, s, k, g, fs, half, ur, ub, vb)
                natural[1, 2 * s + q, at, :] = value[0:4]
                natural[1, 2 * s + 1 - q, at, :] = quiet
                natural[0, 2 * s + q, at, :] = ur[PAD + y, e, s, 0:4]
                natural[0, 2 * s + 1 - q, at, :] = ub[PAD + y, e, s, 0:4]
    for a, out in enumerate((correction, residual)):
        for z in range(8):
            tiles = join_lanes([natural[a, s, 8 * z : 8 * z + 8, :] for s in range(8)])
            for t in range(8):
                out[z, :, t * LANES : (t + 1) * LANES] = tiles[t]


def shifted(value, step, axis):
    size = value.shape[axis]
    where = iota(axis, value.shape[0])
    moved = pltpu.roll(value, -step % size, axis=axis)
    return jnp.where((where >= size - step) if step > 0 else (where < -step), 0.0, moved)


def coarse_kernel(nz, ny):
    height, depth = 4 * ny, 2 * nz
    height2, height3 = height // 2, height // 4

    def body(
        fmine, ftheirs, kmine, ktheirs, error, errorx,
        f, k, g, fs, half, ur, ub, vr, vb, f2, k2, fc, kc, gc, sc, uc, vc, hc, w3, f3,
    ):
        u, v = (ur, ub), (vr, vb)
        zplace, yplace = lax.axis_index("gz"), lax.axis_index("gy")

        def slot(i, j, swaps):
            apart = (zplace * ny + yplace) ^ (i * ny + j)
            return sum(((apart >> step) & 1) << bit for bit, step in enumerate(swaps[:-1]))

        def spread(odd):
            def visit(j, carry):
                for sources, target, swaps in (
                    ((fmine, ftheirs), f, swap_steps(nz, ny)),
                    ((kmine, ktheirs), k, swap_steps(nz, ny, 0)),
                ):
                    order = [slot(i, j, swaps) for i in range(nz)]
                    for m in range(8):
                        pieces = [sources[(i + odd) % 2][order[i], m] for i in range(nz)]
                        for row in range(4):
                            whole = jnp.concatenate([p[2 * row : 2 * row + 2] for p in pieces], axis=0)
                            target[m // 4, 1 + 4 * j + row, m // 2 % 2, m % 2] = whole
                return carry

            lax.fori_loop(0, ny, visit, 0)

        for odd in range(2):
            pl.when(lax.rem(zplace, 2) == odd)(lambda odd=odd: spread(odd))
        blank = jnp.zeros((depth, LANES), F32)
        for line in (0, height + 1):
            for e in range(2):
                for s in range(2):
                    for c in range(2):
                        k[c, line, e, s] = blank
                        u[c][line, e, s] = blank
                        v[c][line, e, s] = blank

        def prepare(c):
            def visit(line, parity):
                for e in range(2):
                    for s in range(2):
                        centre, total = diagonal(k.at[c], k.at[1 - c], line, e, s, (e + parity + c) % 2, 2, closed)
                        scale = 1.0 / total
                        start = 8.0 * f[c, line, e, s] * scale
                        g[c, line, e, s] = scale
                        fs[c, line, e, s] = start
                        if c == 0:
                            half[line, e, s] = 0.125 * total
                            ur[line, e, s] = start
                            vr[line, e, s] = centre * start

            over_lines(0, height - 1, 1, visit, 8)

        def fresh(c, line, parity, e, s):
            q = (e + parity + c) % 2
            near = neighbours(u[1 - c], line, e, s, q, 2, closed)
            flow = neighbours(v[1 - c], line, e, s, q, 2, closed)
            return fs[c, line, e, s] + g[c, line, e, s] * (k[c, line, e, s] * near + flow)

        def relax(c):
            def visit(line, parity):
                for e in range(2):
                    for s in range(2):
                        value = fresh(c, line, parity, e, s)
                        u[c][line, e, s] = value
                        v[c][line, e, s] = k[c, line, e, s] * value

            over_lines(0, height - 1, 1, visit, 8)

        prepare(0)
        prepare(1)
        relax(1)
        relax(0)
        relax(1)

        def restrict(i, carry):
            for s in range(2):
                value, conduct = None, None
                for j in range(2):
                    line = 1 + 2 * i + j
                    for e in range(2):
                        part = half[line, e, s] * (fresh(0, line, j, e, s) - ur[line, e, s])
                        value = part if value is None else value + part
                        part = k[0, line, e, s] + k[1, line, e, s]
                        conduct = part if conduct is None else conduct + part
                f2[s, i] = value * 0.125
                k2[s, i] = conduct * 0.125
            return carry

        lax.fori_loop(0, height2, restrict, 0)

        even = iota(0, depth) % 2 == 0

        def q_is_zero(c, y):
            return even if (y + c) % 2 == 0 else jnp.logical_not(even)

        def coloured(pair, c, y):
            return jnp.where(q_is_zero(c, y), pair[0], pair[1])

        def around(ref, c, y):
            mid = ref[1 + y]
            other = jnp.where(q_is_zero(c, y), shifted(mid, -1, 1), shifted(mid, 1, 1))
            return (mid + other) + (shifted(mid, -1, 0) + shifted(mid, 1, 0)) + (ref[y] + ref[y + 2])

        for c in range(2):
            for line in (0, height2 + 1):
                kc[c, line] = blank
                uc[c, line] = blank
                vc[c, line] = blank
            for y in range(height2):
                kc[c, 1 + y] = coloured((k2[0, y], k2[1, y]), c, y)
                fc[c, y] = coloured((f2[0, y], f2[1, y]), c, y)
        for c in range(2):
            for y in range(height2):
                centre = kc[c, 1 + y]
                total = 6.0 * centre + around(kc.at[1 - c], c, y)
                scale = 1.0 / total
                start = 32.0 * fc[c, y] * scale
                gc[c, y] = scale
                sc[c, y] = start
                if c == 0:
                    hc[y] = total * (0.5 / 16.0)
                    uc[0, 1 + y] = start
                    vc[0, 1 + y] = centre * start

        def fresh2(c, y):
            flow = kc[c, 1 + y] * around(uc.at[1 - c], c, y) + around(vc.at[1 - c], c, y)
            return sc[c, y] + gc[c, y] * flow

        def relax2(c):
            for y in range(height2):
                value = fresh2(c, y)
                uc[c, 1 + y] = value
                vc[c, 1 + y] = kc[c, 1 + y] * value

        relax2(1)
        relax2(0)
        relax2(1)

        def paired(a, b):
            total = (a + b) * 0.125
            return jnp.where(even, total + pltpu.roll(total, depth - 1, axis=0), 0.0)

        conduct = []
        right = []
        for y in range(height3):
            parts = [hc[2 * y + j] * (fresh2(0, 2 * y + j) - uc[0, 1 + 2 * y + j]) for j in range(2)]
            right.append(paired(*parts))
            parts = [kc[0, 1 + 2 * y + j] + kc[1, 1 + 2 * y + j] for j in range(2)]
            conduct.append(paired(*parts))
        moves = ((-2, 0), (2, 0), (-1, 1), (1, 1))
        for y in range(height3):
            centre = conduct[y]
            beside = [shifted(centre, step, axis) for step, axis in moves]
            beside.append(conduct[y - 1] if y else jnp.zeros_like(centre))
            beside.append(conduct[y + 1] if y + 1 < height3 else jnp.zeros_like(centre))
            total = 6.0 * centre
            for part in beside:
                total = total + part
            scale = jnp.where(even, 1.0 / jnp.where(even, total, 1.0), 0.0)
            f3[y] = 128.0 * right[y] * scale
            lane, row = iota(1, depth), iota(0, depth)
            open_faces = (row >= 2, row < depth - 2, lane >= 1, lane < LANES - 1)
            for i in range(6):
                weight = (centre + beside[i]) * scale
                w3[y, i] = jnp.where(open_faces[i], weight, 0.0) if i < 4 else weight
        mixed = (iota(0, depth) // 2 + iota(1, depth)) % 2

        def relax3(c, field):
            result = []
            for y in range(height3):
                mid = field[y]
                value = f3[y]
                for i, (step, axis) in enumerate(moves):
                    value = value + w3[y, i] * pltpu.roll(mid, -step % mid.shape[axis], axis=axis)
                if y:
                    value = value + w3[y, 4] * field[y - 1]
                if y + 1 < height3:
                    value = value + w3[y, 5] * field[y + 1]
                result.append(jnp.where(mixed == (y + c) % 2, value, mid))
            return result

        def two_colours(_, field):
            return tuple(relax3(1, relax3(0, list(field))))

        field = lax.fori_loop(0, 12, two_colours, (blank,) * height3)

        for y in range(height2):
            coarse = field[y // 2]
            value = uc[1, 1 + y] + (coarse + pltpu.roll(coarse, 1, axis=0))
            uc[1, 1 + y] = value
            vc[1, 1 + y] = kc[1, 1 + y] * value
        for c in (0, 1, 0, 1):
            relax2(c)

        for y in range(height2):
            zero = q_is_zero(0, y)
            red, black = uc[0, 1 + y], uc[1, 1 + y]
            f2[0, y] = jnp.where(zero, red, black)
            f2[1, y] = jnp.where(zero, black, red)

        def add(line, parity):
            for e in range(2):
                for s in range(2):
                    value = ub[line, e, s] + f2[s, (line - 1) // 2]
                    ub[line, e, s] = value
                    vb[line, e, s] = k[1, line, e, s] * value

        over_lines(0, height - 1, 1, add, 8)
        for c in (0, 1, 0, 1):
            relax(c)

        for j in range(-3, 7):
            line = 1 + jnp.clip(4 * yplace + j, 0, height - 1)
            for t in range(-3, 7):
                e = t % 2
                at = pl.ds(jnp.clip(2 * zplace + t // 2, 0, depth - 1), 1)
                for s in range(4):
                    row = u[(s + e + j) % 2][line, e, s // 2, at, :]
                    if -2 <= t <= 5:
                        error[j + 3, s, t % 8 : t % 8 + 1, :] = row
                    elif 0 <= j < 8 // 2:
                        errorx[1 if t < 0 else 0, j, s : s + 1, :] = row

    lines, lines2 = (height + 2, 2, 2, depth, LANES), (height2 + 2, depth, LANES)
    flat2 = (2, height2, depth, LANES)
    scratch = [(2, *lines)] * 4 + [lines] * 5 + [flat2, flat2, flat2, (2, *lines2), flat2, flat2]
    scratch += [(2, *lines2), (2, *lines2), flat2[1:], (height3, 6, depth, LANES), (height3, depth, LANES)]
    return body, scratch


def swap_steps(nz, ny, first=None):
    ybits, zbits = ny.bit_length() - 1, nz.bit_length() - 1
    along_y = list(range(ybits - 1, -1, -1))
    if first is not None:
        along_y = [first, *(bit for bit in along_y if bit != first)]
    return [*along_y, *range(ybits + zbits - 1, ybits - 1, -1)]


def swap(block, step, nz, ny):
    return lax.ppermute(block, ("gz", "gy"), [(i, i ^ (1 << step)) for i in range(nz * ny)])


def swapped(block, step, nz, ny):
    return jnp.concatenate([block, swap(block, step, nz, ny)])


def solve_coarse(fmine, ftheirs, kmine, ktheirs, nz, ny):
    body, scratch = coarse_kernel(nz, ny)
    outs = ((10, 4, 8, LANES), (2, 4, 4, LANES))
    return call(body, 11, outs, scratch, fmine, ftheirs, kmine, ktheirs)


def extended(array, sides, width):
    for axis, dim in sides:
        size, length = (lax.axis_size(axis), array.shape[dim])
        up = [(i, (i + 1) % size) for i in range(size - 1)]
        down = [(j, i) for i, j in up]
        last = lax.slice_in_dim(array, length - width, length, axis=dim)
        initial = lax.slice_in_dim(array, 0, width, axis=dim)
        before = lax.ppermute(last, axis, up)
        after = lax.ppermute(initial, axis, down)
        array = jnp.concatenate([before, array, after], axis=dim)
    return array


def coarsen(field):
    total = field[0::2, 0::2, 0::2] + field[0::2, 0::2, 1::2]
    total = total + field[0::2, 1::2, 0::2] + field[0::2, 1::2, 1::2]
    total = total + field[1::2, 0::2, 0::2] + field[1::2, 0::2, 1::2]
    total = total + field[1::2, 1::2, 0::2] + field[1::2, 1::2, 1::2]
    return total * 0.125


def prolong(field):
    return jnp.repeat(jnp.repeat(jnp.repeat(field, 2, axis=0), 2, axis=1), 2, axis=2)


def face_terms(kpad):
    center = kpad[1:-1, 1:-1, 1:-1]
    z_minus = 0.5 * (center + kpad[:-2, 1:-1, 1:-1])
    z_plus = 0.5 * (center + kpad[2:, 1:-1, 1:-1])
    y_minus = 0.5 * (center + kpad[1:-1, :-2, 1:-1])
    y_plus = 0.5 * (center + kpad[1:-1, 2:, 1:-1])
    x_minus = 0.5 * (center + kpad[1:-1, 1:-1, :-2])
    x_plus = 0.5 * (center + kpad[1:-1, 1:-1, 2:])
    total = z_minus + z_plus + y_minus + y_plus + x_minus + x_plus
    return ((z_minus, z_plus, y_minus, y_plus, x_minus, x_plus), total)


def neighbour_sum(weights, upad):
    z_minus, z_plus, y_minus, y_plus, x_minus, x_plus = weights
    acc = z_minus * upad[:-2, 1:-1, 1:-1] + z_plus * upad[2:, 1:-1, 1:-1]
    acc = acc + y_minus * upad[1:-1, :-2, 1:-1] + y_plus * upad[1:-1, 2:, 1:-1]
    acc = acc + x_minus * upad[1:-1, 1:-1, :-2] + x_plus * upad[1:-1, 1:-1, 2:]
    return acc


def extend(field, layout):
    if layout == "column":
        wider = extended(field, (("gy", 1),), 1)
        wider = jnp.pad(wider, ((1, 1), (0, 0), (0, 0)))
    else:
        wider = extended(field, (("gz", 0), ("gy", 1)), 1)
    return jnp.pad(wider, ((0, 0), (0, 0), (1, 1)))


def region_masks(shape, z_start, y_start):
    zpos = lax.broadcasted_iota(jnp.int32, shape, 0) + z_start
    ypos = lax.broadcasted_iota(jnp.int32, shape, 1) + y_start
    xpos = lax.broadcasted_iota(jnp.int32, shape, 2)
    return (zpos + ypos + xpos + 4) % 2


def cycle(rhs, conduct, level, layout, z_start, y_start, z_total, y_total):
    scale = 4.0**level
    weights, total = face_terms(extend(conduct, layout))
    parity = region_masks(rhs.shape, z_start, y_start)
    first = parity == 0
    second = parity == 1

    def relax(field, colour):
        fresh = (scale * rhs + neighbour_sum(weights, extend(field, layout))) / total
        return jnp.where(colour, fresh, field)

    def smooth(field, sweeps):
        for sweep in range(sweeps):
            for colour in (first, second):
                field = relax(field, colour)
        return field

    def remainder(field):
        return rhs - (total * field - neighbour_sum(weights, extend(field, layout))) / scale

    field = jnp.zeros(rhs.shape, jnp.float32)
    if level == LEVELS - 1:
        return (smooth(field, 12), None)
    field = smooth(field, 2)
    rhs_next = coarsen(remainder(field))
    conduct_next = coarsen(conduct)
    joined = layout == "split" and level == 1
    if joined:
        local_depth = rhs_next.shape[0]
        rhs_next, conduct_next = (
            lax.all_gather(rhs_next, "gz", axis=0, tiled=True),
            lax.all_gather(conduct_next, "gz", axis=0, tiled=True),
        )
        error, unused = cycle(
            rhs_next, conduct_next, level + 1, "column", 0, y_start // 2, z_total // 2, y_total // 2
        )
        error = lax.dynamic_slice_in_dim(error, lax.axis_index("gz") * local_depth, local_depth, 0)
    else:
        error, unused = cycle(
            rhs_next,
            conduct_next,
            level + 1,
            layout,
            z_start // 2,
            y_start // 2,
            z_total // 2,
            y_total // 2,
        )
    field = field + prolong(error)
    field = smooth(field, 2)
    return (field, remainder(field))


def natural_coarse(message):
    packed = message.reshape(2, 2, 2, 4, 2, LANES)
    parity = (jnp.arange(2)[:, None, None, None, None] + jnp.arange(4)[None, None, :, None, None]) % 2 == 0
    even = jnp.where(parity, packed[0], packed[1])
    odd = jnp.where(parity, packed[1], packed[0])
    both = jnp.stack([even, odd])
    return both.transpose(4, 1, 3, 5, 2, 0).reshape(4, 4, 4 * LANES)


def solve_coarse_spread(message, kmessage, nz, ny):
    z_start, y_start = 4 * lax.axis_index("gz"), 4 * lax.axis_index("gy")
    field, unused = cycle(
        natural_coarse(message), natural_coarse(kmessage), 1, "split", z_start, y_start, 4 * nz, 4 * ny
    )
    wide = extended(field, (("gz", 0), ("gy", 1)), 3).reshape(10, 10, LANES, 4).transpose(1, 3, 0, 2)
    error = jnp.concatenate([wide[:, :, 3:9], wide[:, :, 1:3]], axis=2)
    return error, jnp.stack([wide[3:7, :, 9], wide[3:7, :, 0]])


def exchange(first, second, axis):
    size = lax.axis_size(axis)
    results = []
    for message, start in ((first, 0), (second, 1)):
        pairs = [(i, i + 1) for i in range(start, size - 1, 2)]
        results.append(lax.ppermute(message, axis, pairs + [(j, i) for i, j in pairs]))
    return results


def on_device(right_side, coefficient):
    nz, ny = lax.axis_size("gz"), lax.axis_size("gy")
    assert right_side.shape == (8, 8, 8 * LANES)
    cells = (2, 2, 8, 2, 4, 4, LANES)
    yface, zface = (16, 2, 4, 4, LANES), (8, 4, 16, LANES)
    coarse = (8, 8, LANES)
    packed = call(pack_kernel, 3, (cells, yface, yface), [(2, 8, 64, LANES)], right_side, coefficient)
    local, ya, yb = packed
    ya, yb = exchange(ya, yb, "gy")
    za, zb, kmessage = call(zpack_kernel, 2, (zface, zface, coarse), [], local)
    za, zb = exchange(za, zb, "gz")
    coarse_cells = 8 * 8 * LANES
    whole = nz * ny * coarse_cells <= WHOLE_COARSE_CELLS and nz & (nz - 1) == 0 and ny & (ny - 1) == 0
    swaps, kswaps = swap_steps(nz, ny), swap_steps(nz, ny, 0)
    kall = kmessage[None]
    if whole:
        kall = swapped(kall, kswaps[0], nz, ny)
        ya, za, zb, kall = lax.optimization_barrier((ya, za, zb, kall))
    relayed = (8 * CORNER_ROWS, LANES)
    scratch = [zface, zface, pltpu.SemaphoreType.DMA((2,))]
    far = [pl.BlockSpec(memory_space=pl.ANY)] * 2
    ca, cb = exchange(*call(relay_kernel, 2, (relayed, relayed), scratch, za, zb, specs=far), "gy")
    if whole:
        for step in kswaps[1:-2]:
            kall = swapped(kall, step, nz, ny)
        ca, cb, kall = lax.optimization_barrier((ca, cb, kall))
        kall = swapped(kall, kswaps[-2], nz, ny)
        ktheirs = swap(kall, kswaps[-1], nz, ny)
    lines, zface = (LINES, 2, 4, 8, LANES), (160, LANES)
    outs = ((2, *lines), (2, *lines), (2, *lines), (8, *lines[1:]), lines, (2, 8, 4, LANES), zface, zface, coarse)
    scratch = [(2, *lines), lines, lines, lines]
    k, g, fs, half, ub, kx, zc, zd, message = call(down_kernel, 6, outs, scratch, local, ya, yb, za, zb, ca, cb)
    fall, half_way = message[None], len(swaps) // 2
    zc, zd = exchange(zc, zd, "gz")
    if whole:
        for step in swaps[:half_way]:
            fall = swapped(fall, step, nz, ny)
        fall, zc, zd = lax.optimization_barrier((fall, zc, zd))
    yface = (5, *lines[1:])
    wide, yc, yd = call(widen_kernel, 2, ((8, *lines[1:]), yface, yface), [], ub, zc, zd)
    if whole:
        fall = swapped(fall, swaps[half_way], nz, ny)
        fall, yc, yd = lax.optimization_barrier((fall, yc, yd))
    yc, yd = exchange(yc, yd, "gy")
    if whole:
        for step in swaps[half_way + 1 : -1]:
            fall = swapped(fall, step, nz, ny)
        fall, yc, yd = lax.optimization_barrier((fall, yc, yd))
        ftheirs = swap(fall, swaps[-1], nz, ny)
        error, errorx = solve_coarse(fall, ftheirs, kall, ktheirs, nz, ny)
    else:
        error, errorx = solve_coarse_spread(message, kmessage, nz, ny)
    block = (8, 8, 8 * LANES)
    scratch = [lines] * 4 + [(2, 8, 4, LANES)] * 2 + [(2, 8, 64, LANES)]
    return call(up_kernel, 6, (block, block), scratch, k, g, fs, half, wide, kx, yc, yd, zc, zd, error, errorx)


def solution(mesh):
    spec = P("gz", "gy", None)
    return jax.shard_map(
        on_device, mesh=mesh, in_specs=(spec, spec), out_specs=(spec, spec), check_vma=False
    )
```

```python
import jax
import jax.numpy as jnp
from jax import lax
from jax.experimental import pallas as pl
from jax.experimental.pallas import tpu as pltpu
from jax.sharding import PartitionSpec as P

LANES = 128
LINES = 18
LEVELS = 4
PAD = 5
F32 = jnp.float32
WHOLE_COARSE_CELLS = 1 << 19


def call(body, micros, outs, scratch, *args, specs=None):
    vmem = pl.BlockSpec(memory_space=pltpu.VMEM)
    return pl.pallas_call(
        body,
        out_shape=[jax.ShapeDtypeStruct(s, F32) for s in outs],
        in_specs=specs or [vmem] * len(args),
        out_specs=[vmem] * len(outs),
        scratch_shapes=[pltpu.VMEM(s, F32) if isinstance(s, tuple) else s for s in scratch],
        cost_estimate=pl.CostEstimate(flops=0, transcendentals=0, bytes_accessed=micros * 3_000_000),
        compiler_params=pltpu.CompilerParams(vmem_limit_bytes=56 << 20),
    )(*args)


def iota(axis, rows=8):
    return lax.broadcasted_iota(jnp.int32, (rows, LANES), axis)


def barrel(arrays, block):
    for bit in (1, 2, 4):
        high = (block & bit) != 0
        arrays = [jnp.where(high, arrays[(j + bit) % 8], arrays[j]) for j in range(8)]
    return arrays


def lane_gather(array, index):
    return jnp.take_along_axis(array, index, axis=1, mode="promise_in_bounds")


def split_lanes(tiles):
    lane = iota(1)
    block = lane // 16
    parts = [lane_gather(tiles[t], 8 * (lane % 16) + (block - t) % 8) for t in range(8)]
    mixed = barrel(parts, block)
    return [pltpu.roll(mixed[-s % 8], (-16 * s) % LANES, axis=1) for s in range(8)]


def join_lanes(arrays):
    lane = iota(1)
    block = lane // 16
    moved = [pltpu.roll(arrays[s], (16 * s) % LANES, axis=1) for s in range(8)]
    mixed = barrel(moved, block)
    return [lane_gather(mixed[-t % 8], 16 * ((lane % 8 + t) % 8) + lane // 8) for t in range(8)]


def put_coarse(message, row, s, value):
    for z in range(4):
        e, c = z % 2, (s + z + row) % 2
        message[(c * 2 + e) * 2 + s // 2, 2 * row + z // 2, :] = value[z]


REACH = ((0, 0, 4), (0, 1, 3), (1, 0, 4), (1, 1, 5))
YFACE = [(a, c, y, n) for a, c, n in REACH for y in range(n)]
ZFACE = sorted(((a, c, d) for a, c, n in REACH for d in range(1, n + 1)), key=lambda r: r[2] - REACH[2 * r[0] + r[1]][2])
CORNER = {1: (12, 0, 12), 2: (8, 16, 8), 3: (4, 12, 4), 4: (1, 24, 4)}
CORNER_ROWS = 28


def own_sides():
    return [lax.rem(lax.axis_index(axis), 2) == 0 for axis in ("gz", "gy")]


def halo_cell(side, distance):
    z = 7 + distance if side == 0 else -distance
    return z % 2, (z // 2) % 8


def pick(flag, a, b):
    return jnp.where(flag, a, b), jnp.where(flag, b, a)


def pack_kernel(f_ref, k_ref, local, ya, yb, natural):
    _, yup = own_sides()
    for a, ref in enumerate((f_ref, k_ref)):
        for z in range(8):
            arrays = split_lanes([ref[z, :, t * LANES : (t + 1) * LANES] for t in range(8)])
            for s in range(8):
                natural[a, s, 8 * z : 8 * z + 8, :] = arrays[s]
    for a in range(2):
        for c in range(2):
            for y in range(8):
                for e in range(2):
                    q = (e + y + c) % 2
                    for s in range(4):
                        local[a, c, y, e, s] = natural[a, 2 * s + q, pl.ds(y + 8 * e, 4, stride=16), :]
    for i, (a, c, y, n) in enumerate(YFACE):
        first, second = pick(yup, y + 8 - n, y)
        ya[i] = local[a, c, first]
        yb[i] = local[a, c, second]


def zpack_kernel(local, za, zb, coarse):
    zup, _ = own_sides()

    def faces(y, carry):
        for i, (a, c, d) in enumerate(ZFACE):
            high, low = 8 - d, d - 1
            for s in range(4):
                up = local[a, c, y, high % 2, s, high // 2 : high // 2 + 1]
                down = local[a, c, y, low % 2, s, low // 2 : low // 2 + 1]
                za[y, s, i : i + 1], zb[y, s, i : i + 1] = pick(zup, up, down)
        return carry

    lax.fori_loop(0, 8, faces, 0)
    for row in range(4):
        for s in range(4):
            total = None
            for c in range(2):
                for y in (2 * row, 2 * row + 1):
                    pair = local[1, c, y, 0, s] + local[1, c, y, 1, s]
                    total = pair if total is None else total + pair
            put_coarse(coarse, row, s, total * 0.125)


def relay_kernel(ya_far, yb_far, ca, cb, faces, sem):
    zup, yabove = own_sides()
    slots = pick(yabove, 0, 1)
    copies = [pltpu.make_async_copy(f, faces.at[t], sem.at[i]) for i, (f, t) in enumerate(zip((ya_far, yb_far), slots))]
    for copy in copies:
        copy.start()
    for copy in copies:
        copy.wait()
    for target, up in ((ca, zup), (cb, jnp.logical_not(zup))):
        places = {d: jnp.where(up, 8 - d, d - 1) for d in range(1, 5)}
        for d, (count, at, _) in CORNER.items():
            for i, (a, c, dz) in enumerate(ZFACE[:count]):
                e, t = lax.rem(places[dz], 2), places[dz] // 2
                for side in range(2):
                    y = d - 1 if side == 0 else REACH[2 * a + c][2] - d
                    line = YFACE.index((a, c, y, REACH[2 * a + c][2]))
                    for s in range(4):
                        base = (4 * side + s) * CORNER_ROWS + at + i
                        target[base : base + 1, :] = faces[side, line, e, s, pl.ds(t, 1)]


def neighbours(ref, line, e, s, q, groups, edge=None, first=None, last=None):
    rows = ref.shape[-2]
    lane = iota(1, rows)
    same = ref[line, e, s]
    if q == 0 and s == 0:
        other = jnp.where(lane == 0, 0.0, pltpu.roll(ref[line, e, groups - 1], 1, axis=1))
    elif q == 1 and s == groups - 1:
        other = jnp.where(lane == LANES - 1, 0.0, pltpu.roll(ref[line, e, 0], LANES - 1, axis=1))
    else:
        other = ref[line, e, s + (1 if q else -1)]
    zsame = ref[line, 1 - e, s]
    zother = pltpu.roll(zsame, 1 if e == 0 else rows - 1, axis=0)
    if edge is not None:
        zother = edge(zother, line, e, s)
    return (same + other) + (zsame + zother) + (ref[line - 1, e, s] + ref[line + 1, e, s])


def closed(zother, line, e, s):
    rows = zother.shape[0]
    return jnp.where(iota(0, rows) == (0 if e == 0 else rows - 1), 0.0, zother)


def over_lines(low, high, offset, visit, lines=4):
    steps, rest = divmod(high - low + 1, lines)

    def step(i, carry):
        for j in range(lines):
            visit(low + offset + j + lines * i, (low + j) % 2)
        return carry

    lax.fori_loop(0, steps, step, 0)
    for y in range(high + 1 - rest, high + 1):
        visit(y + offset, y % 2)


def diagonal(k, kother, line, e, s, q, groups, edge=None):
    centre = k[line, e, s]
    return centre, 6.0 * centre + neighbours(kother, line, e, s, q, groups, edge)


def down_kernel(
    local, ya, yb, za, zb, ca, cb,
    k, g, fs, half, ub, kx, zc, zd, coarse,
    f, ur, vr, vb,
):
    zabove, yabove = own_sides()
    zup = zabove
    blank = jnp.zeros((8, LANES), F32)
    for c in range(2):
        for line in (*range(PAD), *range(PAD + 8, LINES)):
            for e in range(2):
                for s in range(4):
                    k[c, line, e, s] = blank
                    f[c, line, e, s] = blank
    both = (f, k)

    def assemble(y, carry):
        for e in range(2):
            for s in range(4):
                f[1, PAD + y, e, s] = blank
                for a in range(2):
                    for c in range(2):
                        both[a][c, PAD + y, e, s, 0:4] = local[a, c, y, e, s]
        for s in range(4):
            for side, part in enumerate(pick(zabove, za[y, s], zb[y, s])):
                for i, (a, c, d) in enumerate(ZFACE):
                    e, row = halo_cell(side, d)
                    if d == 5:
                        kx[side, y, s : s + 1] = part[i : i + 1]
                    else:
                        both[a][c, PAD + y, e, s, row : row + 1] = part[i : i + 1]
        return carry

    lax.fori_loop(0, 8, assemble, 0)
    for i, (a, c, y, n) in enumerate(YFACE):
        first, second = pick(yabove, PAD + y + 8, PAD + y - n)
        for e in range(2):
            for s in range(4):
                both[a][c, first, e, s, 0:4] = ya[i, e, s]
                both[a][c, second, e, s, 0:4] = yb[i, e, s]
    for yside in range(2):
        for s in range(4):
            for d, (count, at, _) in CORNER.items():
                line, base = PAD + 7 + d if yside == 0 else PAD - d, (4 * yside + s) * CORNER_ROWS + at
                for side, part in enumerate(pick(zabove, ca[base : base + count, :], cb[base : base + count, :])):
                    for i, (a, c, dz) in enumerate(ZFACE[:count]):
                        e, row = halo_cell(side, dz)
                        both[a][c, line, e, s, row : row + 1] = part[i : i + 1]

    rows = iota(0)

    def far(zother, line, e, s):
        beyond = kx[1 - e, line - PAD, s : s + 1]
        return jnp.where(rows == (6 if e == 0 else 5), jnp.broadcast_to(beyond, (8, LANES)), zother)

    def prepare(c, line, parity, edge, keep):
        for e in range(2):
            q = (e + parity + c) % 2
            for s in range(4):
                centre, total = diagonal(k.at[c], k.at[1 - c], line, e, s, q, 4, edge)
                inside = centre != 0.0
                scale = jnp.where(inside, 1.0 / jnp.where(inside, total, 1.0), 0.0)
                start = 2.0 * f[c, line, e, s] * scale
                g[c, line, e, s] = scale
                fs[c, line, e, s] = start
                if keep:
                    half[line - PAD, e, s] = 0.5 * total
                if c == 0:
                    ur[line, e, s] = start
                    vr[line, e, s] = centre * start

    over_lines(-4, -1, PAD, lambda line, parity: prepare(0, line, parity, None, False))
    over_lines(8, 11, PAD, lambda line, parity: prepare(0, line, parity, None, False))
    over_lines(0, 7, PAD, lambda line, parity: prepare(0, line, parity, far, True))
    over_lines(-3, 10, PAD, lambda line, parity: prepare(1, line, parity, None, False))

    def relax(c, low, high):
        sweep(c, low, high, k, g, fs, (ur, ub), (vr, vb))

    relax(1, -3, 10)
    relax(0, -2, 9)
    relax(1, -1, 8)

    for row in range(4):
        for s in range(4):
            total = None
            for y in (2 * row, 2 * row + 1):
                for e in range(2):
                    line = PAD + y
                    value = red_residual(line, y % 2, e, s, k, g, fs, half, ur, ub, vb)
                    total = value if total is None else total + value
            put_coarse(coarse, row, s, total * 0.125)

    for y in range(8):
        for s in range(4):
            for d in range(1, 6):
                at, high, low = (4 * y + s) * 5 + d - 1, 8 - d, d - 1
                up = ub[PAD + y, high % 2, s, high // 2 : high // 2 + 1]
                down = ub[PAD + y, low % 2, s, low // 2 : low // 2 + 1]
                zc[at : at + 1, :], zd[at : at + 1, :] = pick(zup, up, down)


def widen_kernel(ub, zc, zd, wide, yc, yd):
    zabove, yup = own_sides()
    for y in range(8):
        for s in range(4):
            at = (4 * y + s) * 5
            for e in range(2):
                wide[y, e, s, 0:4] = ub[PAD + y, e, s, 0:4]
            for side, part in enumerate(pick(zabove, zc[at : at + 4, :], zd[at : at + 4, :])):
                for d in range(1, 5):
                    e, row = halo_cell(side, d)
                    wide[y, e, s, row : row + 1] = part[d - 1 : d]
    first, second = pick(yup, 3, 0)
    for i in range(5):
        yc[i] = wide[first + i]
        yd[i] = wide[second + i]


def sweep(c, low, high, k, g, fs, u, v, edges=(None, None)):
    def visit(line, parity):
        for e in range(2):
            q = (e + parity + c) % 2
            for s in range(4):
                near = neighbours(u[1 - c], line, e, s, q, 4, edges[0])
                flow = neighbours(v[1 - c], line, e, s, q, 4, edges[1])
                centre = k[c, line, e, s]
                value = fs[c, line, e, s] + g[c, line, e, s] * (centre * near + flow)
                u[c][line, e, s] = value
                v[c][line, e, s] = centre * value

    over_lines(low, high, PAD, visit)


def red_residual(line, parity, e, s, k, g, fs, half, ur, ub, vb):
    q = (e + parity) % 2
    near = neighbours(ub, line, e, s, q, 4)
    flow = neighbours(vb, line, e, s, q, 4)
    fresh = fs[0, line, e, s] + g[0, line, e, s] * (k[0, line, e, s] * near + flow)
    return half[line - PAD, e, s] * (fresh - ur[line, e, s])


def up_kernel(
    k, g, fs, half, wide, kx, yc, yd, zc, zd, error, errorx,
    correction, residual,
    ub, ur, vb, vr, ux, vx, natural,
):
    zabove, yabove = own_sides()
    ub[PAD : PAD + 8] = wide[...]
    first, second = pick(yabove, PAD + 8, 0)
    for i in range(5):
        ub[first + i] = yc[i]
        ub[second + i] = yd[i]
    for y in range(8):
        for s in range(4):
            at = (4 * y + s) * 5 + 4
            for side, part in enumerate(pick(zabove, zc[at : at + 1, :], zd[at : at + 1, :])):
                beyond = kx[side, y, s : s + 1]
                value = part + errorx[side, y // 2, s : s + 1]
                value = jnp.where(beyond != 0.0, value, 0.0)
                ux[side, y, s : s + 1] = value
                vx[side, y, s : s + 1] = beyond * value

    def add(line, parity):
        for e in range(2):
            for s in range(4):
                centre = k[1, line, e, s]
                value = ub[line, e, s] + error[(line + 1) // 2, s]
                value = jnp.where(centre != 0.0, value, 0.0)
                ub[line, e, s] = value
                vb[line, e, s] = centre * value

    over_lines(-5, 12, PAD, add)

    rows = iota(0)

    def far(ref):
        def edge(zother, line, e, s):
            beyond = ref[1 - e, line - PAD, s : s + 1]
            return jnp.where(rows == (6 if e == 0 else 5), jnp.broadcast_to(beyond, (8, LANES)), zother)

        return edge

    u, v = (ur, ub), (vr, vb)
    sweep(0, -4, -1, k, g, fs, u, v)
    sweep(0, 8, 11, k, g, fs, u, v)
    sweep(0, 0, 7, k, g, fs, u, v, (far(ux), far(vx)))
    sweep(1, -3, 10, k, g, fs, u, v)
    sweep(0, -2, 9, k, g, fs, u, v)
    sweep(1, -1, 8, k, g, fs, u, v)

    quiet = jnp.zeros((4, LANES), F32)
    for y in range(8):
        for e in range(2):
            at = pl.ds(y + 8 * e, 4, stride=16)
            q = (e + y) % 2
            for s in range(4):
                value = red_residual(PAD + y, y % 2, e, s, k, g, fs, half, ur, ub, vb)
                natural[1, 2 * s + q, at, :] = value[0:4]
                natural[1, 2 * s + 1 - q, at, :] = quiet
                natural[0, 2 * s + q, at, :] = ur[PAD + y, e, s, 0:4]
                natural[0, 2 * s + 1 - q, at, :] = ub[PAD + y, e, s, 0:4]
    for a, out in enumerate((correction, residual)):
        for z in range(8):
            tiles = join_lanes([natural[a, s, 8 * z : 8 * z + 8, :] for s in range(8)])
            for t in range(8):
                out[z, :, t * LANES : (t + 1) * LANES] = tiles[t]


def shifted(value, step, axis):
    size = value.shape[axis]
    where = iota(axis, value.shape[0])
    moved = pltpu.roll(value, -step % size, axis=axis)
    return jnp.where((where >= size - step) if step > 0 else (where < -step), 0.0, moved)


def coarse_kernel(nz, ny):
    height, depth = 4 * ny, 2 * nz
    height2, height3 = height // 2, height // 4

    def body(
        fmine, ftheirs, kmine, ktheirs, error, errorx,
        f, k, g, fs, half, ur, ub, vr, vb, f2, k2, fc, kc, gc, sc, uc, vc, hc, w3, f3,
    ):
        u, v = (ur, ub), (vr, vb)
        zplace, yplace = lax.axis_index("gz"), lax.axis_index("gy")

        def slot(i, j, swaps):
            apart = (zplace * ny + yplace) ^ (i * ny + j)
            return sum(((apart >> step) & 1) << bit for bit, step in enumerate(swaps[:-1]))

        def spread(odd):
            def visit(j, carry):
                for sources, target, swaps in (
                    ((fmine, ftheirs), f, swap_steps(nz, ny)),
                    ((kmine, ktheirs), k, swap_steps(nz, ny, 0)),
                ):
                    order = [slot(i, j, swaps) for i in range(nz)]
                    for m in range(8):
                        pieces = [sources[(i + odd) % 2][order[i], m] for i in range(nz)]
                        for row in range(4):
                            whole = jnp.concatenate([p[2 * row : 2 * row + 2] for p in pieces], axis=0)
                            target[m // 4, 1 + 4 * j + row, m // 2 % 2, m % 2] = whole
                return carry

            lax.fori_loop(0, ny, visit, 0)

        for odd in range(2):
            pl.when(lax.rem(zplace, 2) == odd)(lambda odd=odd: spread(odd))
        blank = jnp.zeros((depth, LANES), F32)
        for line in (0, height + 1):
            for e in range(2):
                for s in range(2):
                    for c in range(2):
                        k[c, line, e, s] = blank
                        u[c][line, e, s] = blank
                        v[c][line, e, s] = blank

        def prepare(c):
            def visit(line, parity):
                for e in range(2):
                    for s in range(2):
                        centre, total = diagonal(k.at[c], k.at[1 - c], line, e, s, (e + parity + c) % 2, 2, closed)
                        scale = 1.0 / total
                        start = 8.0 * f[c, line, e, s] * scale
                        g[c, line, e, s] = scale
                        fs[c, line, e, s] = start
                        if c == 0:
                            half[line, e, s] = 0.125 * total
                            ur[line, e, s] = start
                            vr[line, e, s] = centre * start

            over_lines(0, height - 1, 1, visit, 8)

        def fresh(c, line, parity, e, s):
            q = (e + parity + c) % 2
            near = neighbours(u[1 - c], line, e, s, q, 2, closed)
            flow = neighbours(v[1 - c], line, e, s, q, 2, closed)
            return fs[c, line, e, s] + g[c, line, e, s] * (k[c, line, e, s] * near + flow)

        def relax(c):
            def visit(line, parity):
                for e in range(2):
                    for s in range(2):
                        value = fresh(c, line, parity, e, s)
                        u[c][line, e, s] = value
                        v[c][line, e, s] = k[c, line, e, s] * value

            over_lines(0, height - 1, 1, visit, 8)

        prepare(0)
        prepare(1)
        relax(1)
        relax(0)
        relax(1)

        def restrict(i, carry):
            for s in range(2):
                value, conduct = None, None
                for j in range(2):
                    line = 1 + 2 * i + j
                    for e in range(2):
                        part = half[line, e, s] * (fresh(0, line, j, e, s) - ur[line, e, s])
                        value = part if value is None else value + part
                        part = k[0, line, e, s] + k[1, line, e, s]
                        conduct = part if conduct is None else conduct + part
                f2[s, i] = value * 0.125
                k2[s, i] = conduct * 0.125
            return carry

        lax.fori_loop(0, height2, restrict, 0)

        even = iota(0, depth) % 2 == 0

        def q_is_zero(c, y):
            return even if (y + c) % 2 == 0 else jnp.logical_not(even)

        def coloured(pair, c, y):
            return jnp.where(q_is_zero(c, y), pair[0], pair[1])

        def around(ref, c, y):
            mid = ref[1 + y]
            other = jnp.where(q_is_zero(c, y), shifted(mid, -1, 1), shifted(mid, 1, 1))
            return (mid + other) + (shifted(mid, -1, 0) + shifted(mid, 1, 0)) + (ref[y] + ref[y + 2])

        for c in range(2):
            for line in (0, height2 + 1):
                kc[c, line] = blank
                uc[c, line] = blank
                vc[c, line] = blank
            for y in range(height2):
                kc[c, 1 + y] = coloured((k2[0, y], k2[1, y]), c, y)
                fc[c, y] = coloured((f2[0, y], f2[1, y]), c, y)
        for c in range(2):
            for y in range(height2):
                centre = kc[c, 1 + y]
                total = 6.0 * centre + around(kc.at[1 - c], c, y)
                scale = 1.0 / total
                start = 32.0 * fc[c, y] * scale
                gc[c, y] = scale
                sc[c, y] = start
                if c == 0:
                    hc[y] = total * (0.5 / 16.0)
                    uc[0, 1 + y] = start
                    vc[0, 1 + y] = centre * start

        def fresh2(c, y):
            flow = kc[c, 1 + y] * around(uc.at[1 - c], c, y) + around(vc.at[1 - c], c, y)
            return sc[c, y] + gc[c, y] * flow

        def relax2(c):
            for y in range(height2):
                value = fresh2(c, y)
                uc[c, 1 + y] = value
                vc[c, 1 + y] = kc[c, 1 + y] * value

        relax2(1)
        relax2(0)
        relax2(1)

        def paired(a, b):
            total = (a + b) * 0.125
            return jnp.where(even, total + pltpu.roll(total, depth - 1, axis=0), 0.0)

        conduct = []
        right = []
        for y in range(height3):
            parts = [hc[2 * y + j] * (fresh2(0, 2 * y + j) - uc[0, 1 + 2 * y + j]) for j in range(2)]
            right.append(paired(*parts))
            parts = [kc[0, 1 + 2 * y + j] + kc[1, 1 + 2 * y + j] for j in range(2)]
            conduct.append(paired(*parts))
        moves = ((-2, 0), (2, 0), (-1, 1), (1, 1))
        for y in range(height3):
            centre = conduct[y]
            beside = [shifted(centre, step, axis) for step, axis in moves]
            beside.append(conduct[y - 1] if y else jnp.zeros_like(centre))
            beside.append(conduct[y + 1] if y + 1 < height3 else jnp.zeros_like(centre))
            total = 6.0 * centre
            for part in beside:
                total = total + part
            scale = jnp.where(even, 1.0 / jnp.where(even, total, 1.0), 0.0)
            f3[y] = 128.0 * right[y] * scale
            lane, row = iota(1, depth), iota(0, depth)
            open_faces = (row >= 2, row < depth - 2, lane >= 1, lane < LANES - 1)
            for i in range(6):
                weight = (centre + beside[i]) * scale
                w3[y, i] = jnp.where(open_faces[i], weight, 0.0) if i < 4 else weight
        mixed = (iota(0, depth) // 2 + iota(1, depth)) % 2

        def relax3(c, field):
            result = []
            for y in range(height3):
                mid = field[y]
                value = f3[y]
                for i, (step, axis) in enumerate(moves):
                    value = value + w3[y, i] * pltpu.roll(mid, -step % mid.shape[axis], axis=axis)
                if y:
                    value = value + w3[y, 4] * field[y - 1]
                if y + 1 < height3:
                    value = value + w3[y, 5] * field[y + 1]
                result.append(jnp.where(mixed == (y + c) % 2, value, mid))
            return result

        def two_colours(_, field):
            return tuple(relax3(1, relax3(0, list(field))))

        field = lax.fori_loop(0, 12, two_colours, (blank,) * height3)

        for y in range(height2):
            coarse = field[y // 2]
            value = uc[1, 1 + y] + (coarse + pltpu.roll(coarse, 1, axis=0))
            uc[1, 1 + y] = value
            vc[1, 1 + y] = kc[1, 1 + y] * value
        for c in (0, 1, 0, 1):
            relax2(c)

        for y in range(height2):
            zero = q_is_zero(0, y)
            red, black = uc[0, 1 + y], uc[1, 1 + y]
            f2[0, y] = jnp.where(zero, red, black)
            f2[1, y] = jnp.where(zero, black, red)

        def add(line, parity):
            for e in range(2):
                for s in range(2):
                    value = ub[line, e, s] + f2[s, (line - 1) // 2]
                    ub[line, e, s] = value
                    vb[line, e, s] = k[1, line, e, s] * value

        over_lines(0, height - 1, 1, add, 8)
        for c in (0, 1, 0, 1):
            relax(c)

        for j in range(-3, 7):
            line = 1 + jnp.clip(4 * yplace + j, 0, height - 1)
            for t in range(-3, 7):
                e = t % 2
                at = pl.ds(jnp.clip(2 * zplace + t // 2, 0, depth - 1), 1)
                for s in range(4):
                    row = u[(s + e + j) % 2][line, e, s // 2, at, :]
                    if -2 <= t <= 5:
                        error[j + 3, s, t % 8 : t % 8 + 1, :] = row
                    elif 0 <= j < 8 // 2:
                        errorx[1 if t < 0 else 0, j, s : s + 1, :] = row

    lines, lines2 = (height + 2, 2, 2, depth, LANES), (height2 + 2, depth, LANES)
    flat2 = (2, height2, depth, LANES)
    scratch = [(2, *lines)] * 4 + [lines] * 5 + [flat2, flat2, flat2, (2, *lines2), flat2, flat2]
    scratch += [(2, *lines2), (2, *lines2), flat2[1:], (height3, 6, depth, LANES), (height3, depth, LANES)]
    return body, scratch


def swap_steps(nz, ny, first=None):
    ybits, zbits = ny.bit_length() - 1, nz.bit_length() - 1
    along_y = list(range(ybits - 1, -1, -1))
    if first is not None:
        along_y = [first, *(bit for bit in along_y if bit != first)]
    return [*along_y, *range(ybits + zbits - 1, ybits - 1, -1)]


def swap(block, step, nz, ny):
    return lax.ppermute(block, ("gz", "gy"), [(i, i ^ (1 << step)) for i in range(nz * ny)])


def swapped(block, step, nz, ny):
    return jnp.concatenate([block, swap(block, step, nz, ny)])


def solve_coarse(fmine, ftheirs, kmine, ktheirs, nz, ny):
    body, scratch = coarse_kernel(nz, ny)
    outs = ((10, 4, 8, LANES), (2, 4, 4, LANES))
    return call(body, 11, outs, scratch, fmine, ftheirs, kmine, ktheirs)


def extended(array, sides, width):
    for axis, dim in sides:
        size, length = (lax.axis_size(axis), array.shape[dim])
        up = [(i, (i + 1) % size) for i in range(size - 1)]
        down = [(j, i) for i, j in up]
        last = lax.slice_in_dim(array, length - width, length, axis=dim)
        initial = lax.slice_in_dim(array, 0, width, axis=dim)
        before = lax.ppermute(last, axis, up)
        after = lax.ppermute(initial, axis, down)
        array = jnp.concatenate([before, array, after], axis=dim)
    return array


def coarsen(field):
    total = field[0::2, 0::2, 0::2] + field[0::2, 0::2, 1::2]
    total = total + field[0::2, 1::2, 0::2] + field[0::2, 1::2, 1::2]
    total = total + field[1::2, 0::2, 0::2] + field[1::2, 0::2, 1::2]
    total = total + field[1::2, 1::2, 0::2] + field[1::2, 1::2, 1::2]
    return total * 0.125


def prolong(field):
    return jnp.repeat(jnp.repeat(jnp.repeat(field, 2, axis=0), 2, axis=1), 2, axis=2)


def face_terms(kpad):
    center = kpad[1:-1, 1:-1, 1:-1]
    z_minus = 0.5 * (center + kpad[:-2, 1:-1, 1:-1])
    z_plus = 0.5 * (center + kpad[2:, 1:-1, 1:-1])
    y_minus = 0.5 * (center + kpad[1:-1, :-2, 1:-1])
    y_plus = 0.5 * (center + kpad[1:-1, 2:, 1:-1])
    x_minus = 0.5 * (center + kpad[1:-1, 1:-1, :-2])
    x_plus = 0.5 * (center + kpad[1:-1, 1:-1, 2:])
    total = z_minus + z_plus + y_minus + y_plus + x_minus + x_plus
    return ((z_minus, z_plus, y_minus, y_plus, x_minus, x_plus), total)


def neighbour_sum(weights, upad):
    z_minus, z_plus, y_minus, y_plus, x_minus, x_plus = weights
    acc = z_minus * upad[:-2, 1:-1, 1:-1] + z_plus * upad[2:, 1:-1, 1:-1]
    acc = acc + y_minus * upad[1:-1, :-2, 1:-1] + y_plus * upad[1:-1, 2:, 1:-1]
    acc = acc + x_minus * upad[1:-1, 1:-1, :-2] + x_plus * upad[1:-1, 1:-1, 2:]
    return acc


def extend(field, layout):
    if layout == "column":
        wider = extended(field, (("gy", 1),), 1)
        wider = jnp.pad(wider, ((1, 1), (0, 0), (0, 0)))
    else:
        wider = extended(field, (("gz", 0), ("gy", 1)), 1)
    return jnp.pad(wider, ((0, 0), (0, 0), (1, 1)))


def region_masks(shape, z_start, y_start):
    zpos = lax.broadcasted_iota(jnp.int32, shape, 0) + z_start
    ypos = lax.broadcasted_iota(jnp.int32, shape, 1) + y_start
    xpos = lax.broadcasted_iota(jnp.int32, shape, 2)
    return (zpos + ypos + xpos + 4) % 2


def cycle(rhs, conduct, level, layout, z_start, y_start, z_total, y_total):
    scale = 4.0**level
    weights, total = face_terms(extend(conduct, layout))
    parity = region_masks(rhs.shape, z_start, y_start)
    first = parity == 0
    second = parity == 1

    def relax(field, colour):
        fresh = (scale * rhs + neighbour_sum(weights, extend(field, layout))) / total
        return jnp.where(colour, fresh, field)

    def smooth(field, sweeps):
        for sweep in range(sweeps):
            for colour in (first, second):
                field = relax(field, colour)
        return field

    def remainder(field):
        return rhs - (total * field - neighbour_sum(weights, extend(field, layout))) / scale

    field = jnp.zeros(rhs.shape, jnp.float32)
    if level == LEVELS - 1:
        return (smooth(field, 12), None)
    field = smooth(field, 2)
    rhs_next = coarsen(remainder(field))
    conduct_next = coarsen(conduct)
    joined = layout == "split" and level == 1
    if joined:
        local_depth = rhs_next.shape[0]
        rhs_next, conduct_next = (
            lax.all_gather(rhs_next, "gz", axis=0, tiled=True),
            lax.all_gather(conduct_next, "gz", axis=0, tiled=True),
        )
        error, unused = cycle(
            rhs_next, conduct_next, level + 1, "column", 0, y_start // 2, z_total // 2, y_total // 2
        )
        error = lax.dynamic_slice_in_dim(error, lax.axis_index("gz") * local_depth, local_depth, 0)
    else:
        error, unused = cycle(
            rhs_next,
            conduct_next,
            level + 1,
            layout,
            z_start // 2,
            y_start // 2,
            z_total // 2,
            y_total // 2,
        )
    field = field + prolong(error)
    field = smooth(field, 2)
    return (field, remainder(field))


def natural_coarse(message):
    packed = message.reshape(2, 2, 2, 4, 2, LANES)
    parity = (jnp.arange(2)[:, None, None, None, None] + jnp.arange(4)[None, None, :, None, None]) % 2 == 0
    even = jnp.where(parity, packed[0], packed[1])
    odd = jnp.where(parity, packed[1], packed[0])
    both = jnp.stack([even, odd])
    return both.transpose(4, 1, 3, 5, 2, 0).reshape(4, 4, 4 * LANES)


def solve_coarse_spread(message, kmessage, nz, ny):
    z_start, y_start = 4 * lax.axis_index("gz"), 4 * lax.axis_index("gy")
    field, unused = cycle(
        natural_coarse(message), natural_coarse(kmessage), 1, "split", z_start, y_start, 4 * nz, 4 * ny
    )
    wide = extended(field, (("gz", 0), ("gy", 1)), 3).reshape(10, 10, LANES, 4).transpose(1, 3, 0, 2)
    error = jnp.concatenate([wide[:, :, 3:9], wide[:, :, 1:3]], axis=2)
    return error, jnp.stack([wide[3:7, :, 9], wide[3:7, :, 0]])


def exchange(first, second, axis):
    size = lax.axis_size(axis)
    results = []
    for message, start in ((first, 0), (second, 1)):
        pairs = [(i, i + 1) for i in range(start, size - 1, 2)]
        results.append(lax.ppermute(message, axis, pairs + [(j, i) for i, j in pairs]))
    return results


def on_device(right_side, coefficient):
    nz, ny = lax.axis_size("gz"), lax.axis_size("gy")
    assert right_side.shape == (8, 8, 8 * LANES)
    cells = (2, 2, 8, 2, 4, 4, LANES)
    yface, zface = (16, 2, 4, 4, LANES), (8, 4, 16, LANES)
    coarse = (8, 8, LANES)
    packed = call(pack_kernel, 3, (cells, yface, yface), [(2, 8, 64, LANES)], right_side, coefficient)
    local, ya, yb = packed
    ya, yb = exchange(ya, yb, "gy")
    za, zb, kmessage = call(zpack_kernel, 2, (zface, zface, coarse), [], local)
    za, zb = exchange(za, zb, "gz")
    coarse_cells = 8 * 8 * LANES
    whole = nz * ny * coarse_cells <= WHOLE_COARSE_CELLS and nz & (nz - 1) == 0 and ny & (ny - 1) == 0
    swaps, kswaps = swap_steps(nz, ny), swap_steps(nz, ny, 0)
    kall = kmessage[None]
    if whole:
        kall = swapped(kall, kswaps[0], nz, ny)
        ya, yb, kall = lax.optimization_barrier((ya, yb, kall))
    relayed = (8 * CORNER_ROWS, LANES)
    scratch = [(2, *yface), pltpu.SemaphoreType.DMA((2,))]
    far = [pl.BlockSpec(memory_space=pl.ANY)] * 2
    ca, cb = exchange(*call(relay_kernel, 2, (relayed, relayed), scratch, ya, yb, specs=far), "gz")
    if whole:
        for step in kswaps[1:-2]:
            kall = swapped(kall, step, nz, ny)
        ca, cb, za, zb, kall = lax.optimization_barrier((ca, cb, za, zb, kall))
        kall = swapped(kall, kswaps[-2], nz, ny)
    lines, zface = (LINES, 2, 4, 8, LANES), (160, LANES)
    outs = ((2, *lines), (2, *lines), (2, *lines), (8, *lines[1:]), lines, (2, 8, 4, LANES), zface, zface, coarse)
    scratch = [(2, *lines), lines, lines, lines]
    k, g, fs, half, ub, kx, zc, zd, message = call(down_kernel, 6, outs, scratch, local, ya, yb, za, zb, ca, cb)
    fall, half_way = message[None], len(swaps) // 2
    if whole:
        fall, kall = lax.optimization_barrier((fall, kall))
        ktheirs = swap(kall, kswaps[-1], nz, ny)
    zc, zd = exchange(zc, zd, "gz")
    if whole:
        for step in swaps[:half_way]:
            fall = swapped(fall, step, nz, ny)
        fall, zc, zd = lax.optimization_barrier((fall, zc, zd))
    yface = (5, *lines[1:])
    wide, yc, yd = call(widen_kernel, 2, ((8, *lines[1:]), yface, yface), [], ub, zc, zd)
    if whole:
        fall = swapped(fall, swaps[half_way], nz, ny)
        fall, yc, yd = lax.optimization_barrier((fall, yc, yd))
    yc, yd = exchange(yc, yd, "gy")
    if whole:
        for step in swaps[half_way + 1 : -1]:
            fall = swapped(fall, step, nz, ny)
        fall, yc, yd = lax.optimization_barrier((fall, yc, yd))
        ftheirs = swap(fall, swaps[-1], nz, ny)
        error, errorx = solve_coarse(fall, ftheirs, kall, ktheirs, nz, ny)
    else:
        error, errorx = solve_coarse_spread(message, kmessage, nz, ny)
    block = (8, 8, 8 * LANES)
    scratch = [lines] * 4 + [(2, 8, 4, LANES)] * 2 + [(2, 8, 64, LANES)]
    return call(up_kernel, 6, (block, block), scratch, k, g, fs, half, wide, kx, yc, yd, zc, zd, error, errorx)


def solution(mesh):
    spec = P("gz", "gy", None)
    return jax.shard_map(
        on_device, mesh=mesh, in_specs=(spec, spec), out_specs=(spec, spec), check_vma=False
    )
```

```python
import jax
import jax.numpy as jnp
from jax import lax
from jax.experimental import pallas as pl
from jax.experimental.pallas import tpu as pltpu
from jax.sharding import PartitionSpec as P

LANES = 128
LINES = 18
LEVELS = 4
PAD = 5
F32 = jnp.float32
VMEM = pl.BlockSpec(memory_space=pltpu.VMEM)
FAR = pl.BlockSpec(memory_space=pl.ANY)
WHOLE_COARSE_CELLS = 1 << 19


def call(body, micros, outs, scratch, *args, specs=None):
    return pl.pallas_call(
        body,
        out_shape=[jax.ShapeDtypeStruct(s, F32) for s in outs],
        in_specs=specs or [VMEM] * len(args),
        out_specs=[VMEM] * len(outs),
        scratch_shapes=[pltpu.VMEM(s, F32) if isinstance(s, tuple) else s for s in scratch],
        cost_estimate=pl.CostEstimate(flops=0, transcendentals=0, bytes_accessed=micros * 3_000_000),
        compiler_params=pltpu.CompilerParams(vmem_limit_bytes=56 << 20),
    )(*args)


def iota(axis, rows=8):
    return lax.broadcasted_iota(jnp.int32, (rows, LANES), axis)


def barrel(arrays, block):
    for bit in (1, 2, 4):
        high = (block & bit) != 0
        arrays = [jnp.where(high, arrays[(j + bit) % 8], arrays[j]) for j in range(8)]
    return arrays


def lane_gather(array, index):
    return jnp.take_along_axis(array, index, axis=1, mode="promise_in_bounds")


def split_lanes(tiles):
    lane = iota(1)
    block = lane // 16
    parts = [lane_gather(tiles[t], 8 * (lane % 16) + (block - t) % 8) for t in range(8)]
    mixed = barrel(parts, block)
    return [pltpu.roll(mixed[-s % 8], (-16 * s) % LANES, axis=1) for s in range(8)]


def join_lanes(arrays):
    lane = iota(1)
    block = lane // 16
    moved = [pltpu.roll(arrays[s], (16 * s) % LANES, axis=1) for s in range(8)]
    mixed = barrel(moved, block)
    return [lane_gather(mixed[-t % 8], 16 * ((lane % 8 + t) % 8) + lane // 8) for t in range(8)]


def put_coarse(message, row, s, value, tail=None):
    for z in range(4):
        e, c = z % 2, (s + z + row) % 2
        m, at = (c * 2 + e) * 2 + s // 2, 2 * row + z // 2
        message[m, at, :] = value[z]
        if tail is not None:
            tail[FACE_ROWS + 8 * m + at, :] = value[z]


REACH = ((0, 0, 4), (0, 1, 3), (1, 0, 4), (1, 1, 5))
YFACE = [(a, c, y, n) for a, c, n in REACH for y in range(n)]
ZFACE = sorted(((a, c, d) for a, c, n in REACH for d in range(1, n + 1)), key=lambda r: r[2] - REACH[2 * r[0] + r[1]][2])
CORNER = {1: (12, 0, 12), 2: (8, 16, 8), 3: (4, 12, 4), 4: (1, 24, 4)}
CORNER_ROWS = 28
FACE_ROWS = 5 * 2 * 4 * 4
DEPTHS = [min(i, 5, LINES - 1 - i) for i in range(LINES)]
ZSTARTS = [4 * sum(DEPTHS[:i]) for i in range(LINES)]
ZROWS = 4 * sum(DEPTHS)


def own_sides():
    return [lax.rem(lax.axis_index(axis), 2) == 0 for axis in ("gz", "gy")]


def halo_cell(side, distance):
    z = 7 + distance if side == 0 else -distance
    return z % 2, (z // 2) % 8


def pick(flag, a, b):
    return jnp.where(flag, a, b), jnp.where(flag, b, a)


def pack_kernel(f_ref, k_ref, local, ya, yb, natural):
    _, yup = own_sides()
    for a, ref in enumerate((f_ref, k_ref)):
        for z in range(8):
            arrays = split_lanes([ref[z, :, t * LANES : (t + 1) * LANES] for t in range(8)])
            for s in range(8):
                natural[a, s, 8 * z : 8 * z + 8, :] = arrays[s]
    for a in range(2):
        for c in range(2):
            for y in range(8):
                for e in range(2):
                    q = (e + y + c) % 2
                    for s in range(4):
                        local[a, c, y, e, s] = natural[a, 2 * s + q, pl.ds(y + 8 * e, 4, stride=16), :]
    for i, (a, c, y, n) in enumerate(YFACE):
        first, second = pick(yup, y + 8 - n, y)
        ya[i] = local[a, c, first]
        yb[i] = local[a, c, second]


def zpack_kernel(local, za, zb, coarse):
    zup, _ = own_sides()

    def faces(y, carry):
        for i, (a, c, d) in enumerate(ZFACE):
            high, low = 8 - d, d - 1
            for s in range(4):
                up = local[a, c, y, high % 2, s, high // 2 : high // 2 + 1]
                down = local[a, c, y, low % 2, s, low // 2 : low // 2 + 1]
                za[y, s, i : i + 1], zb[y, s, i : i + 1] = pick(zup, up, down)
        return carry

    lax.fori_loop(0, 8, faces, 0)
    for row in range(4):
        for s in range(4):
            total = None
            for c in range(2):
                for y in (2 * row, 2 * row + 1):
                    pair = local[1, c, y, 0, s] + local[1, c, y, 1, s]
                    total = pair if total is None else total + pair
            put_coarse(coarse, row, s, total * 0.125)


def relay_kernel(ya_far, yb_far, ca, cb, faces, sem):
    zup, yabove = own_sides()
    slots = pick(yabove, 0, 1)
    copies = [pltpu.make_async_copy(f, faces.at[t], sem.at[i]) for i, (f, t) in enumerate(zip((ya_far, yb_far), slots))]
    for copy in copies:
        copy.start()
    for copy in copies:
        copy.wait()
    for target, up in ((ca, zup), (cb, jnp.logical_not(zup))):
        places = {d: jnp.where(up, 8 - d, d - 1) for d in range(1, 5)}
        for d, (count, at, _) in CORNER.items():
            for i, (a, c, dz) in enumerate(ZFACE[:count]):
                e, t = lax.rem(places[dz], 2), places[dz] // 2
                for side in range(2):
                    y = d - 1 if side == 0 else REACH[2 * a + c][2] - d
                    line = YFACE.index((a, c, y, REACH[2 * a + c][2]))
                    for s in range(4):
                        base = (4 * side + s) * CORNER_ROWS + at + i
                        target[base : base + 1, :] = faces[side, line, e, s, pl.ds(t, 1)]


def neighbours(ref, line, e, s, q, groups, edge=None, first=None, last=None):
    rows = ref.shape[-2]
    lane = iota(1, rows)
    same = ref[line, e, s]
    if q == 0 and s == 0:
        other = jnp.where(lane == 0, 0.0, pltpu.roll(ref[line, e, groups - 1], 1, axis=1))
    elif q == 1 and s == groups - 1:
        other = jnp.where(lane == LANES - 1, 0.0, pltpu.roll(ref[line, e, 0], LANES - 1, axis=1))
    else:
        other = ref[line, e, s + (1 if q else -1)]
    zsame = ref[line, 1 - e, s]
    zother = pltpu.roll(zsame, 1 if e == 0 else rows - 1, axis=0)
    if edge is not None:
        zother = edge(zother, line, e, s)
    return (same + other) + (zsame + zother) + (ref[line - 1, e, s] + ref[line + 1, e, s])


def closed(zother, line, e, s):
    rows = zother.shape[0]
    return jnp.where(iota(0, rows) == (0 if e == 0 else rows - 1), 0.0, zother)


def over_lines(low, high, offset, visit, lines=4):
    steps, rest = divmod(high - low + 1, lines)

    def step(i, carry):
        for j in range(lines):
            visit(low + offset + j + lines * i, (low + j) % 2)
        return carry

    lax.fori_loop(0, steps, step, 0)
    for y in range(high + 1 - rest, high + 1):
        visit(y + offset, y % 2)


def diagonal(k, kother, line, e, s, q, groups, edge=None):
    centre = k[line, e, s]
    return centre, 6.0 * centre + neighbours(kother, line, e, s, q, groups, edge)


def down_kernel(
    local, ya, yb, za, zb, ca_far, cb_far,
    k, g, fs, half, ub, kx, yc, yd, coarse,
    f, ur, vr, vb, ca, cb, sem,
):
    zabove, yabove = own_sides()
    yup = yabove
    copies = [pltpu.make_async_copy(*pair, sem.at[i]) for i, pair in enumerate(((ca_far, ca), (cb_far, cb)))]
    for copy in copies:
        copy.start()
    blank = jnp.zeros((8, LANES), F32)
    for c in range(2):
        for line in (*range(PAD), *range(PAD + 8, LINES)):
            for e in range(2):
                for s in range(4):
                    k[c, line, e, s] = blank
                    f[c, line, e, s] = blank
    both = (f, k)

    def assemble(y, carry):
        for e in range(2):
            for s in range(4):
                f[1, PAD + y, e, s] = blank
                for a in range(2):
                    for c in range(2):
                        both[a][c, PAD + y, e, s, 0:4] = local[a, c, y, e, s]
        for s in range(4):
            for side, part in enumerate(pick(zabove, za[y, s], zb[y, s])):
                for i, (a, c, d) in enumerate(ZFACE):
                    e, row = halo_cell(side, d)
                    if d == 5:
                        kx[side, y, s : s + 1] = part[i : i + 1]
                    else:
                        both[a][c, PAD + y, e, s, row : row + 1] = part[i : i + 1]
        return carry

    lax.fori_loop(0, 8, assemble, 0)
    for i, (a, c, y, n) in enumerate(YFACE):
        first, second = pick(yabove, PAD + y + 8, PAD + y - n)
        for e in range(2):
            for s in range(4):
                both[a][c, first, e, s, 0:4] = ya[i, e, s]
                both[a][c, second, e, s, 0:4] = yb[i, e, s]
    for copy in copies:
        copy.wait()
    for yside in range(2):
        for s in range(4):
            for d, (count, at, _) in CORNER.items():
                line, base = PAD + 7 + d if yside == 0 else PAD - d, (4 * yside + s) * CORNER_ROWS + at
                for side, part in enumerate(pick(zabove, ca[base : base + count, :], cb[base : base + count, :])):
                    for i, (a, c, dz) in enumerate(ZFACE[:count]):
                        e, row = halo_cell(side, dz)
                        both[a][c, line, e, s, row : row + 1] = part[i : i + 1]

    rows = iota(0)

    def far(zother, line, e, s):
        beyond = kx[1 - e, line - PAD, s : s + 1]
        return jnp.where(rows == (6 if e == 0 else 5), jnp.broadcast_to(beyond, (8, LANES)), zother)

    def prepare(c, line, parity, edge, keep):
        for e in range(2):
            q = (e + parity + c) % 2
            for s in range(4):
                centre, total = diagonal(k.at[c], k.at[1 - c], line, e, s, q, 4, edge)
                inside = centre != 0.0
                scale = jnp.where(inside, 1.0 / jnp.where(inside, total, 1.0), 0.0)
                start = 2.0 * f[c, line, e, s] * scale
                g[c, line, e, s] = scale
                fs[c, line, e, s] = start
                if keep:
                    half[line - PAD, e, s] = 0.5 * total
                if c == 0:
                    ur[line, e, s] = start
                    vr[line, e, s] = centre * start

    over_lines(-4, -1, PAD, lambda line, parity: prepare(0, line, parity, None, False))
    over_lines(8, 11, PAD, lambda line, parity: prepare(0, line, parity, None, False))
    over_lines(0, 7, PAD, lambda line, parity: prepare(0, line, parity, far, True))
    over_lines(-3, 10, PAD, lambda line, parity: prepare(1, line, parity, None, False))

    def relax(c, low, high):
        sweep(c, low, high, k, g, fs, (ur, ub), (vr, vb))

    relax(1, -3, 10)
    relax(0, -2, 9)
    relax(1, -1, 8)

    for row in range(4):
        for s in range(4):
            total = None
            for y in (2 * row, 2 * row + 1):
                for e in range(2):
                    line = PAD + y
                    value = red_residual(line, y % 2, e, s, k, g, fs, half, ur, ub, vb)
                    total = value if total is None else total + value
            put_coarse(coarse, row, s, total * 0.125, yc)

    first, second = pick(yup, PAD + 3, PAD)
    for i in range(5):
        for e in range(2):
            for s in range(4):
                at = ((i * 2 + e) * 4 + s) * 4
                yc[at : at + 4, :] = ub[first + i, e, s, 0:4]
                yd[at : at + 4, :] = ub[second + i, e, s, 0:4]


def widen_kernel(ub, yc_far, yd_far, zc, zd, faces, sem):
    zup, yabove = own_sides()
    slots, face = pick(yabove, 0, 1), pl.ds(0, FACE_ROWS)
    copies = [
        pltpu.make_async_copy(f.at[face], faces.at[t], sem.at[i]) for i, (f, t) in enumerate(zip((yc_far, yd_far), slots))
    ]
    for copy in copies:
        copy.start()

    def put(line, fetch):
        for target, up in ((zc, zup), (zd, jnp.logical_not(zup))):
            for d in range(1, DEPTHS[line] + 1):
                z = jnp.where(up, 8 - d, d - 1)
                for s in range(4):
                    at = ZSTARTS[line] + s * DEPTHS[line] + d - 1
                    target[at : at + 1, :] = fetch(lax.rem(z, 2), s, z // 2)

    for line in range(PAD, PAD + 8):
        put(line, lambda e, s, t: ub[line, e, s, pl.ds(t, 1)])
    for copy in copies:
        copy.wait()
    for i in range(5):
        for side, line in enumerate((PAD + 8 + i, i)):
            put(line, lambda e, s, t: faces[side, pl.ds(((i * 2 + e) * 4 + s) * 4 + t, 1), :])


def sweep(c, low, high, k, g, fs, u, v, edges=(None, None)):
    def visit(line, parity):
        for e in range(2):
            q = (e + parity + c) % 2
            for s in range(4):
                near = neighbours(u[1 - c], line, e, s, q, 4, edges[0])
                flow = neighbours(v[1 - c], line, e, s, q, 4, edges[1])
                centre = k[c, line, e, s]
                value = fs[c, line, e, s] + g[c, line, e, s] * (centre * near + flow)
                u[c][line, e, s] = value
                v[c][line, e, s] = centre * value

    over_lines(low, high, PAD, visit)


def red_residual(line, parity, e, s, k, g, fs, half, ur, ub, vb):
    q = (e + parity) % 2
    near = neighbours(ub, line, e, s, q, 4)
    flow = neighbours(vb, line, e, s, q, 4)
    fresh = fs[0, line, e, s] + g[0, line, e, s] * (k[0, line, e, s] * near + flow)
    return half[line - PAD, e, s] * (fresh - ur[line, e, s])


def up_kernel(
    k, g, fs, half, old, kx, yc, yd, zc, zd, error, errorx,
    correction, residual,
    ub, ur, vb, vr, ux, vx, natural,
):
    zabove, yabove = own_sides()
    for y in range(8):
        for e in range(2):
            for s in range(4):
                ub[PAD + y, e, s, 0:4] = old[PAD + y, e, s, 0:4]
    first, second = pick(yabove, PAD + 8, 0)
    for i in range(5):
        for e in range(2):
            for s in range(4):
                at = ((i * 2 + e) * 4 + s) * 4
                ub[first + i, e, s, 0:4] = yc[at : at + 4, :]
                ub[second + i, e, s, 0:4] = yd[at : at + 4, :]
    quiet = jnp.zeros((4, LANES), F32)
    for line, depth in enumerate(DEPTHS):
        for s in range(4):
            if depth < 4:
                for e in range(2):
                    ub[line, e, s, 4:8] = quiet
            if not depth:
                continue
            at = ZSTARTS[line] + s * depth
            for side, part in enumerate(pick(zabove, zc[at : at + depth, :], zd[at : at + depth, :])):
                for d in range(1, min(depth, 4) + 1):
                    e, row = halo_cell(side, d)
                    ub[line, e, s, row : row + 1] = part[d - 1 : d]
                if depth == 5:
                    y = line - PAD
                    beyond = kx[side, y, s : s + 1]
                    value = part[4:5] + errorx[side, y // 2, s : s + 1]
                    value = jnp.where(beyond != 0.0, value, 0.0)
                    ux[side, y, s : s + 1] = value
                    vx[side, y, s : s + 1] = beyond * value

    def add(line, parity):
        for e in range(2):
            for s in range(4):
                centre = k[1, line, e, s]
                value = ub[line, e, s] + error[(line + 1) // 2, s]
                value = jnp.where(centre != 0.0, value, 0.0)
                ub[line, e, s] = value
                vb[line, e, s] = centre * value

    over_lines(-5, 12, PAD, add)

    rows = iota(0)

    def far(ref):
        def edge(zother, line, e, s):
            beyond = ref[1 - e, line - PAD, s : s + 1]
            return jnp.where(rows == (6 if e == 0 else 5), jnp.broadcast_to(beyond, (8, LANES)), zother)

        return edge

    u, v = (ur, ub), (vr, vb)
    sweep(0, -4, -1, k, g, fs, u, v)
    sweep(0, 8, 11, k, g, fs, u, v)
    sweep(0, 0, 7, k, g, fs, u, v, (far(ux), far(vx)))
    sweep(1, -3, 10, k, g, fs, u, v)
    sweep(0, -2, 9, k, g, fs, u, v)
    sweep(1, -1, 8, k, g, fs, u, v)

    quiet = jnp.zeros((4, LANES), F32)
    for y in range(8):
        for e in range(2):
            at = pl.ds(y + 8 * e, 4, stride=16)
            q = (e + y) % 2
            for s in range(4):
                value = red_residual(PAD + y, y % 2, e, s, k, g, fs, half, ur, ub, vb)
                natural[1, 2 * s + q, at, :] = value[0:4]
                natural[1, 2 * s + 1 - q, at, :] = quiet
                natural[0, 2 * s + q, at, :] = ur[PAD + y, e, s, 0:4]
                natural[0, 2 * s + 1 - q, at, :] = ub[PAD + y, e, s, 0:4]
    for a, out in enumerate((correction, residual)):
        for z in range(8):
            tiles = join_lanes([natural[a, s, 8 * z : 8 * z + 8, :] for s in range(8)])
            for t in range(8):
                out[z, :, t * LANES : (t + 1) * LANES] = tiles[t]


def shifted(value, step, axis):
    size = value.shape[axis]
    where = iota(axis, value.shape[0])
    moved = pltpu.roll(value, -step % size, axis=axis)
    return jnp.where((where >= size - step) if step > 0 else (where < -step), 0.0, moved)


def coarse_kernel(nz, ny):
    height, depth = 4 * ny, 2 * nz
    height2, height3 = height // 2, height // 4

    def body(
        fmine, ftheirs_far, kmine, ktheirs, error, errorx,
        f, k, g, fs, half, ur, ub, vr, vb, f2, k2, fc, kc, gc, sc, uc, vc, hc, w3, f3, ftheirs, sem,
    ):
        u, v = (ur, ub), (vr, vb)
        zplace, yplace = lax.axis_index("gz"), lax.axis_index("gy")

        def slot(i, j, swaps):
            apart = (zplace * ny + yplace) ^ (i * ny + j)
            return sum(((apart >> step) & 1) << bit for bit, step in enumerate(swaps[:-1]))

        def spread(odd, sources, target, swaps):
            def visit(j, carry):
                order = [slot(i, j, swaps) for i in range(nz)]
                for m in range(8):
                    pieces = [sources[(i + odd) % 2][order[i], m] for i in range(nz)]
                    for row in range(4):
                        whole = jnp.concatenate([p[2 * row : 2 * row + 2] for p in pieces], axis=0)
                        target[m // 4, 1 + 4 * j + row, m // 2 % 2, m % 2] = whole
                return carry

            lax.fori_loop(0, ny, visit, 0)

        def spread_either(*args):
            for odd in range(2):
                pl.when(lax.rem(zplace, 2) == odd)(lambda odd=odd: spread(odd, *args))

        copy = pltpu.make_async_copy(ftheirs_far, ftheirs, sem)
        copy.start()
        spread_either((kmine, ktheirs), k, swap_steps(nz, ny))
        copy.wait()
        spread_either((fmine, ftheirs), f, swap_steps(nz, ny, 0))
        blank = jnp.zeros((depth, LANES), F32)
        for line in (0, height + 1):
            for e in range(2):
                for s in range(2):
                    for c in range(2):
                        k[c, line, e, s] = blank
                        u[c][line, e, s] = blank
                        v[c][line, e, s] = blank

        def prepare(c):
            def visit(line, parity):
                for e in range(2):
                    for s in range(2):
                        centre, total = diagonal(k.at[c], k.at[1 - c], line, e, s, (e + parity + c) % 2, 2, closed)
                        scale = 1.0 / total
                        start = 8.0 * f[c, line, e, s] * scale
                        g[c, line, e, s] = scale
                        fs[c, line, e, s] = start
                        if c == 0:
                            half[line, e, s] = 0.125 * total
                            ur[line, e, s] = start
                            vr[line, e, s] = centre * start

            over_lines(0, height - 1, 1, visit, 8)

        def fresh(c, line, parity, e, s):
            q = (e + parity + c) % 2
            near = neighbours(u[1 - c], line, e, s, q, 2, closed)
            flow = neighbours(v[1 - c], line, e, s, q, 2, closed)
            return fs[c, line, e, s] + g[c, line, e, s] * (k[c, line, e, s] * near + flow)

        def relax(c):
            def visit(line, parity):
                for e in range(2):
                    for s in range(2):
                        value = fresh(c, line, parity, e, s)
                        u[c][line, e, s] = value
                        v[c][line, e, s] = k[c, line, e, s] * value

            over_lines(0, height - 1, 1, visit, 8)

        prepare(0)
        prepare(1)
        relax(1)
        relax(0)
        relax(1)

        def restrict(i, carry):
            for s in range(2):
                value, conduct = None, None
                for j in range(2):
                    line = 1 + 2 * i + j
                    for e in range(2):
                        part = half[line, e, s] * (fresh(0, line, j, e, s) - ur[line, e, s])
                        value = part if value is None else value + part
                        part = k[0, line, e, s] + k[1, line, e, s]
                        conduct = part if conduct is None else conduct + part
                f2[s, i] = value * 0.125
                k2[s, i] = conduct * 0.125
            return carry

        lax.fori_loop(0, height2, restrict, 0)

        even = iota(0, depth) % 2 == 0

        def q_is_zero(c, y):
            return even if (y + c) % 2 == 0 else jnp.logical_not(even)

        def coloured(pair, c, y):
            return jnp.where(q_is_zero(c, y), pair[0], pair[1])

        def around(ref, c, y):
            mid = ref[1 + y]
            other = jnp.where(q_is_zero(c, y), shifted(mid, -1, 1), shifted(mid, 1, 1))
            return (mid + other) + (shifted(mid, -1, 0) + shifted(mid, 1, 0)) + (ref[y] + ref[y + 2])

        for c in range(2):
            for line in (0, height2 + 1):
                kc[c, line] = blank
                uc[c, line] = blank
                vc[c, line] = blank
            for y in range(height2):
                kc[c, 1 + y] = coloured((k2[0, y], k2[1, y]), c, y)
                fc[c, y] = coloured((f2[0, y], f2[1, y]), c, y)
        for c in range(2):
            for y in range(height2):
                centre = kc[c, 1 + y]
                total = 6.0 * centre + around(kc.at[1 - c], c, y)
                scale = 1.0 / total
                start = 32.0 * fc[c, y] * scale
                gc[c, y] = scale
                sc[c, y] = start
                if c == 0:
                    hc[y] = total * (0.5 / 16.0)
                    uc[0, 1 + y] = start
                    vc[0, 1 + y] = centre * start

        def fresh2(c, y):
            flow = kc[c, 1 + y] * around(uc.at[1 - c], c, y) + around(vc.at[1 - c], c, y)
            return sc[c, y] + gc[c, y] * flow

        def relax2(c):
            for y in range(height2):
                value = fresh2(c, y)
                uc[c, 1 + y] = value
                vc[c, 1 + y] = kc[c, 1 + y] * value

        relax2(1)
        relax2(0)
        relax2(1)

        def paired(a, b):
            total = (a + b) * 0.125
            return jnp.where(even, total + pltpu.roll(total, depth - 1, axis=0), 0.0)

        conduct = []
        right = []
        for y in range(height3):
            parts = [hc[2 * y + j] * (fresh2(0, 2 * y + j) - uc[0, 1 + 2 * y + j]) for j in range(2)]
            right.append(paired(*parts))
            parts = [kc[0, 1 + 2 * y + j] + kc[1, 1 + 2 * y + j] for j in range(2)]
            conduct.append(paired(*parts))
        moves = ((-2, 0), (2, 0), (-1, 1), (1, 1))
        for y in range(height3):
            centre = conduct[y]
            beside = [shifted(centre, step, axis) for step, axis in moves]
            beside.append(conduct[y - 1] if y else jnp.zeros_like(centre))
            beside.append(conduct[y + 1] if y + 1 < height3 else jnp.zeros_like(centre))
            total = 6.0 * centre
            for part in beside:
                total = total + part
            scale = jnp.where(even, 1.0 / jnp.where(even, total, 1.0), 0.0)
            f3[y] = 128.0 * right[y] * scale
            lane, row = iota(1, depth), iota(0, depth)
            open_faces = (row >= 2, row < depth - 2, lane >= 1, lane < LANES - 1)
            for i in range(6):
                weight = (centre + beside[i]) * scale
                w3[y, i] = jnp.where(open_faces[i], weight, 0.0) if i < 4 else weight
        mixed = (iota(0, depth) // 2 + iota(1, depth)) % 2

        def relax3(c, field):
            result = []
            for y in range(height3):
                mid = field[y]
                value = f3[y]
                for i, (step, axis) in enumerate(moves):
                    value = value + w3[y, i] * pltpu.roll(mid, -step % mid.shape[axis], axis=axis)
                if y:
                    value = value + w3[y, 4] * field[y - 1]
                if y + 1 < height3:
                    value = value + w3[y, 5] * field[y + 1]
                result.append(jnp.where(mixed == (y + c) % 2, value, mid))
            return result

        def two_colours(_, field):
            return tuple(relax3(1, relax3(0, list(field))))

        field = lax.fori_loop(0, 12, two_colours, (blank,) * height3)

        for y in range(height2):
            coarse = field[y // 2]
            value = uc[1, 1 + y] + (coarse + pltpu.roll(coarse, 1, axis=0))
            uc[1, 1 + y] = value
            vc[1, 1 + y] = kc[1, 1 + y] * value
        for c in (0, 1, 0, 1):
            relax2(c)

        for y in range(height2):
            zero = q_is_zero(0, y)
            red, black = uc[0, 1 + y], uc[1, 1 + y]
            f2[0, y] = jnp.where(zero, red, black)
            f2[1, y] = jnp.where(zero, black, red)

        def add(line, parity):
            for e in range(2):
                for s in range(2):
                    value = ub[line, e, s] + f2[s, (line - 1) // 2]
                    ub[line, e, s] = value
                    vb[line, e, s] = k[1, line, e, s] * value

        over_lines(0, height - 1, 1, add, 8)
        for c in (0, 1, 0, 1):
            relax(c)

        for j in range(-3, 7):
            line = 1 + jnp.clip(4 * yplace + j, 0, height - 1)
            for t in range(-3, 7):
                e = t % 2
                at = pl.ds(jnp.clip(2 * zplace + t // 2, 0, depth - 1), 1)
                for s in range(4):
                    row = u[(s + e + j) % 2][line, e, s // 2, at, :]
                    if -2 <= t <= 5:
                        error[j + 3, s, t % 8 : t % 8 + 1, :] = row
                    elif 0 <= j < 8 // 2:
                        errorx[1 if t < 0 else 0, j, s : s + 1, :] = row

    lines, lines2 = (height + 2, 2, 2, depth, LANES), (height2 + 2, depth, LANES)
    flat2 = (2, height2, depth, LANES)
    scratch = [(2, *lines)] * 4 + [lines] * 5 + [flat2, flat2, flat2, (2, *lines2), flat2, flat2]
    scratch += [(2, *lines2), (2, *lines2), flat2[1:], (height3, 6, depth, LANES), (height3, depth, LANES)]
    scratch += [(nz * ny // 2, 8, 8, LANES), pltpu.SemaphoreType.DMA(())]
    return body, scratch


def swap_steps(nz, ny, first=None):
    ybits, zbits = ny.bit_length() - 1, nz.bit_length() - 1
    along_y = list(range(ybits - 1, -1, -1))
    if first is not None:
        along_y = [first, *(bit for bit in along_y if bit != first)]
    return [*along_y, *range(ybits + zbits - 1, ybits - 1, -1)]


def swap(block, step, nz, ny):
    return lax.ppermute(block, ("gz", "gy"), [(i, i ^ (1 << step)) for i in range(nz * ny)])


def swapped(block, step, nz, ny):
    return jnp.concatenate([block, swap(block, step, nz, ny)])


def solve_coarse(fmine, ftheirs, kmine, ktheirs, nz, ny):
    body, scratch = coarse_kernel(nz, ny)
    outs = ((10, 4, 8, LANES), (2, 4, 4, LANES))
    return call(body, 11, outs, scratch, fmine, ftheirs, kmine, ktheirs, specs=[VMEM, FAR, VMEM, VMEM])


def extended(array, sides, width):
    for axis, dim in sides:
        size, length = (lax.axis_size(axis), array.shape[dim])
        up = [(i, (i + 1) % size) for i in range(size - 1)]
        down = [(j, i) for i, j in up]
        last = lax.slice_in_dim(array, length - width, length, axis=dim)
        initial = lax.slice_in_dim(array, 0, width, axis=dim)
        before = lax.ppermute(last, axis, up)
        after = lax.ppermute(initial, axis, down)
        array = jnp.concatenate([before, array, after], axis=dim)
    return array


def coarsen(field):
    total = field[0::2, 0::2, 0::2] + field[0::2, 0::2, 1::2]
    total = total + field[0::2, 1::2, 0::2] + field[0::2, 1::2, 1::2]
    total = total + field[1::2, 0::2, 0::2] + field[1::2, 0::2, 1::2]
    total = total + field[1::2, 1::2, 0::2] + field[1::2, 1::2, 1::2]
    return total * 0.125


def prolong(field):
    return jnp.repeat(jnp.repeat(jnp.repeat(field, 2, axis=0), 2, axis=1), 2, axis=2)


def face_terms(kpad):
    center = kpad[1:-1, 1:-1, 1:-1]
    z_minus = 0.5 * (center + kpad[:-2, 1:-1, 1:-1])
    z_plus = 0.5 * (center + kpad[2:, 1:-1, 1:-1])
    y_minus = 0.5 * (center + kpad[1:-1, :-2, 1:-1])
    y_plus = 0.5 * (center + kpad[1:-1, 2:, 1:-1])
    x_minus = 0.5 * (center + kpad[1:-1, 1:-1, :-2])
    x_plus = 0.5 * (center + kpad[1:-1, 1:-1, 2:])
    total = z_minus + z_plus + y_minus + y_plus + x_minus + x_plus
    return ((z_minus, z_plus, y_minus, y_plus, x_minus, x_plus), total)


def neighbour_sum(weights, upad):
    z_minus, z_plus, y_minus, y_plus, x_minus, x_plus = weights
    acc = z_minus * upad[:-2, 1:-1, 1:-1] + z_plus * upad[2:, 1:-1, 1:-1]
    acc = acc + y_minus * upad[1:-1, :-2, 1:-1] + y_plus * upad[1:-1, 2:, 1:-1]
    acc = acc + x_minus * upad[1:-1, 1:-1, :-2] + x_plus * upad[1:-1, 1:-1, 2:]
    return acc


def extend(field, layout):
    if layout == "column":
        wider = extended(field, (("gy", 1),), 1)
        wider = jnp.pad(wider, ((1, 1), (0, 0), (0, 0)))
    else:
        wider = extended(field, (("gz", 0), ("gy", 1)), 1)
    return jnp.pad(wider, ((0, 0), (0, 0), (1, 1)))


def region_masks(shape, z_start, y_start):
    zpos = lax.broadcasted_iota(jnp.int32, shape, 0) + z_start
    ypos = lax.broadcasted_iota(jnp.int32, shape, 1) + y_start
    xpos = lax.broadcasted_iota(jnp.int32, shape, 2)
    return (zpos + ypos + xpos + 4) % 2


def cycle(rhs, conduct, level, layout, z_start, y_start, z_total, y_total):
    scale = 4.0**level
    weights, total = face_terms(extend(conduct, layout))
    parity = region_masks(rhs.shape, z_start, y_start)
    first = parity == 0
    second = parity == 1

    def relax(field, colour):
        fresh = (scale * rhs + neighbour_sum(weights, extend(field, layout))) / total
        return jnp.where(colour, fresh, field)

    def smooth(field, sweeps):
        for sweep in range(sweeps):
            for colour in (first, second):
                field = relax(field, colour)
        return field

    def remainder(field):
        return rhs - (total * field - neighbour_sum(weights, extend(field, layout))) / scale

    field = jnp.zeros(rhs.shape, jnp.float32)
    if level == LEVELS - 1:
        return (smooth(field, 12), None)
    field = smooth(field, 2)
    rhs_next = coarsen(remainder(field))
    conduct_next = coarsen(conduct)
    joined = layout == "split" and level == 1
    if joined:
        local_depth = rhs_next.shape[0]
        rhs_next, conduct_next = (
            lax.all_gather(rhs_next, "gz", axis=0, tiled=True),
            lax.all_gather(conduct_next, "gz", axis=0, tiled=True),
        )
        error, unused = cycle(
            rhs_next, conduct_next, level + 1, "column", 0, y_start // 2, z_total // 2, y_total // 2
        )
        error = lax.dynamic_slice_in_dim(error, lax.axis_index("gz") * local_depth, local_depth, 0)
    else:
        error, unused = cycle(
            rhs_next,
            conduct_next,
            level + 1,
            layout,
            z_start // 2,
            y_start // 2,
            z_total // 2,
            y_total // 2,
        )
    field = field + prolong(error)
    field = smooth(field, 2)
    return (field, remainder(field))


def natural_coarse(message):
    packed = message.reshape(2, 2, 2, 4, 2, LANES)
    parity = (jnp.arange(2)[:, None, None, None, None] + jnp.arange(4)[None, None, :, None, None]) % 2 == 0
    even = jnp.where(parity, packed[0], packed[1])
    odd = jnp.where(parity, packed[1], packed[0])
    both = jnp.stack([even, odd])
    return both.transpose(4, 1, 3, 5, 2, 0).reshape(4, 4, 4 * LANES)


def solve_coarse_spread(message, kmessage, nz, ny):
    z_start, y_start = 4 * lax.axis_index("gz"), 4 * lax.axis_index("gy")
    field, unused = cycle(
        natural_coarse(message), natural_coarse(kmessage), 1, "split", z_start, y_start, 4 * nz, 4 * ny
    )
    wide = extended(field, (("gz", 0), ("gy", 1)), 3).reshape(10, 10, LANES, 4).transpose(1, 3, 0, 2)
    error = jnp.concatenate([wide[:, :, 3:9], wide[:, :, 1:3]], axis=2)
    return error, jnp.stack([wide[3:7, :, 9], wide[3:7, :, 0]])


def exchange(first, second, axis):
    size = lax.axis_size(axis)
    results = []
    for message, start in ((first, 0), (second, 1)):
        pairs = [(i, i + 1) for i in range(start, size - 1, 2)]
        results.append(lax.ppermute(message, axis, pairs + [(j, i) for i, j in pairs]))
    return results


def on_device(right_side, coefficient):
    nz, ny = lax.axis_size("gz"), lax.axis_size("gy")
    assert right_side.shape == (8, 8, 8 * LANES)
    cells = (2, 2, 8, 2, 4, 4, LANES)
    yface, zface = (16, 2, 4, 4, LANES), (8, 4, 16, LANES)
    coarse = (8, 8, LANES)
    packed = call(pack_kernel, 3, (cells, yface, yface), [(2, 8, 64, LANES)], right_side, coefficient)
    local, ya, yb = packed
    ya, yb = exchange(ya, yb, "gy")
    za, zb, kmessage = call(zpack_kernel, 2, (zface, zface, coarse), [], local)
    za, zb = exchange(za, zb, "gz")
    coarse_cells = 8 * 8 * LANES
    whole = nz * ny * coarse_cells <= WHOLE_COARSE_CELLS and nz & (nz - 1) == 0 and ny & (ny - 1) == 0
    swaps, kswaps = swap_steps(nz, ny, 0), swap_steps(nz, ny)
    kall = kmessage[None]
    if whole:
        kall = swapped(kall, kswaps[0], nz, ny)
        ya, yb, za, zb, kall = lax.optimization_barrier((ya, yb, za, zb, kall))
    relayed, sems = (8 * CORNER_ROWS, LANES), pltpu.SemaphoreType.DMA((2,))
    corners = call(relay_kernel, 2, (relayed, relayed), [(2, *yface), sems], ya, yb, specs=[FAR] * 2)
    ca, cb = exchange(*corners, "gz")
    if whole:
        for step in kswaps[1:-3]:
            kall = swapped(kall, step, nz, ny)
        ca, cb, kall = lax.optimization_barrier((ca, cb, kall))
        kall = swapped(kall, kswaps[-3], nz, ny)
    lines, face = (LINES, 2, 4, 8, LANES), (FACE_ROWS, LANES)
    outs = ((2, *lines), (2, *lines), (2, *lines), (8, *lines[1:]), lines, (2, 8, 4, LANES))
    outs += ((FACE_ROWS + 64, LANES), face, coarse)
    scratch = [(2, *lines), lines, lines, lines, relayed, relayed, sems]
    k, g, fs, half, ub, kx, yc, yd, message = call(
        down_kernel, 6, outs, scratch, local, ya, yb, za, zb, ca, cb, specs=[VMEM] * 5 + [FAR] * 2
    )
    if whole:
        yc, kall = lax.optimization_barrier((yc, kall))
    yc, yd = exchange(yc, yd, "gy")
    if whole:
        fall = jnp.stack([message, yc[FACE_ROWS:].reshape(message.shape)])
        fall = swapped(fall, swaps[1], nz, ny)
        kall = swapped(kall, kswaps[-2], nz, ny)
        fall, yc, yd = lax.optimization_barrier((fall, yc, yd))
        for step in swaps[2:-2]:
            fall = swapped(fall, step, nz, ny)
    zface = (ZROWS, LANES)
    zc, zd = call(widen_kernel, 2, (zface, zface), [(2, *face), sems], ub, yc, yd, specs=[VMEM, FAR, FAR])
    if whole:
        fall, zc, zd = lax.optimization_barrier((fall, zc, zd))
    zc, zd = exchange(zc, zd, "gz")
    if whole:
        fall = swapped(fall, swaps[-2], nz, ny)
        ktheirs = swap(kall, kswaps[-1], nz, ny)
        fall, kall, ktheirs, zc, zd = lax.optimization_barrier((fall, kall, ktheirs, zc, zd))
        ftheirs = swap(fall, swaps[-1], nz, ny)
        error, errorx = solve_coarse(fall, ftheirs, kall, ktheirs, nz, ny)
    else:
        error, errorx = solve_coarse_spread(message, kmessage, nz, ny)
    block = (8, 8, 8 * LANES)
    scratch = [lines] * 4 + [(2, 8, 4, LANES)] * 2 + [(2, 8, 64, LANES)]
    return call(up_kernel, 6, (block, block), scratch, k, g, fs, half, ub, kx, yc, yd, zc, zd, error, errorx)


def solution(mesh):
    spec = P("gz", "gy", None)
    return jax.shard_map(
        on_device, mesh=mesh, in_specs=(spec, spec), out_specs=(spec, spec), check_vma=False
    )
```

```python
import jax
import jax.numpy as jnp
from jax import lax
from jax.experimental import pallas as pl
from jax.experimental.pallas import tpu as pltpu
from jax.sharding import PartitionSpec as P

LANES = 128
LINES = 18
LEVELS = 4
PAD = 5
F32 = jnp.float32
VMEM = pl.BlockSpec(memory_space=pltpu.VMEM)
FAR = pl.BlockSpec(memory_space=pl.ANY)
WHOLE_COARSE_CELLS = 1 << 19


def call(body, micros, outs, scratch, *args, specs=None):
    return pl.pallas_call(
        body,
        out_shape=[jax.ShapeDtypeStruct(s, F32) for s in outs],
        in_specs=specs or [VMEM] * len(args),
        out_specs=[VMEM] * len(outs),
        scratch_shapes=[pltpu.VMEM(s, F32) if isinstance(s, tuple) else s for s in scratch],
        cost_estimate=pl.CostEstimate(flops=0, transcendentals=0, bytes_accessed=micros * 3_000_000),
        compiler_params=pltpu.CompilerParams(vmem_limit_bytes=18 << 20),
    )(*args)


def iota(axis, rows=8):
    return lax.broadcasted_iota(jnp.int32, (rows, LANES), axis)


def barrel(arrays, block):
    for bit in (1, 2, 4):
        high = (block & bit) != 0
        arrays = [jnp.where(high, arrays[(j + bit) % 8], arrays[j]) for j in range(8)]
    return arrays


def lane_gather(array, index):
    return jnp.take_along_axis(array, index, axis=1, mode="promise_in_bounds")


def split_lanes(tiles):
    lane = iota(1)
    block = lane // 16
    parts = [lane_gather(tiles[t], 8 * (lane % 16) + (block - t) % 8) for t in range(8)]
    mixed = barrel(parts, block)
    return [pltpu.roll(mixed[-s % 8], (-16 * s) % LANES, axis=1) for s in range(8)]


def join_lanes(arrays):
    lane = iota(1)
    block = lane // 16
    moved = [pltpu.roll(arrays[s], (16 * s) % LANES, axis=1) for s in range(8)]
    mixed = barrel(moved, block)
    return [lane_gather(mixed[-t % 8], 16 * ((lane % 8 + t) % 8) + lane // 8) for t in range(8)]


def put_coarse(message, row, s, value, tail=None):
    for z in range(4):
        e, c = z % 2, (s + z + row) % 2
        m, at = (c * 2 + e) * 2 + s // 2, 2 * row + z // 2
        message[m, at, :] = value[z]
        if tail is not None:
            tail[FACE_ROWS + 8 * m + at, :] = value[z]


REACH = ((0, 0, 4), (0, 1, 3), (1, 0, 4), (1, 1, 5))
YFACE = [(a, c, y, n) for a, c, n in REACH for y in range(n)]
ZFACE = sorted(((a, c, d) for a, c, n in REACH for d in range(1, n + 1)), key=lambda r: r[2] - REACH[2 * r[0] + r[1]][2])
CORNER = {1: (12, 0, 12), 2: (8, 16, 8), 3: (4, 12, 4), 4: (1, 24, 4)}
CORNER_ROWS = 28
FACE_ROWS = 5 * 2 * 4 * 4
DEPTHS = [min(i, 5, LINES - 1 - i) for i in range(LINES)]
ZSTARTS = [4 * sum(DEPTHS[:i]) for i in range(LINES)]
ZROWS = 4 * sum(DEPTHS)


def own_sides():
    return [lax.rem(lax.axis_index(axis), 2) == 0 for axis in ("gz", "gy")]


def halo_cell(side, distance):
    z = 7 + distance if side == 0 else -distance
    return z % 2, (z // 2) % 8


def pick(flag, a, b):
    return jnp.where(flag, a, b), jnp.where(flag, b, a)


def pack_kernel(f_ref, k_ref, local, ya, yb, natural):
    _, yup = own_sides()
    for a, ref in enumerate((f_ref, k_ref)):
        for z in range(8):
            arrays = split_lanes([ref[z, :, t * LANES : (t + 1) * LANES] for t in range(8)])
            for s in range(8):
                natural[a, s, 8 * z : 8 * z + 8, :] = arrays[s]
    for a in range(2):
        for c in range(2):
            for y in range(8):
                for e in range(2):
                    q = (e + y + c) % 2
                    for s in range(4):
                        local[a, c, y, e, s] = natural[a, 2 * s + q, pl.ds(y + 8 * e, 4, stride=16), :]
    for i, (a, c, y, n) in enumerate(YFACE):
        first, second = pick(yup, y + 8 - n, y)
        ya[i] = local[a, c, first]
        yb[i] = local[a, c, second]


def zpack_kernel(local, za, zb, coarse):
    zup, _ = own_sides()

    def faces(y, carry):
        for i, (a, c, d) in enumerate(ZFACE):
            high, low = 8 - d, d - 1
            for s in range(4):
                up = local[a, c, y, high % 2, s, high // 2 : high // 2 + 1]
                down = local[a, c, y, low % 2, s, low // 2 : low // 2 + 1]
                za[y, s, i : i + 1], zb[y, s, i : i + 1] = pick(zup, up, down)
        return carry

    lax.fori_loop(0, 8, faces, 0)
    for row in range(4):
        for s in range(4):
            total = None
            for c in range(2):
                for y in (2 * row, 2 * row + 1):
                    pair = local[1, c, y, 0, s] + local[1, c, y, 1, s]
                    total = pair if total is None else total + pair
            put_coarse(coarse, row, s, total * 0.125)


def relay_kernel(ya_far, yb_far, ca, cb, faces, sem):
    zup, yabove = own_sides()
    slots = pick(yabove, 0, 1)
    copies = [pltpu.make_async_copy(f, faces.at[t], sem.at[i]) for i, (f, t) in enumerate(zip((ya_far, yb_far), slots))]
    for copy in copies:
        copy.start()
    for copy in copies:
        copy.wait()
    for target, up in ((ca, zup), (cb, jnp.logical_not(zup))):
        places = {d: jnp.where(up, 8 - d, d - 1) for d in range(1, 5)}
        for d, (count, at, _) in CORNER.items():
            for i, (a, c, dz) in enumerate(ZFACE[:count]):
                e, t = lax.rem(places[dz], 2), places[dz] // 2
                for side in range(2):
                    y = d - 1 if side == 0 else REACH[2 * a + c][2] - d
                    line = YFACE.index((a, c, y, REACH[2 * a + c][2]))
                    for s in range(4):
                        base = (4 * side + s) * CORNER_ROWS + at + i
                        target[base : base + 1, :] = faces[side, line, e, s, pl.ds(t, 1)]


def neighbours(ref, line, e, s, q, groups, edge=None, first=None, last=None):
    rows = ref.shape[-2]
    lane = iota(1, rows)
    same = ref[line, e, s]
    if q == 0 and s == 0:
        other = jnp.where(lane == 0, 0.0, pltpu.roll(ref[line, e, groups - 1], 1, axis=1))
    elif q == 1 and s == groups - 1:
        other = jnp.where(lane == LANES - 1, 0.0, pltpu.roll(ref[line, e, 0], LANES - 1, axis=1))
    else:
        other = ref[line, e, s + (1 if q else -1)]
    zsame = ref[line, 1 - e, s]
    zother = pltpu.roll(zsame, 1 if e == 0 else rows - 1, axis=0)
    if edge is not None:
        zother = edge(zother, line, e, s)
    return (same + other) + (zsame + zother) + (ref[line - 1, e, s] + ref[line + 1, e, s])


def closed(zother, line, e, s):
    rows = zother.shape[0]
    return jnp.where(iota(0, rows) == (0 if e == 0 else rows - 1), 0.0, zother)


def over_lines(low, high, offset, visit, lines=4):
    steps, rest = divmod(high - low + 1, lines)

    def step(i, carry):
        for j in range(lines):
            visit(low + offset + j + lines * i, (low + j) % 2)
        return carry

    lax.fori_loop(0, steps, step, 0)
    for y in range(high + 1 - rest, high + 1):
        visit(y + offset, y % 2)


def diagonal(k, kother, line, e, s, q, groups, edge=None):
    centre = k[line, e, s]
    return centre, 6.0 * centre + neighbours(kother, line, e, s, q, groups, edge)


def down_kernel(
    local, ya, yb, za, zb, ca_far, cb_far,
    k, g, fs, half, ub, kx, yc, yd, coarse,
    f, ur, vr, vb, ca, cb, sem,
):
    zabove, yabove = own_sides()
    yup = yabove
    copies = [pltpu.make_async_copy(*pair, sem.at[i]) for i, pair in enumerate(((ca_far, ca), (cb_far, cb)))]
    for copy in copies:
        copy.start()
    blank = jnp.zeros((8, LANES), F32)
    for c in range(2):
        for line in (*range(PAD), *range(PAD + 8, LINES)):
            for e in range(2):
                for s in range(4):
                    k[c, line, e, s] = blank
                    f[c, line, e, s] = blank
    both = (f, k)

    def assemble(y, carry):
        for e in range(2):
            for s in range(4):
                f[1, PAD + y, e, s] = blank
                for a in range(2):
                    for c in range(2):
                        both[a][c, PAD + y, e, s, 0:4] = local[a, c, y, e, s]
        for s in range(4):
            for side, part in enumerate(pick(zabove, za[y, s], zb[y, s])):
                for i, (a, c, d) in enumerate(ZFACE):
                    e, row = halo_cell(side, d)
                    if d == 5:
                        kx[side, y, s : s + 1] = part[i : i + 1]
                    else:
                        both[a][c, PAD + y, e, s, row : row + 1] = part[i : i + 1]
        return carry

    lax.fori_loop(0, 8, assemble, 0)
    for i, (a, c, y, n) in enumerate(YFACE):
        first, second = pick(yabove, PAD + y + 8, PAD + y - n)
        for e in range(2):
            for s in range(4):
                both[a][c, first, e, s, 0:4] = ya[i, e, s]
                both[a][c, second, e, s, 0:4] = yb[i, e, s]
    for copy in copies:
        copy.wait()
    for yside in range(2):
        for s in range(4):
            for d, (count, at, _) in CORNER.items():
                line, base = PAD + 7 + d if yside == 0 else PAD - d, (4 * yside + s) * CORNER_ROWS + at
                for side, part in enumerate(pick(zabove, ca[base : base + count, :], cb[base : base + count, :])):
                    for i, (a, c, dz) in enumerate(ZFACE[:count]):
                        e, row = halo_cell(side, dz)
                        both[a][c, line, e, s, row : row + 1] = part[i : i + 1]

    rows = iota(0)

    def far(zother, line, e, s):
        beyond = kx[1 - e, line - PAD, s : s + 1]
        return jnp.where(rows == (6 if e == 0 else 5), jnp.broadcast_to(beyond, (8, LANES)), zother)

    def prepare(c, line, parity, edge, keep):
        for e in range(2):
            q = (e + parity + c) % 2
            for s in range(4):
                centre, total = diagonal(k.at[c], k.at[1 - c], line, e, s, q, 4, edge)
                inside = centre != 0.0
                scale = jnp.where(inside, 1.0 / jnp.where(inside, total, 1.0), 0.0)
                start = 2.0 * f[c, line, e, s] * scale
                g[c, line, e, s] = scale
                fs[c, line, e, s] = start
                if keep:
                    half[line - PAD, e, s] = 0.5 * total
                if c == 0:
                    ur[line, e, s] = start
                    vr[line, e, s] = centre * start

    over_lines(-4, -1, PAD, lambda line, parity: prepare(0, line, parity, None, False))
    over_lines(8, 11, PAD, lambda line, parity: prepare(0, line, parity, None, False))
    over_lines(0, 7, PAD, lambda line, parity: prepare(0, line, parity, far, True))
    over_lines(-3, 10, PAD, lambda line, parity: prepare(1, line, parity, None, False))

    def relax(c, low, high):
        sweep(c, low, high, k, g, fs, (ur, ub), (vr, vb))

    relax(1, -3, 10)
    relax(0, -2, 9)
    relax(1, -1, 8)

    for row in range(4):
        for s in range(4):
            total = None
            for y in (2 * row, 2 * row + 1):
                for e in range(2):
                    line = PAD + y
                    value = red_residual(line, y % 2, e, s, k, g, fs, half, ur, ub, vb)
                    total = value if total is None else total + value
            put_coarse(coarse, row, s, total * 0.125, yc)

    first, second = pick(yup, PAD + 3, PAD)
    for i in range(5):
        for e in range(2):
            for s in range(4):
                at = ((i * 2 + e) * 4 + s) * 4
                yc[at : at + 4, :] = ub[first + i, e, s, 0:4]
                yd[at : at + 4, :] = ub[second + i, e, s, 0:4]


def widen_kernel(ub, yc_far, yd_far, zc, zd, faces, sem):
    zup, yabove = own_sides()
    slots, face = pick(yabove, 0, 1), pl.ds(0, FACE_ROWS)
    copies = [
        pltpu.make_async_copy(f.at[face], faces.at[t], sem.at[i]) for i, (f, t) in enumerate(zip((yc_far, yd_far), slots))
    ]
    for copy in copies:
        copy.start()

    def put(line, fetch):
        for target, up in ((zc, zup), (zd, jnp.logical_not(zup))):
            for d in range(1, DEPTHS[line] + 1):
                z = jnp.where(up, 8 - d, d - 1)
                for s in range(4):
                    at = ZSTARTS[line] + s * DEPTHS[line] + d - 1
                    target[at : at + 1, :] = fetch(lax.rem(z, 2), s, z // 2)

    for line in range(PAD, PAD + 8):
        put(line, lambda e, s, t: ub[line, e, s, pl.ds(t, 1)])
    for copy in copies:
        copy.wait()
    for i in range(5):
        for side, line in enumerate((PAD + 8 + i, i)):
            put(line, lambda e, s, t: faces[side, pl.ds(((i * 2 + e) * 4 + s) * 4 + t, 1), :])


def sweep(c, low, high, k, g, fs, u, v, edges=(None, None)):
    def visit(line, parity):
        for e in range(2):
            q = (e + parity + c) % 2
            for s in range(4):
                near = neighbours(u[1 - c], line, e, s, q, 4, edges[0])
                flow = neighbours(v[1 - c], line, e, s, q, 4, edges[1])
                centre = k[c, line, e, s]
                value = fs[c, line, e, s] + g[c, line, e, s] * (centre * near + flow)
                u[c][line, e, s] = value
                v[c][line, e, s] = centre * value

    over_lines(low, high, PAD, visit)


def red_residual(line, parity, e, s, k, g, fs, half, ur, ub, vb):
    q = (e + parity) % 2
    near = neighbours(ub, line, e, s, q, 4)
    flow = neighbours(vb, line, e, s, q, 4)
    fresh = fs[0, line, e, s] + g[0, line, e, s] * (k[0, line, e, s] * near + flow)
    return half[line - PAD, e, s] * (fresh - ur[line, e, s])


def up_kernel(
    k, g, fs, half, old, kx, yc, yd, zc, zd, error, errorx,
    correction, residual,
    ub, ur, vb, vr, ux, vx, natural,
):
    zabove, yabove = own_sides()
    for y in range(8):
        for e in range(2):
            for s in range(4):
                ub[PAD + y, e, s, 0:4] = old[PAD + y, e, s, 0:4]
    first, second = pick(yabove, PAD + 8, 0)
    for i in range(5):
        for e in range(2):
            for s in range(4):
                at = ((i * 2 + e) * 4 + s) * 4
                ub[first + i, e, s, 0:4] = yc[at : at + 4, :]
                ub[second + i, e, s, 0:4] = yd[at : at + 4, :]
    quiet = jnp.zeros((4, LANES), F32)
    for line, depth in enumerate(DEPTHS):
        for s in range(4):
            if depth < 4:
                for e in range(2):
                    ub[line, e, s, 4:8] = quiet
            if not depth:
                continue
            at = ZSTARTS[line] + s * depth
            for side, part in enumerate(pick(zabove, zc[at : at + depth, :], zd[at : at + depth, :])):
                for d in range(1, min(depth, 4) + 1):
                    e, row = halo_cell(side, d)
                    ub[line, e, s, row : row + 1] = part[d - 1 : d]
                if depth == 5:
                    y = line - PAD
                    beyond = kx[side, y, s : s + 1]
                    value = part[4:5] + errorx[side, y // 2, s : s + 1]
                    value = jnp.where(beyond != 0.0, value, 0.0)
                    ux[side, y, s : s + 1] = value
                    vx[side, y, s : s + 1] = beyond * value

    def add(line, parity):
        for e in range(2):
            for s in range(4):
                centre = k[1, line, e, s]
                value = ub[line, e, s] + error[(line + 1) // 2, s]
                value = jnp.where(centre != 0.0, value, 0.0)
                ub[line, e, s] = value
                vb[line, e, s] = centre * value

    over_lines(-5, 12, PAD, add)

    rows = iota(0)

    def far(ref):
        def edge(zother, line, e, s):
            beyond = ref[1 - e, line - PAD, s : s + 1]
            return jnp.where(rows == (6 if e == 0 else 5), jnp.broadcast_to(beyond, (8, LANES)), zother)

        return edge

    u, v = (ur, ub), (vr, vb)
    sweep(0, -4, -1, k, g, fs, u, v)
    sweep(0, 8, 11, k, g, fs, u, v)
    sweep(0, 0, 7, k, g, fs, u, v, (far(ux), far(vx)))
    sweep(1, -3, 10, k, g, fs, u, v)
    sweep(0, -2, 9, k, g, fs, u, v)
    sweep(1, -1, 8, k, g, fs, u, v)

    quiet = jnp.zeros((4, LANES), F32)
    for y in range(8):
        for e in range(2):
            at = pl.ds(y + 8 * e, 4, stride=16)
            q = (e + y) % 2
            for s in range(4):
                value = red_residual(PAD + y, y % 2, e, s, k, g, fs, half, ur, ub, vb)
                natural[1, 2 * s + q, at, :] = value[0:4]
                natural[1, 2 * s + 1 - q, at, :] = quiet
                natural[0, 2 * s + q, at, :] = ur[PAD + y, e, s, 0:4]
                natural[0, 2 * s + 1 - q, at, :] = ub[PAD + y, e, s, 0:4]
    for a, out in enumerate((correction, residual)):
        for z in range(8):
            tiles = join_lanes([natural[a, s, 8 * z : 8 * z + 8, :] for s in range(8)])
            for t in range(8):
                out[z, :, t * LANES : (t + 1) * LANES] = tiles[t]


def shifted(value, step, axis):
    size = value.shape[axis]
    where = iota(axis, value.shape[0])
    moved = pltpu.roll(value, -step % size, axis=axis)
    return jnp.where((where >= size - step) if step > 0 else (where < -step), 0.0, moved)


def coarse_kernel(nz, ny):
    height, depth = 4 * ny, 2 * nz
    height2, height3 = height // 2, height // 4

    def body(
        fmine, ftheirs_far, kmine, ktheirs, error, errorx,
        f, k, g, fs, half, ur, ub, vr, vb, f2, k2, fc, kc, gc, sc, uc, vc, hc, w3, f3, ftheirs, sem,
    ):
        u, v = (ur, ub), (vr, vb)
        zplace, yplace = lax.axis_index("gz"), lax.axis_index("gy")

        def slot(i, j, swaps):
            apart = (zplace * ny + yplace) ^ (i * ny + j)
            return sum(((apart >> step) & 1) << bit for bit, step in enumerate(swaps[:-1]))

        def spread(odd, sources, target, swaps):
            def visit(j, carry):
                order = [slot(i, j, swaps) for i in range(nz)]
                for m in range(8):
                    pieces = [sources[(i + odd) % 2][order[i], m] for i in range(nz)]
                    for row in range(4):
                        whole = jnp.concatenate([p[2 * row : 2 * row + 2] for p in pieces], axis=0)
                        target[m // 4, 1 + 4 * j + row, m // 2 % 2, m % 2] = whole
                return carry

            lax.fori_loop(0, ny, visit, 0)

        def spread_either(*args):
            for odd in range(2):
                pl.when(lax.rem(zplace, 2) == odd)(lambda odd=odd: spread(odd, *args))

        copy = pltpu.make_async_copy(ftheirs_far, ftheirs, sem)
        copy.start()
        spread_either((kmine, ktheirs), k, swap_steps(nz, ny))
        copy.wait()
        spread_either((fmine, ftheirs), f, swap_steps(nz, ny, 0))
        blank = jnp.zeros((depth, LANES), F32)
        for line in (0, height + 1):
            for e in range(2):
                for s in range(2):
                    for c in range(2):
                        k[c, line, e, s] = blank
                        u[c][line, e, s] = blank
                        v[c][line, e, s] = blank

        def prepare(c):
            def visit(line, parity):
                for e in range(2):
                    for s in range(2):
                        centre, total = diagonal(k.at[c], k.at[1 - c], line, e, s, (e + parity + c) % 2, 2, closed)
                        scale = 1.0 / total
                        start = 8.0 * f[c, line, e, s] * scale
                        g[c, line, e, s] = scale
                        fs[c, line, e, s] = start
                        if c == 0:
                            half[line, e, s] = 0.125 * total
                            ur[line, e, s] = start
                            vr[line, e, s] = centre * start

            over_lines(0, height - 1, 1, visit, 8)

        def fresh(c, line, parity, e, s):
            q = (e + parity + c) % 2
            near = neighbours(u[1 - c], line, e, s, q, 2, closed)
            flow = neighbours(v[1 - c], line, e, s, q, 2, closed)
            return fs[c, line, e, s] + g[c, line, e, s] * (k[c, line, e, s] * near + flow)

        def relax(c):
            def visit(line, parity):
                for e in range(2):
                    for s in range(2):
                        value = fresh(c, line, parity, e, s)
                        u[c][line, e, s] = value
                        v[c][line, e, s] = k[c, line, e, s] * value

            over_lines(0, height - 1, 1, visit, 8)

        prepare(0)
        prepare(1)
        relax(1)
        relax(0)
        relax(1)

        def restrict(i, carry):
            for s in range(2):
                value, conduct = None, None
                for j in range(2):
                    line = 1 + 2 * i + j
                    for e in range(2):
                        part = half[line, e, s] * (fresh(0, line, j, e, s) - ur[line, e, s])
                        value = part if value is None else value + part
                        part = k[0, line, e, s] + k[1, line, e, s]
                        conduct = part if conduct is None else conduct + part
                f2[s, i] = value * 0.125
                k2[s, i] = conduct * 0.125
            return carry

        lax.fori_loop(0, height2, restrict, 0)

        even = iota(0, depth) % 2 == 0

        def q_is_zero(c, y):
            return even if (y + c) % 2 == 0 else jnp.logical_not(even)

        def coloured(pair, c, y):
            return jnp.where(q_is_zero(c, y), pair[0], pair[1])

        def around(ref, c, y):
            mid = ref[1 + y]
            other = jnp.where(q_is_zero(c, y), shifted(mid, -1, 1), shifted(mid, 1, 1))
            return (mid + other) + (shifted(mid, -1, 0) + shifted(mid, 1, 0)) + (ref[y] + ref[y + 2])

        for c in range(2):
            for line in (0, height2 + 1):
                kc[c, line] = blank
                uc[c, line] = blank
                vc[c, line] = blank
            for y in range(height2):
                kc[c, 1 + y] = coloured((k2[0, y], k2[1, y]), c, y)
                fc[c, y] = coloured((f2[0, y], f2[1, y]), c, y)
        for c in range(2):
            for y in range(height2):
                centre = kc[c, 1 + y]
                total = 6.0 * centre + around(kc.at[1 - c], c, y)
                scale = 1.0 / total
                start = 32.0 * fc[c, y] * scale
                gc[c, y] = scale
                sc[c, y] = start
                if c == 0:
                    hc[y] = total * (0.5 / 16.0)
                    uc[0, 1 + y] = start
                    vc[0, 1 + y] = centre * start

        def fresh2(c, y):
            flow = kc[c, 1 + y] * around(uc.at[1 - c], c, y) + around(vc.at[1 - c], c, y)
            return sc[c, y] + gc[c, y] * flow

        def relax2(c):
            for y in range(height2):
                value = fresh2(c, y)
                uc[c, 1 + y] = value
                vc[c, 1 + y] = kc[c, 1 + y] * value

        relax2(1)
        relax2(0)
        relax2(1)

        def paired(a, b):
            total = (a + b) * 0.125
            return jnp.where(even, total + pltpu.roll(total, depth - 1, axis=0), 0.0)

        conduct = []
        right = []
        for y in range(height3):
            parts = [hc[2 * y + j] * (fresh2(0, 2 * y + j) - uc[0, 1 + 2 * y + j]) for j in range(2)]
            right.append(paired(*parts))
            parts = [kc[0, 1 + 2 * y + j] + kc[1, 1 + 2 * y + j] for j in range(2)]
            conduct.append(paired(*parts))
        moves = ((-2, 0), (2, 0), (-1, 1), (1, 1))
        for y in range(height3):
            centre = conduct[y]
            beside = [shifted(centre, step, axis) for step, axis in moves]
            beside.append(conduct[y - 1] if y else jnp.zeros_like(centre))
            beside.append(conduct[y + 1] if y + 1 < height3 else jnp.zeros_like(centre))
            total = 6.0 * centre
            for part in beside:
                total = total + part
            scale = jnp.where(even, 1.0 / jnp.where(even, total, 1.0), 0.0)
            f3[y] = 128.0 * right[y] * scale
            lane, row = iota(1, depth), iota(0, depth)
            open_faces = (row >= 2, row < depth - 2, lane >= 1, lane < LANES - 1)
            for i in range(6):
                weight = (centre + beside[i]) * scale
                w3[y, i] = jnp.where(open_faces[i], weight, 0.0) if i < 4 else weight
        mixed = (iota(0, depth) // 2 + iota(1, depth)) % 2

        def relax3(c, field):
            result = []
            for y in range(height3):
                mid = field[y]
                value = f3[y]
                for i, (step, axis) in enumerate(moves):
                    value = value + w3[y, i] * pltpu.roll(mid, -step % mid.shape[axis], axis=axis)
                if y:
                    value = value + w3[y, 4] * field[y - 1]
                if y + 1 < height3:
                    value = value + w3[y, 5] * field[y + 1]
                result.append(jnp.where(mixed == (y + c) % 2, value, mid))
            return result

        def two_colours(_, field):
            return tuple(relax3(1, relax3(0, list(field))))

        field = lax.fori_loop(0, 12, two_colours, (blank,) * height3)

        for y in range(height2):
            coarse = field[y // 2]
            value = uc[1, 1 + y] + (coarse + pltpu.roll(coarse, 1, axis=0))
            uc[1, 1 + y] = value
            vc[1, 1 + y] = kc[1, 1 + y] * value
        for c in (0, 1, 0, 1):
            relax2(c)

        for y in range(height2):
            zero = q_is_zero(0, y)
            red, black = uc[0, 1 + y], uc[1, 1 + y]
            f2[0, y] = jnp.where(zero, red, black)
            f2[1, y] = jnp.where(zero, black, red)

        def add(line, parity):
            for e in range(2):
                for s in range(2):
                    value = ub[line, e, s] + f2[s, (line - 1) // 2]
                    ub[line, e, s] = value
                    vb[line, e, s] = k[1, line, e, s] * value

        over_lines(0, height - 1, 1, add, 8)
        for c in (0, 1, 0, 1):
            relax(c)

        for j in range(-3, 7):
            line = 1 + jnp.clip(4 * yplace + j, 0, height - 1)
            for t in range(-3, 7):
                e = t % 2
                at = pl.ds(jnp.clip(2 * zplace + t // 2, 0, depth - 1), 1)
                for s in range(4):
                    row = u[(s + e + j) % 2][line, e, s // 2, at, :]
                    if -2 <= t <= 5:
                        error[j + 3, s, t % 8 : t % 8 + 1, :] = row
                    elif 0 <= j < 8 // 2:
                        errorx[1 if t < 0 else 0, j, s : s + 1, :] = row

    lines, lines2 = (height + 2, 2, 2, depth, LANES), (height2 + 2, depth, LANES)
    flat2 = (2, height2, depth, LANES)
    scratch = [(2, *lines)] * 4 + [lines] * 5 + [flat2, flat2, flat2, (2, *lines2), flat2, flat2]
    scratch += [(2, *lines2), (2, *lines2), flat2[1:], (height3, 6, depth, LANES), (height3, depth, LANES)]
    scratch += [(nz * ny // 2, 8, 8, LANES), pltpu.SemaphoreType.DMA(())]
    return body, scratch


def swap_steps(nz, ny, first=None):
    ybits, zbits = ny.bit_length() - 1, nz.bit_length() - 1
    along_y = list(range(ybits - 1, -1, -1))
    if first is not None:
        along_y = [first, *(bit for bit in along_y if bit != first)]
    return [*along_y, *range(ybits + zbits - 1, ybits - 1, -1)]


def swap(block, step, nz, ny):
    return lax.ppermute(block, ("gz", "gy"), [(i, i ^ (1 << step)) for i in range(nz * ny)])


def swapped(block, step, nz, ny):
    return jnp.concatenate([block, swap(block, step, nz, ny)])


def solve_coarse(fmine, ftheirs, kmine, ktheirs, nz, ny):
    body, scratch = coarse_kernel(nz, ny)
    outs = ((10, 4, 8, LANES), (2, 4, 4, LANES))
    return call(body, 11, outs, scratch, fmine, ftheirs, kmine, ktheirs, specs=[VMEM, FAR, VMEM, VMEM])


def extended(array, sides, width):
    for axis, dim in sides:
        size, length = (lax.axis_size(axis), array.shape[dim])
        up = [(i, (i + 1) % size) for i in range(size - 1)]
        down = [(j, i) for i, j in up]
        last = lax.slice_in_dim(array, length - width, length, axis=dim)
        initial = lax.slice_in_dim(array, 0, width, axis=dim)
        before = lax.ppermute(last, axis, up)
        after = lax.ppermute(initial, axis, down)
        array = jnp.concatenate([before, array, after], axis=dim)
    return array


def coarsen(field):
    total = field[0::2, 0::2, 0::2] + field[0::2, 0::2, 1::2]
    total = total + field[0::2, 1::2, 0::2] + field[0::2, 1::2, 1::2]
    total = total + field[1::2, 0::2, 0::2] + field[1::2, 0::2, 1::2]
    total = total + field[1::2, 1::2, 0::2] + field[1::2, 1::2, 1::2]
    return total * 0.125


def prolong(field):
    return jnp.repeat(jnp.repeat(jnp.repeat(field, 2, axis=0), 2, axis=1), 2, axis=2)


def face_terms(kpad):
    center = kpad[1:-1, 1:-1, 1:-1]
    z_minus = 0.5 * (center + kpad[:-2, 1:-1, 1:-1])
    z_plus = 0.5 * (center + kpad[2:, 1:-1, 1:-1])
    y_minus = 0.5 * (center + kpad[1:-1, :-2, 1:-1])
    y_plus = 0.5 * (center + kpad[1:-1, 2:, 1:-1])
    x_minus = 0.5 * (center + kpad[1:-1, 1:-1, :-2])
    x_plus = 0.5 * (center + kpad[1:-1, 1:-1, 2:])
    total = z_minus + z_plus + y_minus + y_plus + x_minus + x_plus
    return ((z_minus, z_plus, y_minus, y_plus, x_minus, x_plus), total)


def neighbour_sum(weights, upad):
    z_minus, z_plus, y_minus, y_plus, x_minus, x_plus = weights
    acc = z_minus * upad[:-2, 1:-1, 1:-1] + z_plus * upad[2:, 1:-1, 1:-1]
    acc = acc + y_minus * upad[1:-1, :-2, 1:-1] + y_plus * upad[1:-1, 2:, 1:-1]
    acc = acc + x_minus * upad[1:-1, 1:-1, :-2] + x_plus * upad[1:-1, 1:-1, 2:]
    return acc


def extend(field, layout):
    if layout == "column":
        wider = extended(field, (("gy", 1),), 1)
        wider = jnp.pad(wider, ((1, 1), (0, 0), (0, 0)))
    else:
        wider = extended(field, (("gz", 0), ("gy", 1)), 1)
    return jnp.pad(wider, ((0, 0), (0, 0), (1, 1)))


def region_masks(shape, z_start, y_start):
    zpos = lax.broadcasted_iota(jnp.int32, shape, 0) + z_start
    ypos = lax.broadcasted_iota(jnp.int32, shape, 1) + y_start
    xpos = lax.broadcasted_iota(jnp.int32, shape, 2)
    return (zpos + ypos + xpos + 4) % 2


def cycle(rhs, conduct, level, layout, z_start, y_start, z_total, y_total):
    scale = 4.0**level
    weights, total = face_terms(extend(conduct, layout))
    parity = region_masks(rhs.shape, z_start, y_start)
    first = parity == 0
    second = parity == 1

    def relax(field, colour):
        fresh = (scale * rhs + neighbour_sum(weights, extend(field, layout))) / total
        return jnp.where(colour, fresh, field)

    def smooth(field, sweeps):
        for sweep in range(sweeps):
            for colour in (first, second):
                field = relax(field, colour)
        return field

    def remainder(field):
        return rhs - (total * field - neighbour_sum(weights, extend(field, layout))) / scale

    field = jnp.zeros(rhs.shape, jnp.float32)
    if level == LEVELS - 1:
        return (smooth(field, 12), None)
    field = smooth(field, 2)
    rhs_next = coarsen(remainder(field))
    conduct_next = coarsen(conduct)
    joined = layout == "split" and level == 1
    if joined:
        local_depth = rhs_next.shape[0]
        rhs_next, conduct_next = (
            lax.all_gather(rhs_next, "gz", axis=0, tiled=True),
            lax.all_gather(conduct_next, "gz", axis=0, tiled=True),
        )
        error, unused = cycle(
            rhs_next, conduct_next, level + 1, "column", 0, y_start // 2, z_total // 2, y_total // 2
        )
        error = lax.dynamic_slice_in_dim(error, lax.axis_index("gz") * local_depth, local_depth, 0)
    else:
        error, unused = cycle(
            rhs_next,
            conduct_next,
            level + 1,
            layout,
            z_start // 2,
            y_start // 2,
            z_total // 2,
            y_total // 2,
        )
    field = field + prolong(error)
    field = smooth(field, 2)
    return (field, remainder(field))


def natural_coarse(message):
    packed = message.reshape(2, 2, 2, 4, 2, LANES)
    parity = (jnp.arange(2)[:, None, None, None, None] + jnp.arange(4)[None, None, :, None, None]) % 2 == 0
    even = jnp.where(parity, packed[0], packed[1])
    odd = jnp.where(parity, packed[1], packed[0])
    both = jnp.stack([even, odd])
    return both.transpose(4, 1, 3, 5, 2, 0).reshape(4, 4, 4 * LANES)


def solve_coarse_spread(message, kmessage, nz, ny):
    z_start, y_start = 4 * lax.axis_index("gz"), 4 * lax.axis_index("gy")
    field, unused = cycle(
        natural_coarse(message), natural_coarse(kmessage), 1, "split", z_start, y_start, 4 * nz, 4 * ny
    )
    wide = extended(field, (("gz", 0), ("gy", 1)), 3).reshape(10, 10, LANES, 4).transpose(1, 3, 0, 2)
    error = jnp.concatenate([wide[:, :, 3:9], wide[:, :, 1:3]], axis=2)
    return error, jnp.stack([wide[3:7, :, 9], wide[3:7, :, 0]])


def exchange(first, second, axis):
    size = lax.axis_size(axis)
    results = []
    for message, start in ((first, 0), (second, 1)):
        pairs = [(i, i + 1) for i in range(start, size - 1, 2)]
        results.append(lax.ppermute(message, axis, pairs + [(j, i) for i, j in pairs]))
    return results


def on_device(right_side, coefficient):
    nz, ny = lax.axis_size("gz"), lax.axis_size("gy")
    assert right_side.shape == (8, 8, 8 * LANES)
    cells = (2, 2, 8, 2, 4, 4, LANES)
    yface, zface = (16, 2, 4, 4, LANES), (8, 4, 16, LANES)
    coarse = (8, 8, LANES)
    packed = call(pack_kernel, 3, (cells, yface, yface), [(2, 8, 64, LANES)], right_side, coefficient)
    local, ya, yb = packed
    ya, yb = exchange(ya, yb, "gy")
    za, zb, kmessage = call(zpack_kernel, 2, (zface, zface, coarse), [], local)
    za, zb = exchange(za, zb, "gz")
    coarse_cells = 8 * 8 * LANES
    whole = nz * ny * coarse_cells <= WHOLE_COARSE_CELLS and nz & (nz - 1) == 0 and ny & (ny - 1) == 0
    swaps, kswaps = swap_steps(nz, ny, 0), swap_steps(nz, ny)
    kall = kmessage[None]
    if whole:
        kall = swapped(kall, kswaps[0], nz, ny)
        ya, yb, za, zb, kall = lax.optimization_barrier((ya, yb, za, zb, kall))
    relayed, sems = (8 * CORNER_ROWS, LANES), pltpu.SemaphoreType.DMA((2,))
    corners = call(relay_kernel, 2, (relayed, relayed), [(2, *yface), sems], ya, yb, specs=[FAR] * 2)
    ca, cb = exchange(*corners, "gz")
    if whole:
        for step in kswaps[1:-3]:
            kall = swapped(kall, step, nz, ny)
        ca, cb, kall = lax.optimization_barrier((ca, cb, kall))
        kall = swapped(kall, kswaps[-3], nz, ny)
    lines, face = (LINES, 2, 4, 8, LANES), (FACE_ROWS, LANES)
    outs = ((2, *lines), (2, *lines), (2, *lines), (8, *lines[1:]), lines, (2, 8, 4, LANES))
    outs += ((FACE_ROWS + 64, LANES), face, coarse)
    scratch = [(2, *lines), lines, lines, lines, relayed, relayed, sems]
    k, g, fs, half, ub, kx, yc, yd, message = call(
        down_kernel, 6, outs, scratch, local, ya, yb, za, zb, ca, cb, specs=[VMEM] * 5 + [FAR] * 2
    )
    if whole:
        yc, kall = lax.optimization_barrier((yc, kall))
    yc, yd = exchange(yc, yd, "gy")
    if whole:
        fall = jnp.stack([message, yc[FACE_ROWS:].reshape(message.shape)])
        fall = swapped(fall, swaps[1], nz, ny)
        kall = swapped(kall, kswaps[-2], nz, ny)
        fall, yc, yd = lax.optimization_barrier((fall, yc, yd))
        for step in swaps[2:-2]:
            fall = swapped(fall, step, nz, ny)
    zface = (ZROWS, LANES)
    zc, zd = call(widen_kernel, 2, (zface, zface), [(2, *face), sems], ub, yc, yd, specs=[VMEM, FAR, FAR])
    if whole:
        fall, zc, zd = lax.optimization_barrier((fall, zc, zd))
    zc, zd = exchange(zc, zd, "gz")
    if whole:
        fall = swapped(fall, swaps[-2], nz, ny)
        ktheirs = swap(kall, kswaps[-1], nz, ny)
        fall, kall, ktheirs, zc, zd = lax.optimization_barrier((fall, kall, ktheirs, zc, zd))
        ftheirs = swap(fall, swaps[-1], nz, ny)
        error, errorx = solve_coarse(fall, ftheirs, kall, ktheirs, nz, ny)
    else:
        error, errorx = solve_coarse_spread(message, kmessage, nz, ny)
    block = (8, 8, 8 * LANES)
    scratch = [lines] * 4 + [(2, 8, 4, LANES)] * 2 + [(2, 8, 64, LANES)]
    return call(up_kernel, 6, (block, block), scratch, k, g, fs, half, ub, kx, yc, yd, zc, zd, error, errorx)


def solution(mesh):
    spec = P("gz", "gy", None)
    return jax.shard_map(
        on_device, mesh=mesh, in_specs=(spec, spec), out_specs=(spec, spec), check_vma=False
    )
```

```python
import jax
import jax.numpy as jnp
from jax import lax
from jax.experimental import pallas as pl
from jax.experimental.pallas import tpu as pltpu
from jax.sharding import PartitionSpec as P

LANES = 128
LINES = 18
LEVELS = 4
PAD = 5
F32 = jnp.float32
VMEM = pl.BlockSpec(memory_space=pltpu.VMEM)
FAR = pl.BlockSpec(memory_space=pl.ANY)
WHOLE_COARSE_CELLS = 1 << 19


def call(body, micros, outs, scratch, *args, specs=None):
    return pl.pallas_call(
        body,
        out_shape=[jax.ShapeDtypeStruct(s, F32) for s in outs],
        in_specs=specs or [VMEM] * len(args),
        out_specs=[VMEM] * len(outs),
        scratch_shapes=[pltpu.VMEM(s, F32) if isinstance(s, tuple) else s for s in scratch],
        cost_estimate=pl.CostEstimate(flops=0, transcendentals=0, bytes_accessed=micros * 3_000_000),
        compiler_params=pltpu.CompilerParams(vmem_limit_bytes=18 << 20),
    )(*args)


def iota(axis, rows=8):
    return lax.broadcasted_iota(jnp.int32, (rows, LANES), axis)


def barrel(arrays, block):
    for bit in (1, 2, 4):
        high = (block & bit) != 0
        arrays = [jnp.where(high, arrays[(j + bit) % 8], arrays[j]) for j in range(8)]
    return arrays


def lane_gather(array, index):
    return jnp.take_along_axis(array, index, axis=1, mode="promise_in_bounds")


def split_lanes(tiles):
    lane = iota(1)
    block = lane // 16
    parts = [lane_gather(tiles[t], 8 * (lane % 16) + (block - t) % 8) for t in range(8)]
    mixed = barrel(parts, block)
    return [pltpu.roll(mixed[-s % 8], (-16 * s) % LANES, axis=1) for s in range(8)]


def join_lanes(arrays):
    lane = iota(1)
    block = lane // 16
    moved = [pltpu.roll(arrays[s], (16 * s) % LANES, axis=1) for s in range(8)]
    mixed = barrel(moved, block)
    return [lane_gather(mixed[-t % 8], 16 * ((lane % 8 + t) % 8) + lane // 8) for t in range(8)]


def put_coarse(message, row, s, value, tail=None):
    for z in range(4):
        e, c = z % 2, (s + z + row) % 2
        m, at = (c * 2 + e) * 2 + s // 2, 2 * row + z // 2
        message[m, at, :] = value[z]
        if tail is not None:
            tail[FACE_ROWS + 8 * m + at, :] = value[z]


REACH = ((0, 0, 4), (0, 1, 3), (1, 0, 4), (1, 1, 5))
YFACE = [(a, c, y, n) for a, c, n in REACH for y in range(n)]
ZFACE = sorted(((a, c, d) for a, c, n in REACH for d in range(1, n + 1)), key=lambda r: r[2] - REACH[2 * r[0] + r[1]][2])
CORNER = {1: (12, 0, 12), 2: (8, 16, 8), 3: (4, 12, 4), 4: (1, 24, 4)}
CORNER_ROWS = 28
FACE_ROWS = 5 * 2 * 4 * 4
DEPTHS = [min(i, 5, LINES - 1 - i) for i in range(LINES)]
ZSTARTS = [4 * sum(DEPTHS[:i]) for i in range(LINES)]
ZROWS = 4 * sum(DEPTHS)


def own_sides():
    return [lax.rem(lax.axis_index(axis), 2) == 0 for axis in ("gz", "gy")]


def halo_cell(side, distance):
    z = 7 + distance if side == 0 else -distance
    return z % 2, (z // 2) % 8


def pick(flag, a, b):
    return jnp.where(flag, a, b), jnp.where(flag, b, a)


def pack_kernel(f_ref, k_ref, local, ya, yb, natural):
    _, yup = own_sides()
    for a, ref in enumerate((f_ref, k_ref)):
        for z in range(8):
            arrays = split_lanes([ref[z, :, t * LANES : (t + 1) * LANES] for t in range(8)])
            for s in range(8):
                natural[a, s, 8 * z : 8 * z + 8, :] = arrays[s]
    for a in range(2):
        for c in range(2):
            for y in range(8):
                for e in range(2):
                    q = (e + y + c) % 2
                    for s in range(4):
                        local[a, c, y, e, s] = natural[a, 2 * s + q, pl.ds(y + 8 * e, 4, stride=16), :]
    for i, (a, c, y, n) in enumerate(YFACE):
        first, second = pick(yup, y + 8 - n, y)
        ya[i] = local[a, c, first]
        yb[i] = local[a, c, second]


def zpack_kernel(local, za, zb, coarse):
    zup, _ = own_sides()

    def faces(y, carry):
        for i, (a, c, d) in enumerate(ZFACE):
            high, low = 8 - d, d - 1
            for s in range(4):
                up = local[a, c, y, high % 2, s, high // 2 : high // 2 + 1]
                down = local[a, c, y, low % 2, s, low // 2 : low // 2 + 1]
                za[y, s, i : i + 1], zb[y, s, i : i + 1] = pick(zup, up, down)
        return carry

    lax.fori_loop(0, 8, faces, 0)
    for row in range(4):
        for s in range(4):
            total = None
            for c in range(2):
                for y in (2 * row, 2 * row + 1):
                    pair = local[1, c, y, 0, s] + local[1, c, y, 1, s]
                    total = pair if total is None else total + pair
            put_coarse(coarse, row, s, total * 0.125)


def relay_kernel(ya_far, yb_far, ca, cb, faces, sem):
    zup, yabove = own_sides()
    slots = pick(yabove, 0, 1)
    copies = [pltpu.make_async_copy(f, faces.at[t], sem.at[i]) for i, (f, t) in enumerate(zip((ya_far, yb_far), slots))]
    for copy in copies:
        copy.start()
    for copy in copies:
        copy.wait()
    for target, up in ((ca, zup), (cb, jnp.logical_not(zup))):
        places = {d: jnp.where(up, 8 - d, d - 1) for d in range(1, 5)}
        for d, (count, at, _) in CORNER.items():
            for i, (a, c, dz) in enumerate(ZFACE[:count]):
                e, t = lax.rem(places[dz], 2), places[dz] // 2
                for side in range(2):
                    y = d - 1 if side == 0 else REACH[2 * a + c][2] - d
                    line = YFACE.index((a, c, y, REACH[2 * a + c][2]))
                    for s in range(4):
                        base = (4 * side + s) * CORNER_ROWS + at + i
                        target[base : base + 1, :] = faces[side, line, e, s, pl.ds(t, 1)]


def neighbours(ref, line, e, s, q, groups, edge=None, first=None, last=None):
    rows = ref.shape[-2]
    lane = iota(1, rows)
    same = ref[line, e, s]
    if q == 0 and s == 0:
        other = jnp.where(lane == 0, 0.0, pltpu.roll(ref[line, e, groups - 1], 1, axis=1))
    elif q == 1 and s == groups - 1:
        other = jnp.where(lane == LANES - 1, 0.0, pltpu.roll(ref[line, e, 0], LANES - 1, axis=1))
    else:
        other = ref[line, e, s + (1 if q else -1)]
    zsame = ref[line, 1 - e, s]
    zother = pltpu.roll(zsame, 1 if e == 0 else rows - 1, axis=0)
    if edge is not None:
        zother = edge(zother, line, e, s)
    return (same + other) + (zsame + zother) + (ref[line - 1, e, s] + ref[line + 1, e, s])


def closed(zother, line, e, s):
    rows = zother.shape[0]
    return jnp.where(iota(0, rows) == (0 if e == 0 else rows - 1), 0.0, zother)


def over_lines(low, high, offset, visit, lines=4):
    steps, rest = divmod(high - low + 1, lines)

    def step(i, carry):
        for j in range(lines):
            visit(low + offset + j + lines * i, (low + j) % 2)
        return carry

    lax.fori_loop(0, steps, step, 0)
    for y in range(high + 1 - rest, high + 1):
        visit(y + offset, y % 2)


def diagonal(k, kother, line, e, s, q, groups, edge=None):
    centre = k[line, e, s]
    return centre, 6.0 * centre + neighbours(kother, line, e, s, q, groups, edge)


def down_kernel(
    local, ya, yb, za, zb, ca_far, cb_far,
    k, g, fs, half, ub, kx, yc, yd, coarse,
    f, ur, vr, vb, ca, cb, sem,
):
    zabove, yabove = own_sides()
    yup = yabove
    copies = [pltpu.make_async_copy(*pair, sem.at[i]) for i, pair in enumerate(((ca_far, ca), (cb_far, cb)))]
    for copy in copies:
        copy.start()
    blank = jnp.zeros((8, LANES), F32)
    for c in range(2):
        for line in (*range(PAD), *range(PAD + 8, LINES)):
            for e in range(2):
                for s in range(4):
                    k[c, line, e, s] = blank
                    f[c, line, e, s] = blank
    both = (f, k)

    def assemble(y, carry):
        for e in range(2):
            for s in range(4):
                f[1, PAD + y, e, s] = blank
                for a in range(2):
                    for c in range(2):
                        both[a][c, PAD + y, e, s, 0:4] = local[a, c, y, e, s]
        for s in range(4):
            for side, part in enumerate(pick(zabove, za[y, s], zb[y, s])):
                for i, (a, c, d) in enumerate(ZFACE):
                    e, row = halo_cell(side, d)
                    if d == 5:
                        kx[side, y, s : s + 1] = part[i : i + 1]
                    else:
                        both[a][c, PAD + y, e, s, row : row + 1] = part[i : i + 1]
        return carry

    lax.fori_loop(0, 8, assemble, 0)
    for i, (a, c, y, n) in enumerate(YFACE):
        first, second = pick(yabove, PAD + y + 8, PAD + y - n)
        for e in range(2):
            for s in range(4):
                both[a][c, first, e, s, 0:4] = ya[i, e, s]
                both[a][c, second, e, s, 0:4] = yb[i, e, s]
    for copy in copies:
        copy.wait()
    for yside in range(2):
        for s in range(4):
            for d, (count, at, _) in CORNER.items():
                line, base = PAD + 7 + d if yside == 0 else PAD - d, (4 * yside + s) * CORNER_ROWS + at
                for side, part in enumerate(pick(zabove, ca[base : base + count, :], cb[base : base + count, :])):
                    for i, (a, c, dz) in enumerate(ZFACE[:count]):
                        e, row = halo_cell(side, dz)
                        both[a][c, line, e, s, row : row + 1] = part[i : i + 1]

    rows = iota(0)

    def far(zother, line, e, s):
        beyond = kx[1 - e, line - PAD, s : s + 1]
        return jnp.where(rows == (6 if e == 0 else 5), jnp.broadcast_to(beyond, (8, LANES)), zother)

    def prepare(c, line, parity, edge, keep):
        for e in range(2):
            q = (e + parity + c) % 2
            for s in range(4):
                centre, total = diagonal(k.at[c], k.at[1 - c], line, e, s, q, 4, edge)
                inside = centre != 0.0
                scale = jnp.where(inside, 1.0 / jnp.where(inside, total, 1.0), 0.0)
                start = 2.0 * f[c, line, e, s] * scale
                g[c, line, e, s] = scale
                fs[c, line, e, s] = start
                if keep:
                    half[line - PAD, e, s] = 0.5 * total
                if c == 0:
                    ur[line, e, s] = start
                    vr[line, e, s] = centre * start

    over_lines(-4, -1, PAD, lambda line, parity: prepare(0, line, parity, None, False))
    over_lines(8, 11, PAD, lambda line, parity: prepare(0, line, parity, None, False))
    over_lines(0, 7, PAD, lambda line, parity: prepare(0, line, parity, far, True))
    over_lines(-3, 10, PAD, lambda line, parity: prepare(1, line, parity, None, False))

    def relax(c, low, high):
        sweep(c, low, high, k, g, fs, (ur, ub), (vr, vb))

    relax(1, -3, 10)
    relax(0, -2, 9)
    relax(1, -1, 8)

    for row in range(4):
        for s in range(4):
            total = None
            for y in (2 * row, 2 * row + 1):
                for e in range(2):
                    line = PAD + y
                    value = red_residual(line, y % 2, e, s, k, g, fs, half, ur, ub, vb)
                    total = value if total is None else total + value
            put_coarse(coarse, row, s, total * 0.125, yc)

    first, second = pick(yup, PAD + 3, PAD)
    for i in range(5):
        for e in range(2):
            for s in range(4):
                at = ((i * 2 + e) * 4 + s) * 4
                yc[at : at + 4, :] = ub[first + i, e, s, 0:4]
                yd[at : at + 4, :] = ub[second + i, e, s, 0:4]


def widen_kernel(ub, yc_far, yd_far, zc, zd, faces, sem):
    zup, yabove = own_sides()
    slots, face = pick(yabove, 0, 1), pl.ds(0, FACE_ROWS)
    copies = [
        pltpu.make_async_copy(f.at[face], faces.at[t], sem.at[i]) for i, (f, t) in enumerate(zip((yc_far, yd_far), slots))
    ]
    for copy in copies:
        copy.start()

    def put(line, fetch):
        for target, up in ((zc, zup), (zd, jnp.logical_not(zup))):
            for d in range(1, DEPTHS[line] + 1):
                z = jnp.where(up, 8 - d, d - 1)
                for s in range(4):
                    at = ZSTARTS[line] + s * DEPTHS[line] + d - 1
                    target[at : at + 1, :] = fetch(lax.rem(z, 2), s, z // 2)

    for line in range(PAD, PAD + 8):
        put(line, lambda e, s, t: ub[line, e, s, pl.ds(t, 1)])
    for copy in copies:
        copy.wait()
    for i in range(5):
        for side, line in enumerate((PAD + 8 + i, i)):
            put(line, lambda e, s, t: faces[side, pl.ds(((i * 2 + e) * 4 + s) * 4 + t, 1), :])


def sweep(c, low, high, k, g, fs, u, v, edges=(None, None)):
    def visit(line, parity):
        for e in range(2):
            q = (e + parity + c) % 2
            for s in range(4):
                near = neighbours(u[1 - c], line, e, s, q, 4, edges[0])
                flow = neighbours(v[1 - c], line, e, s, q, 4, edges[1])
                centre = k[c, line, e, s]
                value = fs[c, line, e, s] + g[c, line, e, s] * (centre * near + flow)
                u[c][line, e, s] = value
                v[c][line, e, s] = centre * value

    over_lines(low, high, PAD, visit)


def red_residual(line, parity, e, s, k, g, fs, half, ur, ub, vb):
    q = (e + parity) % 2
    near = neighbours(ub, line, e, s, q, 4)
    flow = neighbours(vb, line, e, s, q, 4)
    fresh = fs[0, line, e, s] + g[0, line, e, s] * (k[0, line, e, s] * near + flow)
    return half[line - PAD, e, s] * (fresh - ur[line, e, s])


def up_kernel(
    k, g, fs, half, old, kx, yc, yd, zc, zd, error, errorx,
    correction, residual,
    ub, ur, vb, vr, ux, vx, natural,
):
    zabove, yabove = own_sides()
    for y in range(8):
        for e in range(2):
            for s in range(4):
                ub[PAD + y, e, s, 0:4] = old[PAD + y, e, s, 0:4]
    first, second = pick(yabove, PAD + 8, 0)
    for i in range(5):
        for e in range(2):
            for s in range(4):
                at = ((i * 2 + e) * 4 + s) * 4
                ub[first + i, e, s, 0:4] = yc[at : at + 4, :]
                ub[second + i, e, s, 0:4] = yd[at : at + 4, :]
    quiet = jnp.zeros((4, LANES), F32)
    for line, depth in enumerate(DEPTHS):
        for s in range(4):
            if depth < 4:
                for e in range(2):
                    ub[line, e, s, 4:8] = quiet
            if not depth:
                continue
            at = ZSTARTS[line] + s * depth
            for side, part in enumerate(pick(zabove, zc[at : at + depth, :], zd[at : at + depth, :])):
                for d in range(1, min(depth, 4) + 1):
                    e, row = halo_cell(side, d)
                    ub[line, e, s, row : row + 1] = part[d - 1 : d]
                if depth == 5:
                    y = line - PAD
                    beyond = kx[side, y, s : s + 1]
                    value = part[4:5] + errorx[side, y // 2, s : s + 1]
                    value = jnp.where(beyond != 0.0, value, 0.0)
                    ux[side, y, s : s + 1] = value
                    vx[side, y, s : s + 1] = beyond * value

    def add(line, parity):
        for e in range(2):
            for s in range(4):
                centre = k[1, line, e, s]
                value = ub[line, e, s] + error[(line + 1) // 2, s]
                value = jnp.where(centre != 0.0, value, 0.0)
                ub[line, e, s] = value
                vb[line, e, s] = centre * value

    over_lines(-5, 12, PAD, add)

    rows = iota(0)

    def far(ref):
        def edge(zother, line, e, s):
            beyond = ref[1 - e, line - PAD, s : s + 1]
            return jnp.where(rows == (6 if e == 0 else 5), jnp.broadcast_to(beyond, (8, LANES)), zother)

        return edge

    u, v = (ur, ub), (vr, vb)
    sweep(0, -4, -1, k, g, fs, u, v)
    sweep(0, 8, 11, k, g, fs, u, v)
    sweep(0, 0, 7, k, g, fs, u, v, (far(ux), far(vx)))
    sweep(1, -3, 10, k, g, fs, u, v)
    sweep(0, -2, 9, k, g, fs, u, v)
    sweep(1, -1, 8, k, g, fs, u, v)

    quiet = jnp.zeros((4, LANES), F32)
    for y in range(8):
        for e in range(2):
            at = pl.ds(y + 8 * e, 4, stride=16)
            q = (e + y) % 2
            for s in range(4):
                value = red_residual(PAD + y, y % 2, e, s, k, g, fs, half, ur, ub, vb)
                natural[1, 2 * s + q, at, :] = value[0:4]
                natural[1, 2 * s + 1 - q, at, :] = quiet
                natural[0, 2 * s + q, at, :] = ur[PAD + y, e, s, 0:4]
                natural[0, 2 * s + 1 - q, at, :] = ub[PAD + y, e, s, 0:4]
    for a, out in enumerate((correction, residual)):
        for z in range(8):
            tiles = join_lanes([natural[a, s, 8 * z : 8 * z + 8, :] for s in range(8)])
            for t in range(8):
                out[z, :, t * LANES : (t + 1) * LANES] = tiles[t]


def shifted(value, step, axis):
    size = value.shape[axis]
    where = iota(axis, value.shape[0])
    moved = pltpu.roll(value, -step % size, axis=axis)
    return jnp.where((where >= size - step) if step > 0 else (where < -step), 0.0, moved)


def coarse_kernel(nz, ny):
    height, depth = 4 * ny, 2 * nz
    height2, height3 = height // 2, height // 4

    def body(
        fmine, ftheirs_far, kmine, ktheirs, error, errorx,
        f, k, g, fs, half, ur, ub, vr, vb, f2, k2, fc, kc, gc, sc, uc, vc, hc, w3, f3, ftheirs, sem,
    ):
        u, v = (ur, ub), (vr, vb)
        zplace, yplace = lax.axis_index("gz"), lax.axis_index("gy")

        def slot(i, j, swaps):
            apart = (zplace * ny + yplace) ^ (i * ny + j)
            return sum(((apart >> step) & 1) << bit for bit, step in enumerate(swaps[:-1]))

        def spread(odd, sources, target, swaps):
            def visit(j, carry):
                order = [slot(i, j, swaps) for i in range(nz)]
                for m in range(8):
                    pieces = [sources[(i + odd) % 2][order[i], m] for i in range(nz)]
                    for row in range(4):
                        whole = jnp.concatenate([p[2 * row : 2 * row + 2] for p in pieces], axis=0)
                        target[m // 4, 1 + 4 * j + row, m // 2 % 2, m % 2] = whole
                return carry

            lax.fori_loop(0, ny, visit, 0)

        def spread_either(*args):
            for odd in range(2):
                pl.when(lax.rem(zplace, 2) == odd)(lambda odd=odd: spread(odd, *args))

        copy = pltpu.make_async_copy(ftheirs_far, ftheirs, sem)
        copy.start()
        spread_either((kmine, ktheirs), k, swap_steps(nz, ny))
        copy.wait()
        spread_either((fmine, ftheirs), f, swap_steps(nz, ny, 0))
        blank = jnp.zeros((depth, LANES), F32)
        for line in (0, height + 1):
            for e in range(2):
                for s in range(2):
                    for c in range(2):
                        k[c, line, e, s] = blank
                        u[c][line, e, s] = blank
                        v[c][line, e, s] = blank

        def prepare(c):
            def visit(line, parity):
                for e in range(2):
                    for s in range(2):
                        centre, total = diagonal(k.at[c], k.at[1 - c], line, e, s, (e + parity + c) % 2, 2, closed)
                        scale = 1.0 / total
                        start = 8.0 * f[c, line, e, s] * scale
                        g[c, line, e, s] = scale
                        fs[c, line, e, s] = start
                        if c == 0:
                            half[line, e, s] = 0.125 * total
                            ur[line, e, s] = start
                            vr[line, e, s] = centre * start

            over_lines(0, height - 1, 1, visit, 8)

        def fresh(c, line, parity, e, s):
            q = (e + parity + c) % 2
            near = neighbours(u[1 - c], line, e, s, q, 2, closed)
            flow = neighbours(v[1 - c], line, e, s, q, 2, closed)
            return fs[c, line, e, s] + g[c, line, e, s] * (k[c, line, e, s] * near + flow)

        def relax(c):
            def visit(line, parity):
                for e in range(2):
                    for s in range(2):
                        value = fresh(c, line, parity, e, s)
                        u[c][line, e, s] = value
                        v[c][line, e, s] = k[c, line, e, s] * value

            over_lines(0, height - 1, 1, visit, 8)

        prepare(0)
        prepare(1)
        relax(1)
        relax(0)
        relax(1)

        def restrict(i, carry):
            for s in range(2):
                value, conduct = None, None
                for j in range(2):
                    line = 1 + 2 * i + j
                    for e in range(2):
                        part = half[line, e, s] * (fresh(0, line, j, e, s) - ur[line, e, s])
                        value = part if value is None else value + part
                        part = k[0, line, e, s] + k[1, line, e, s]
                        conduct = part if conduct is None else conduct + part
                f2[s, i] = value * 0.125
                k2[s, i] = conduct * 0.125
            return carry

        lax.fori_loop(0, height2, restrict, 0)

        even = iota(0, depth) % 2 == 0

        def q_is_zero(c, y):
            return even if (y + c) % 2 == 0 else jnp.logical_not(even)

        def coloured(pair, c, y):
            return jnp.where(q_is_zero(c, y), pair[0], pair[1])

        def around(ref, c, y):
            mid = ref[1 + y]
            other = jnp.where(q_is_zero(c, y), shifted(mid, -1, 1), shifted(mid, 1, 1))
            return (mid + other) + (shifted(mid, -1, 0) + shifted(mid, 1, 0)) + (ref[y] + ref[y + 2])

        for c in range(2):
            for line in (0, height2 + 1):
                kc[c, line] = blank
                uc[c, line] = blank
                vc[c, line] = blank
            for y in range(height2):
                kc[c, 1 + y] = coloured((k2[0, y], k2[1, y]), c, y)
                fc[c, y] = coloured((f2[0, y], f2[1, y]), c, y)
        for c in range(2):
            for y in range(height2):
                centre = kc[c, 1 + y]
                total = 6.0 * centre + around(kc.at[1 - c], c, y)
                scale = 1.0 / total
                start = 32.0 * fc[c, y] * scale
                gc[c, y] = scale
                sc[c, y] = start
                if c == 0:
                    hc[y] = total * (0.5 / 16.0)
                    uc[0, 1 + y] = start
                    vc[0, 1 + y] = centre * start

        def fresh2(c, y):
            flow = kc[c, 1 + y] * around(uc.at[1 - c], c, y) + around(vc.at[1 - c], c, y)
            return sc[c, y] + gc[c, y] * flow

        def relax2(c):
            for y in range(height2):
                value = fresh2(c, y)
                uc[c, 1 + y] = value
                vc[c, 1 + y] = kc[c, 1 + y] * value

        relax2(1)
        relax2(0)
        relax2(1)

        def paired(a, b):
            total = (a + b) * 0.125
            return jnp.where(even, total + pltpu.roll(total, depth - 1, axis=0), 0.0)

        conduct = []
        right = []
        for y in range(height3):
            parts = [hc[2 * y + j] * (fresh2(0, 2 * y + j) - uc[0, 1 + 2 * y + j]) for j in range(2)]
            right.append(paired(*parts))
            parts = [kc[0, 1 + 2 * y + j] + kc[1, 1 + 2 * y + j] for j in range(2)]
            conduct.append(paired(*parts))
        moves = ((-2, 0), (2, 0), (-1, 1), (1, 1))
        for y in range(height3):
            centre = conduct[y]
            beside = [shifted(centre, step, axis) for step, axis in moves]
            beside.append(conduct[y - 1] if y else jnp.zeros_like(centre))
            beside.append(conduct[y + 1] if y + 1 < height3 else jnp.zeros_like(centre))
            total = 6.0 * centre
            for part in beside:
                total = total + part
            scale = jnp.where(even, 1.0 / jnp.where(even, total, 1.0), 0.0)
            f3[y] = 128.0 * right[y] * scale
            lane, row = iota(1, depth), iota(0, depth)
            open_faces = (row >= 2, row < depth - 2, lane >= 1, lane < LANES - 1)
            for i in range(6):
                weight = (centre + beside[i]) * scale
                w3[y, i] = jnp.where(open_faces[i], weight, 0.0) if i < 4 else weight
        mixed = (iota(0, depth) // 2 + iota(1, depth)) % 2

        def relax3(c, field):
            result = []
            for y in range(height3):
                mid = field[y]
                value = f3[y]
                for i, (step, axis) in enumerate(moves):
                    value = value + w3[y, i] * pltpu.roll(mid, -step % mid.shape[axis], axis=axis)
                if y:
                    value = value + w3[y, 4] * field[y - 1]
                if y + 1 < height3:
                    value = value + w3[y, 5] * field[y + 1]
                result.append(jnp.where(mixed == (y + c) % 2, value, mid))
            return result

        def two_colours(_, field):
            return tuple(relax3(1, relax3(0, list(field))))

        field = lax.fori_loop(0, 12, two_colours, (blank,) * height3)

        for y in range(height2):
            coarse = field[y // 2]
            value = uc[1, 1 + y] + (coarse + pltpu.roll(coarse, 1, axis=0))
            uc[1, 1 + y] = value
            vc[1, 1 + y] = kc[1, 1 + y] * value
        for c in (0, 1, 0, 1):
            relax2(c)

        for y in range(height2):
            zero = q_is_zero(0, y)
            red, black = uc[0, 1 + y], uc[1, 1 + y]
            f2[0, y] = jnp.where(zero, red, black)
            f2[1, y] = jnp.where(zero, black, red)

        def add(line, parity):
            for e in range(2):
                for s in range(2):
                    value = ub[line, e, s] + f2[s, (line - 1) // 2]
                    ub[line, e, s] = value
                    vb[line, e, s] = k[1, line, e, s] * value

        over_lines(0, height - 1, 1, add, 8)
        for c in (0, 1, 0, 1):
            relax(c)

        for j in range(-3, 7):
            line = 1 + jnp.clip(4 * yplace + j, 0, height - 1)
            for t in range(-3, 7):
                e = t % 2
                at = pl.ds(jnp.clip(2 * zplace + t // 2, 0, depth - 1), 1)
                for s in range(4):
                    row = u[(s + e + j) % 2][line, e, s // 2, at, :]
                    if -2 <= t <= 5:
                        error[j + 3, s, t % 8 : t % 8 + 1, :] = row
                    elif 0 <= j < 8 // 2:
                        errorx[1 if t < 0 else 0, j, s : s + 1, :] = row

    lines, lines2 = (height + 2, 2, 2, depth, LANES), (height2 + 2, depth, LANES)
    flat2 = (2, height2, depth, LANES)
    scratch = [(2, *lines)] * 4 + [lines] * 5 + [flat2, flat2, flat2, (2, *lines2), flat2, flat2]
    scratch += [(2, *lines2), (2, *lines2), flat2[1:], (height3, 6, depth, LANES), (height3, depth, LANES)]
    scratch += [(nz * ny // 2, 8, 8, LANES), pltpu.SemaphoreType.DMA(())]
    return body, scratch


def swap_steps(nz, ny, first=None):
    ybits, zbits = ny.bit_length() - 1, nz.bit_length() - 1
    along_y = list(range(ybits - 1, -1, -1))
    if first is not None:
        along_y = [first, *(bit for bit in along_y if bit != first)]
    return [*along_y, *range(ybits + zbits - 1, ybits - 1, -1)]


def swap(block, step, nz, ny):
    return lax.ppermute(block, ("gz", "gy"), [(i, i ^ (1 << step)) for i in range(nz * ny)])


def swapped(block, step, nz, ny):
    return jnp.concatenate([block, swap(block, step, nz, ny)])


def solve_coarse(fmine, ftheirs, kmine, ktheirs, nz, ny):
    body, scratch = coarse_kernel(nz, ny)
    outs = ((10, 4, 8, LANES), (2, 4, 4, LANES))
    return call(body, 11, outs, scratch, fmine, ftheirs, kmine, ktheirs, specs=[VMEM, FAR, VMEM, VMEM])


def extended(array, sides, width):
    for axis, dim in sides:
        size, length = (lax.axis_size(axis), array.shape[dim])
        up = [(i, (i + 1) % size) for i in range(size - 1)]
        down = [(j, i) for i, j in up]
        last = lax.slice_in_dim(array, length - width, length, axis=dim)
        initial = lax.slice_in_dim(array, 0, width, axis=dim)
        before = lax.ppermute(last, axis, up)
        after = lax.ppermute(initial, axis, down)
        array = jnp.concatenate([before, array, after], axis=dim)
    return array


def coarsen(field):
    total = field[0::2, 0::2, 0::2] + field[0::2, 0::2, 1::2]
    total = total + field[0::2, 1::2, 0::2] + field[0::2, 1::2, 1::2]
    total = total + field[1::2, 0::2, 0::2] + field[1::2, 0::2, 1::2]
    total = total + field[1::2, 1::2, 0::2] + field[1::2, 1::2, 1::2]
    return total * 0.125


def prolong(field):
    return jnp.repeat(jnp.repeat(jnp.repeat(field, 2, axis=0), 2, axis=1), 2, axis=2)


def face_terms(kpad):
    center = kpad[1:-1, 1:-1, 1:-1]
    z_minus = 0.5 * (center + kpad[:-2, 1:-1, 1:-1])
    z_plus = 0.5 * (center + kpad[2:, 1:-1, 1:-1])
    y_minus = 0.5 * (center + kpad[1:-1, :-2, 1:-1])
    y_plus = 0.5 * (center + kpad[1:-1, 2:, 1:-1])
    x_minus = 0.5 * (center + kpad[1:-1, 1:-1, :-2])
    x_plus = 0.5 * (center + kpad[1:-1, 1:-1, 2:])
    total = z_minus + z_plus + y_minus + y_plus + x_minus + x_plus
    return ((z_minus, z_plus, y_minus, y_plus, x_minus, x_plus), total)


def neighbour_sum(weights, upad):
    z_minus, z_plus, y_minus, y_plus, x_minus, x_plus = weights
    acc = z_minus * upad[:-2, 1:-1, 1:-1] + z_plus * upad[2:, 1:-1, 1:-1]
    acc = acc + y_minus * upad[1:-1, :-2, 1:-1] + y_plus * upad[1:-1, 2:, 1:-1]
    acc = acc + x_minus * upad[1:-1, 1:-1, :-2] + x_plus * upad[1:-1, 1:-1, 2:]
    return acc


def extend(field, layout):
    if layout == "column":
        wider = extended(field, (("gy", 1),), 1)
        wider = jnp.pad(wider, ((1, 1), (0, 0), (0, 0)))
    else:
        wider = extended(field, (("gz", 0), ("gy", 1)), 1)
    return jnp.pad(wider, ((0, 0), (0, 0), (1, 1)))


def region_masks(shape, z_start, y_start):
    zpos = lax.broadcasted_iota(jnp.int32, shape, 0) + z_start
    ypos = lax.broadcasted_iota(jnp.int32, shape, 1) + y_start
    xpos = lax.broadcasted_iota(jnp.int32, shape, 2)
    return (zpos + ypos + xpos + 4) % 2


def cycle(rhs, conduct, level, layout, z_start, y_start, z_total, y_total):
    scale = 4.0**level
    weights, total = face_terms(extend(conduct, layout))
    parity = region_masks(rhs.shape, z_start, y_start)
    first = parity == 0
    second = parity == 1

    def relax(field, colour):
        fresh = (scale * rhs + neighbour_sum(weights, extend(field, layout))) / total
        return jnp.where(colour, fresh, field)

    def smooth(field, sweeps):
        for sweep in range(sweeps):
            for colour in (first, second):
                field = relax(field, colour)
        return field

    def remainder(field):
        return rhs - (total * field - neighbour_sum(weights, extend(field, layout))) / scale

    field = jnp.zeros(rhs.shape, jnp.float32)
    if level == LEVELS - 1:
        return (smooth(field, 12), None)
    field = smooth(field, 2)
    rhs_next = coarsen(remainder(field))
    conduct_next = coarsen(conduct)
    joined = layout == "split" and level == 1
    if joined:
        local_depth = rhs_next.shape[0]
        rhs_next, conduct_next = (
            lax.all_gather(rhs_next, "gz", axis=0, tiled=True),
            lax.all_gather(conduct_next, "gz", axis=0, tiled=True),
        )
        error, unused = cycle(
            rhs_next, conduct_next, level + 1, "column", 0, y_start // 2, z_total // 2, y_total // 2
        )
        error = lax.dynamic_slice_in_dim(error, lax.axis_index("gz") * local_depth, local_depth, 0)
    else:
        error, unused = cycle(
            rhs_next,
            conduct_next,
            level + 1,
            layout,
            z_start // 2,
            y_start // 2,
            z_total // 2,
            y_total // 2,
        )
    field = field + prolong(error)
    field = smooth(field, 2)
    return (field, remainder(field))


def natural_coarse(message):
    packed = message.reshape(2, 2, 2, 4, 2, LANES)
    parity = (jnp.arange(2)[:, None, None, None, None] + jnp.arange(4)[None, None, :, None, None]) % 2 == 0
    even = jnp.where(parity, packed[0], packed[1])
    odd = jnp.where(parity, packed[1], packed[0])
    both = jnp.stack([even, odd])
    return both.transpose(4, 1, 3, 5, 2, 0).reshape(4, 4, 4 * LANES)


def solve_coarse_spread(message, kmessage, nz, ny):
    z_start, y_start = 4 * lax.axis_index("gz"), 4 * lax.axis_index("gy")
    field, unused = cycle(
        natural_coarse(message), natural_coarse(kmessage), 1, "split", z_start, y_start, 4 * nz, 4 * ny
    )
    wide = extended(field, (("gz", 0), ("gy", 1)), 3).reshape(10, 10, LANES, 4).transpose(1, 3, 0, 2)
    error = jnp.concatenate([wide[:, :, 3:9], wide[:, :, 1:3]], axis=2)
    return error, jnp.stack([wide[3:7, :, 9], wide[3:7, :, 0]])


def exchange(first, second, axis):
    size = lax.axis_size(axis)
    results = []
    for message, start in ((first, 0), (second, 1)):
        pairs = [(i, i + 1) for i in range(start, size - 1, 2)]
        results.append(lax.ppermute(message, axis, pairs + [(j, i) for i, j in pairs]))
    return results


def on_device(right_side, coefficient):
    nz, ny = lax.axis_size("gz"), lax.axis_size("gy")
    assert right_side.shape == (8, 8, 8 * LANES)
    cells = (2, 2, 8, 2, 4, 4, LANES)
    yface, zface = (16, 2, 4, 4, LANES), (8, 4, 16, LANES)
    coarse = (8, 8, LANES)
    packed = call(pack_kernel, 3, (cells, yface, yface), [(2, 8, 64, LANES)], right_side, coefficient)
    local, ya, yb = packed
    ya, yb = exchange(ya, yb, "gy")
    za, zb, kmessage = call(zpack_kernel, 2, (zface, zface, coarse), [], local)
    za, zb = exchange(za, zb, "gz")
    coarse_cells = 8 * 8 * LANES
    whole = nz * ny * coarse_cells <= WHOLE_COARSE_CELLS and nz & (nz - 1) == 0 and ny & (ny - 1) == 0
    swaps, kswaps = swap_steps(nz, ny, 0), swap_steps(nz, ny)
    kall = kmessage[None]
    if whole:
        kall = swapped(kall, kswaps[0], nz, ny)
        ya, yb, za, zb, kall = lax.optimization_barrier((ya, yb, za, zb, kall))
    relayed, sems = (8 * CORNER_ROWS, LANES), pltpu.SemaphoreType.DMA((2,))
    corners = call(relay_kernel, 2, (relayed, relayed), [(2, *yface), sems], ya, yb, specs=[FAR] * 2)
    ca, cb = exchange(*corners, "gz")
    if whole:
        for step in kswaps[1:-3]:
            kall = swapped(kall, step, nz, ny)
    lines, face = (LINES, 2, 4, 8, LANES), (FACE_ROWS, LANES)
    outs = ((2, *lines), (2, *lines), (2, *lines), (8, *lines[1:]), lines, (2, 8, 4, LANES))
    outs += ((FACE_ROWS + 64, LANES), face, coarse)
    scratch = [(2, *lines), lines, lines, lines, relayed, relayed, sems]
    k, g, fs, half, ub, kx, yc, yd, message = call(
        down_kernel, 6, outs, scratch, local, ya, yb, za, zb, ca, cb, specs=[VMEM] * 5 + [FAR] * 2
    )
    if whole:
        yc, kall = lax.optimization_barrier((yc, kall))
    yc, yd = exchange(yc, yd, "gy")
    if whole:
        fall = jnp.stack([message, yc[FACE_ROWS:].reshape(message.shape)])
        kall = swapped(kall, kswaps[-3], nz, ny)
        fall = swapped(fall, swaps[1], nz, ny)
        fall, kall = lax.optimization_barrier((fall, kall))
        kall = swapped(kall, kswaps[-2], nz, ny)
        for step in swaps[2:-2]:
            fall = swapped(fall, step, nz, ny)
    zface = (ZROWS, LANES)
    zc, zd = call(widen_kernel, 1, (zface, zface), [(2, *face), sems], ub, yc, yd, specs=[VMEM, FAR, FAR])
    if whole:
        fall, kall, zc, zd = lax.optimization_barrier((fall, kall, zc, zd))
    zc, zd = exchange(zc, zd, "gz")
    if whole:
        fall = swapped(fall, swaps[-2], nz, ny)
        ktheirs = swap(kall, kswaps[-1], nz, ny)
        fall, kall, ktheirs, zc, zd = lax.optimization_barrier((fall, kall, ktheirs, zc, zd))
        ftheirs = swap(fall, swaps[-1], nz, ny)
        error, errorx = solve_coarse(fall, ftheirs, kall, ktheirs, nz, ny)
    else:
        error, errorx = solve_coarse_spread(message, kmessage, nz, ny)
    block = (8, 8, 8 * LANES)
    scratch = [lines] * 4 + [(2, 8, 4, LANES)] * 2 + [(2, 8, 64, LANES)]
    return call(up_kernel, 6, (block, block), scratch, k, g, fs, half, ub, kx, yc, yd, zc, zd, error, errorx)


def solution(mesh):
    spec = P("gz", "gy", None)
    return jax.shard_map(
        on_device, mesh=mesh, in_specs=(spec, spec), out_specs=(spec, spec), check_vma=False
    )
```

```python
import jax
import jax.numpy as jnp
from jax import lax
from jax.experimental import pallas as pl
from jax.experimental.pallas import tpu as pltpu
from jax.sharding import PartitionSpec as P

LANES = 128
LINES = 18
LEVELS = 4
PAD = 5
F32 = jnp.float32
VMEM = pl.BlockSpec(memory_space=pltpu.VMEM)
FAR = pl.BlockSpec(memory_space=pl.ANY)
WHOLE_COARSE_CELLS = 1 << 19


def call(body, micros, outs, scratch, *args, specs=None):
    return pl.pallas_call(
        body,
        out_shape=[jax.ShapeDtypeStruct(s, F32) for s in outs],
        in_specs=specs or [VMEM] * len(args),
        out_specs=[VMEM] * len(outs),
        scratch_shapes=[pltpu.VMEM(s, F32) if isinstance(s, tuple) else s for s in scratch],
        cost_estimate=pl.CostEstimate(flops=0, transcendentals=0, bytes_accessed=micros * 3_000_000),
        compiler_params=pltpu.CompilerParams(vmem_limit_bytes=18 << 20),
    )(*args)


def iota(axis, rows=8):
    return lax.broadcasted_iota(jnp.int32, (rows, LANES), axis)


def barrel(arrays, block):
    for bit in (1, 2, 4):
        high = (block & bit) != 0
        arrays = [jnp.where(high, arrays[(j + bit) % 8], arrays[j]) for j in range(8)]
    return arrays


def lane_gather(array, index):
    return jnp.take_along_axis(array, index, axis=1, mode="promise_in_bounds")


def split_lanes(tiles):
    lane = iota(1)
    block = lane // 16
    parts = [lane_gather(tiles[t], 8 * (lane % 16) + (block - t) % 8) for t in range(8)]
    mixed = barrel(parts, block)
    return [pltpu.roll(mixed[-s % 8], (-16 * s) % LANES, axis=1) for s in range(8)]


def join_lanes(arrays):
    lane = iota(1)
    block = lane // 16
    moved = [pltpu.roll(arrays[s], (16 * s) % LANES, axis=1) for s in range(8)]
    mixed = barrel(moved, block)
    return [lane_gather(mixed[-t % 8], 16 * ((lane % 8 + t) % 8) + lane // 8) for t in range(8)]


def put_coarse(message, row, s, value, tail=None):
    for z in range(4):
        e, c = z % 2, (s + z + row) % 2
        m, at = (c * 2 + e) * 2 + s // 2, 2 * row + z // 2
        message[m, at, :] = value[z]
        if tail is not None:
            tail[FACE_ROWS + 8 * m + at, :] = value[z]


REACH = ((0, 0, 4), (0, 1, 3), (1, 0, 4), (1, 1, 5))
YFACE = [(a, c, y, n) for a, c, n in REACH for y in range(n)]
ZFACE = sorted(((a, c, d) for a, c, n in REACH for d in range(1, n + 1)), key=lambda r: r[2] - REACH[2 * r[0] + r[1]][2])
CORNER = {1: (12, 0, 12), 2: (8, 16, 8), 3: (4, 12, 4), 4: (1, 24, 4)}
CORNER_ROWS = 28
FACE_ROWS = 5 * 2 * 4 * 4
DEPTHS = [min(i, 5, LINES - 1 - i) for i in range(LINES)]
ZSTARTS = [4 * sum(DEPTHS[:i]) for i in range(LINES)]
ZROWS = 4 * sum(DEPTHS)


def own_sides():
    return [lax.rem(lax.axis_index(axis), 2) == 0 for axis in ("gz", "gy")]


def halo_cell(side, distance):
    z = 7 + distance if side == 0 else -distance
    return z % 2, (z // 2) % 8


def pick(flag, a, b):
    return jnp.where(flag, a, b), jnp.where(flag, b, a)


def pack_kernel(f_ref, k_ref, local, ya, yb, natural):
    _, yup = own_sides()
    for a, ref in enumerate((f_ref, k_ref)):
        for z in range(8):
            arrays = split_lanes([ref[z, :, t * LANES : (t + 1) * LANES] for t in range(8)])
            for s in range(8):
                natural[a, s, 8 * z : 8 * z + 8, :] = arrays[s]
    for a in range(2):
        for c in range(2):
            for y in range(8):
                for e in range(2):
                    q = (e + y + c) % 2
                    for s in range(4):
                        local[a, c, y, e, s] = natural[a, 2 * s + q, pl.ds(y + 8 * e, 4, stride=16), :]
    for i, (a, c, y, n) in enumerate(YFACE):
        first, second = pick(yup, y + 8 - n, y)
        ya[i] = local[a, c, first]
        yb[i] = local[a, c, second]


def zpack_kernel(local, za, zb, coarse):
    zup, _ = own_sides()

    def faces(y, carry):
        for i, (a, c, d) in enumerate(ZFACE):
            high, low = 8 - d, d - 1
            for s in range(4):
                up = local[a, c, y, high % 2, s, high // 2 : high // 2 + 1]
                down = local[a, c, y, low % 2, s, low // 2 : low // 2 + 1]
                za[y, s, i : i + 1], zb[y, s, i : i + 1] = pick(zup, up, down)
        return carry

    lax.fori_loop(0, 8, faces, 0)
    for row in range(4):
        for s in range(4):
            total = None
            for c in range(2):
                for y in (2 * row, 2 * row + 1):
                    pair = local[1, c, y, 0, s] + local[1, c, y, 1, s]
                    total = pair if total is None else total + pair
            put_coarse(coarse, row, s, total * 0.125)


def relay_kernel(ya_far, yb_far, ca, cb, faces, sem):
    zup, yabove = own_sides()
    slots = pick(yabove, 0, 1)
    copies = [pltpu.make_async_copy(f, faces.at[t], sem.at[i]) for i, (f, t) in enumerate(zip((ya_far, yb_far), slots))]
    for copy in copies:
        copy.start()
    for copy in copies:
        copy.wait()
    for target, up in ((ca, zup), (cb, jnp.logical_not(zup))):
        places = {d: jnp.where(up, 8 - d, d - 1) for d in range(1, 5)}
        for d, (count, at, _) in CORNER.items():
            for i, (a, c, dz) in enumerate(ZFACE[:count]):
                e, t = lax.rem(places[dz], 2), places[dz] // 2
                for side in range(2):
                    y = d - 1 if side == 0 else REACH[2 * a + c][2] - d
                    line = YFACE.index((a, c, y, REACH[2 * a + c][2]))
                    for s in range(4):
                        base = (4 * side + s) * CORNER_ROWS + at + i
                        target[base : base + 1, :] = faces[side, line, e, s, pl.ds(t, 1)]


def neighbours(ref, line, e, s, q, groups, edge=None, first=None, last=None):
    rows = ref.shape[-2]
    lane = iota(1, rows)
    same = ref[line, e, s]
    if q == 0 and s == 0:
        other = jnp.where(lane == 0, 0.0, pltpu.roll(ref[line, e, groups - 1], 1, axis=1))
    elif q == 1 and s == groups - 1:
        other = jnp.where(lane == LANES - 1, 0.0, pltpu.roll(ref[line, e, 0], LANES - 1, axis=1))
    else:
        other = ref[line, e, s + (1 if q else -1)]
    zsame = ref[line, 1 - e, s]
    zother = pltpu.roll(zsame, 1 if e == 0 else rows - 1, axis=0)
    if edge is not None:
        zother = edge(zother, line, e, s)
    return (same + other) + (zsame + zother) + (ref[line - 1, e, s] + ref[line + 1, e, s])


def closed(zother, line, e, s):
    rows = zother.shape[0]
    return jnp.where(iota(0, rows) == (0 if e == 0 else rows - 1), 0.0, zother)


def over_lines(low, high, offset, visit, lines=4):
    steps, rest = divmod(high - low + 1, lines)

    def step(i, carry):
        for j in range(lines):
            visit(low + offset + j + lines * i, (low + j) % 2)
        return carry

    lax.fori_loop(0, steps, step, 0)
    for y in range(high + 1 - rest, high + 1):
        visit(y + offset, y % 2)


def diagonal(k, kother, line, e, s, q, groups, edge=None):
    centre = k[line, e, s]
    return centre, 6.0 * centre + neighbours(kother, line, e, s, q, groups, edge)


def down_kernel(
    local, ya, yb, za, zb, ca_far, cb_far,
    k, g, fs, half, ub, kx, yc, yd, coarse,
    f, ur, vr, vb, ca, cb, sem,
):
    zabove, yabove = own_sides()
    yup = yabove
    copies = [pltpu.make_async_copy(*pair, sem.at[i]) for i, pair in enumerate(((ca_far, ca), (cb_far, cb)))]
    for copy in copies:
        copy.start()
    blank = jnp.zeros((8, LANES), F32)
    for c in range(2):
        for line in (*range(PAD), *range(PAD + 8, LINES)):
            for e in range(2):
                for s in range(4):
                    k[c, line, e, s] = blank
                    f[c, line, e, s] = blank
    both = (f, k)

    def assemble(y, carry):
        for e in range(2):
            for s in range(4):
                f[1, PAD + y, e, s] = blank
                for a in range(2):
                    for c in range(2):
                        both[a][c, PAD + y, e, s, 0:4] = local[a, c, y, e, s]
        for s in range(4):
            for side, part in enumerate(pick(zabove, za[y, s], zb[y, s])):
                for i, (a, c, d) in enumerate(ZFACE):
                    e, row = halo_cell(side, d)
                    if d == 5:
                        kx[side, y, s : s + 1] = part[i : i + 1]
                    else:
                        both[a][c, PAD + y, e, s, row : row + 1] = part[i : i + 1]
        return carry

    lax.fori_loop(0, 8, assemble, 0)
    for i, (a, c, y, n) in enumerate(YFACE):
        first, second = pick(yabove, PAD + y + 8, PAD + y - n)
        for e in range(2):
            for s in range(4):
                both[a][c, first, e, s, 0:4] = ya[i, e, s]
                both[a][c, second, e, s, 0:4] = yb[i, e, s]
    for copy in copies:
        copy.wait()
    for yside in range(2):
        for s in range(4):
            for d, (count, at, _) in CORNER.items():
                line, base = PAD + 7 + d if yside == 0 else PAD - d, (4 * yside + s) * CORNER_ROWS + at
                for side, part in enumerate(pick(zabove, ca[base : base + count, :], cb[base : base + count, :])):
                    for i, (a, c, dz) in enumerate(ZFACE[:count]):
                        e, row = halo_cell(side, dz)
                        both[a][c, line, e, s, row : row + 1] = part[i : i + 1]

    rows = iota(0)

    def far(zother, line, e, s):
        beyond = kx[1 - e, line - PAD, s : s + 1]
        return jnp.where(rows == (6 if e == 0 else 5), jnp.broadcast_to(beyond, (8, LANES)), zother)

    def prepare(c, line, parity, edge, keep):
        for e in range(2):
            q = (e + parity + c) % 2
            for s in range(4):
                centre, total = diagonal(k.at[c], k.at[1 - c], line, e, s, q, 4, edge)
                inside = centre != 0.0
                scale = jnp.where(inside, 1.0 / jnp.where(inside, total, 1.0), 0.0)
                start = 2.0 * f[c, line, e, s] * scale
                g[c, line, e, s] = scale
                fs[c, line, e, s] = start
                if keep:
                    half[line - PAD, e, s] = 0.5 * total
                if c == 0:
                    ur[line, e, s] = start
                    vr[line, e, s] = centre * start

    over_lines(-4, -1, PAD, lambda line, parity: prepare(0, line, parity, None, False))
    over_lines(8, 11, PAD, lambda line, parity: prepare(0, line, parity, None, False))
    over_lines(0, 7, PAD, lambda line, parity: prepare(0, line, parity, far, True))
    over_lines(-3, 10, PAD, lambda line, parity: prepare(1, line, parity, None, False))

    def relax(c, low, high):
        sweep(c, low, high, k, g, fs, (ur, ub), (vr, vb))

    relax(1, -3, 10)
    relax(0, -2, 9)
    relax(1, -1, 8)

    for row in range(4):
        for s in range(4):
            total = None
            for y in (2 * row, 2 * row + 1):
                for e in range(2):
                    line = PAD + y
                    value = red_residual(line, y % 2, e, s, k, g, fs, half, ur, ub, vb)
                    total = value if total is None else total + value
            put_coarse(coarse, row, s, total * 0.125, yc)

    first, second = pick(yup, PAD + 3, PAD)
    for i in range(5):
        for e in range(2):
            for s in range(4):
                at = ((i * 2 + e) * 4 + s) * 4
                yc[at : at + 4, :] = ub[first + i, e, s, 0:4]
                yd[at : at + 4, :] = ub[second + i, e, s, 0:4]


def widen_kernel(ub, yc_far, yd_far, zc, zd, faces, sem):
    zup, yabove = own_sides()
    slots, face = pick(yabove, 0, 1), pl.ds(0, FACE_ROWS)
    copies = [
        pltpu.make_async_copy(f.at[face], faces.at[t], sem.at[i]) for i, (f, t) in enumerate(zip((yc_far, yd_far), slots))
    ]
    for copy in copies:
        copy.start()

    def put(line, fetch):
        for target, up in ((zc, zup), (zd, jnp.logical_not(zup))):
            for d in range(1, DEPTHS[line] + 1):
                z = jnp.where(up, 8 - d, d - 1)
                for s in range(4):
                    at = ZSTARTS[line] + s * DEPTHS[line] + d - 1
                    target[at : at + 1, :] = fetch(lax.rem(z, 2), s, z // 2)

    for line in range(PAD, PAD + 8):
        put(line, lambda e, s, t: ub[line, e, s, pl.ds(t, 1)])
    for copy in copies:
        copy.wait()
    for i in range(5):
        for side, line in enumerate((PAD + 8 + i, i)):
            put(line, lambda e, s, t: faces[side, pl.ds(((i * 2 + e) * 4 + s) * 4 + t, 1), :])


def sweep(c, low, high, k, g, fs, u, v, edges=(None, None)):
    def visit(line, parity):
        for e in range(2):
            q = (e + parity + c) % 2
            for s in range(4):
                near = neighbours(u[1 - c], line, e, s, q, 4, edges[0])
                flow = neighbours(v[1 - c], line, e, s, q, 4, edges[1])
                centre = k[c, line, e, s]
                value = fs[c, line, e, s] + g[c, line, e, s] * (centre * near + flow)
                u[c][line, e, s] = value
                v[c][line, e, s] = centre * value

    over_lines(low, high, PAD, visit)


def red_residual(line, parity, e, s, k, g, fs, half, ur, ub, vb):
    q = (e + parity) % 2
    near = neighbours(ub, line, e, s, q, 4)
    flow = neighbours(vb, line, e, s, q, 4)
    fresh = fs[0, line, e, s] + g[0, line, e, s] * (k[0, line, e, s] * near + flow)
    return half[line - PAD, e, s] * (fresh - ur[line, e, s])


def up_kernel(
    k, g, fs, half, old, kx, yc, yd, zc, zd, error, errorx,
    correction, residual,
    ub, ur, vb, vr, ux, vx, natural,
):
    zabove, yabove = own_sides()
    for y in range(8):
        for e in range(2):
            for s in range(4):
                ub[PAD + y, e, s, 0:4] = old[PAD + y, e, s, 0:4]
    first, second = pick(yabove, PAD + 8, 0)
    for i in range(5):
        for e in range(2):
            for s in range(4):
                at = ((i * 2 + e) * 4 + s) * 4
                ub[first + i, e, s, 0:4] = yc[at : at + 4, :]
                ub[second + i, e, s, 0:4] = yd[at : at + 4, :]
    quiet = jnp.zeros((4, LANES), F32)
    for line, depth in enumerate(DEPTHS):
        for s in range(4):
            if depth < 4:
                for e in range(2):
                    ub[line, e, s, 4:8] = quiet
            if not depth:
                continue
            at = ZSTARTS[line] + s * depth
            for side, part in enumerate(pick(zabove, zc[at : at + depth, :], zd[at : at + depth, :])):
                for d in range(1, min(depth, 4) + 1):
                    e, row = halo_cell(side, d)
                    ub[line, e, s, row : row + 1] = part[d - 1 : d]
                if depth == 5:
                    y = line - PAD
                    beyond = kx[side, y, s : s + 1]
                    value = part[4:5] + errorx[side, y // 2, s : s + 1]
                    value = jnp.where(beyond != 0.0, value, 0.0)
                    ux[side, y, s : s + 1] = value
                    vx[side, y, s : s + 1] = beyond * value

    def add(line, parity):
        for e in range(2):
            for s in range(4):
                centre = k[1, line, e, s]
                value = ub[line, e, s] + error[(line + 1) // 2, s]
                value = jnp.where(centre != 0.0, value, 0.0)
                ub[line, e, s] = value
                vb[line, e, s] = centre * value

    over_lines(-5, 12, PAD, add)

    rows = iota(0)

    def far(ref):
        def edge(zother, line, e, s):
            beyond = ref[1 - e, line - PAD, s : s + 1]
            return jnp.where(rows == (6 if e == 0 else 5), jnp.broadcast_to(beyond, (8, LANES)), zother)

        return edge

    u, v = (ur, ub), (vr, vb)
    sweep(0, -4, -1, k, g, fs, u, v)
    sweep(0, 8, 11, k, g, fs, u, v)
    sweep(0, 0, 7, k, g, fs, u, v, (far(ux), far(vx)))
    sweep(1, -3, 10, k, g, fs, u, v)
    sweep(0, -2, 9, k, g, fs, u, v)
    sweep(1, -1, 8, k, g, fs, u, v)

    quiet = jnp.zeros((4, LANES), F32)
    for y in range(8):
        for e in range(2):
            at = pl.ds(y + 8 * e, 4, stride=16)
            q = (e + y) % 2
            for s in range(4):
                value = red_residual(PAD + y, y % 2, e, s, k, g, fs, half, ur, ub, vb)
                natural[1, 2 * s + q, at, :] = value[0:4]
                natural[1, 2 * s + 1 - q, at, :] = quiet
                natural[0, 2 * s + q, at, :] = ur[PAD + y, e, s, 0:4]
                natural[0, 2 * s + 1 - q, at, :] = ub[PAD + y, e, s, 0:4]
    for a, out in enumerate((correction, residual)):
        for z in range(8):
            tiles = join_lanes([natural[a, s, 8 * z : 8 * z + 8, :] for s in range(8)])
            for t in range(8):
                out[z, :, t * LANES : (t + 1) * LANES] = tiles[t]


def shifted(value, step, axis):
    size = value.shape[axis]
    where = iota(axis, value.shape[0])
    moved = pltpu.roll(value, -step % size, axis=axis)
    return jnp.where((where >= size - step) if step > 0 else (where < -step), 0.0, moved)


class Coarse:
    def __init__(self, nz, ny):
        self.nz, self.ny = nz, ny
        self.height, self.depth = 4 * ny, 2 * nz
        self.height2, self.height3 = self.height // 2, self.height // 4
        tile = (self.depth, LANES)
        self.lines, self.lines2 = (self.height + 2, 2, 2, *tile), (self.height2 + 2, *tile)
        self.flat2 = (2, self.height2, *tile)
        self.ready = ((2, *self.lines), (2, *self.lines), self.lines)
        self.ready += ((2, *self.lines2), self.flat2, self.flat2[1:])
        self.ready += ((self.height3, 6, *tile), (self.height3, *tile))

    def spread(self, sources, target, swaps):
        nz, ny = self.nz, self.ny
        zplace, yplace = lax.axis_index("gz"), lax.axis_index("gy")

        def slot(i, j):
            apart = (zplace * ny + yplace) ^ (i * ny + j)
            return sum(((apart >> step) & 1) << bit for bit, step in enumerate(swaps[:-1]))

        def run(odd):
            def visit(j, carry):
                order = [slot(i, j) for i in range(nz)]
                for m in range(8):
                    pieces = [sources[(i + odd) % 2][order[i], m] for i in range(nz)]
                    for row in range(4):
                        whole = jnp.concatenate([p[2 * row : 2 * row + 2] for p in pieces], axis=0)
                        target[m // 4, 1 + 4 * j + row, m // 2 % 2, m % 2] = whole
                return carry

            lax.fori_loop(0, ny, visit, 0)

        for odd in range(2):
            pl.when(lax.rem(zplace, 2) == odd)(lambda odd=odd: run(odd))

    def zero(self, c, y):
        even = iota(0, self.depth) % 2 == 0
        return even if (y + c) % 2 == 0 else jnp.logical_not(even)

    def around(self, ref, c, y):
        mid = ref[1 + y]
        other = jnp.where(self.zero(c, y), shifted(mid, -1, 1), shifted(mid, 1, 1))
        return (mid + other) + (shifted(mid, -1, 0) + shifted(mid, 1, 0)) + (ref[y] + ref[y + 2])

    def paired(self, a, b):
        total = (a + b) * 0.125
        even = iota(0, self.depth) % 2 == 0
        return jnp.where(even, total + pltpu.roll(total, self.depth - 1, axis=0), 0.0)


MOVES = ((-2, 0), (2, 0), (-1, 1), (1, 1))


def prepare_coarse(kmine, ktheirs, nz, ny):
    grid = Coarse(nz, ny)
    height, depth, height2, height3 = grid.height, grid.depth, grid.height2, grid.height3

    def body(kmine, ktheirs, k, g, half, kc, gc, hc, w3, g3, k2):
        grid.spread((kmine, ktheirs), k, swap_steps(nz, ny))
        blank = jnp.zeros((depth, LANES), F32)
        for c in range(2):
            for line in (0, height + 1):
                for e in range(2):
                    for s in range(2):
                        k[c, line, e, s] = blank
            for line in (0, height2 + 1):
                kc[c, line] = blank

        def prepare(line, parity):
            for c in range(2):
                for e in range(2):
                    for s in range(2):
                        _, total = diagonal(k.at[c], k.at[1 - c], line, e, s, (e + parity + c) % 2, 2, closed)
                        g[c, line, e, s] = 1.0 / total
                        if c == 0:
                            half[line, e, s] = 0.125 * total

        over_lines(0, height - 1, 1, prepare, 4)

        def restrict(i, carry):
            for s in range(2):
                total = None
                for j in range(2):
                    for e in range(2):
                        part = k[0, 1 + 2 * i + j, e, s] + k[1, 1 + 2 * i + j, e, s]
                        total = part if total is None else total + part
                k2[s, i] = total * 0.125
            return carry

        lax.fori_loop(0, height2, restrict, 0)
        for c in range(2):
            for y in range(height2):
                kc[c, 1 + y] = jnp.where(grid.zero(c, y), k2[0, y], k2[1, y])
        for c in range(2):
            for y in range(height2):
                total = 6.0 * kc[c, 1 + y] + grid.around(kc.at[1 - c], c, y)
                gc[c, y] = 1.0 / total
                if c == 0:
                    hc[y] = total * (0.5 / 16.0)
        conduct = []
        for y in range(height3):
            conduct.append(grid.paired(*[kc[0, 1 + 2 * y + j] + kc[1, 1 + 2 * y + j] for j in range(2)]))
        even = iota(0, depth) % 2 == 0
        lane, row = iota(1, depth), iota(0, depth)
        open_faces = (row >= 2, row < depth - 2, lane >= 1, lane < LANES - 1)
        for y in range(height3):
            centre = conduct[y]
            beside = [shifted(centre, step, axis) for step, axis in MOVES]
            beside.append(conduct[y - 1] if y else jnp.zeros_like(centre))
            beside.append(conduct[y + 1] if y + 1 < height3 else jnp.zeros_like(centre))
            total = 6.0 * centre
            for part in beside:
                total = total + part
            scale = jnp.where(even, 1.0 / jnp.where(even, total, 1.0), 0.0)
            g3[y] = scale
            for i in range(6):
                weight = (centre + beside[i]) * scale
                w3[y, i] = jnp.where(open_faces[i], weight, 0.0) if i < 4 else weight

    return call(body, 4, grid.ready, [grid.flat2], kmine, ktheirs)


def coarse_kernel(nz, ny):
    grid = Coarse(nz, ny)
    height, depth, height2, height3 = grid.height, grid.depth, grid.height2, grid.height3

    def body(
        fmine, ftheirs, k, g, half, kc, gc, hc, w3, g3, error, errorx,
        f, fs, ur, ub, vr, vb, f2, fc, sc, uc, vc, f3,
    ):
        u, v = (ur, ub), (vr, vb)
        zplace, yplace = lax.axis_index("gz"), lax.axis_index("gy")
        grid.spread((fmine, ftheirs), f, swap_steps(nz, ny, 0))
        blank = jnp.zeros((depth, LANES), F32)
        for line in (0, height + 1):
            for e in range(2):
                for s in range(2):
                    for c in range(2):
                        u[c][line, e, s] = blank
                        v[c][line, e, s] = blank

        def begin(line, parity):
            for e in range(2):
                for s in range(2):
                    start = 8.0 * f[0, line, e, s] * g[0, line, e, s]
                    fs[0, line, e, s] = start
                    ur[line, e, s] = start
                    vr[line, e, s] = k[0, line, e, s] * start
                    fs[1, line, e, s] = 8.0 * f[1, line, e, s] * g[1, line, e, s]

        over_lines(0, height - 1, 1, begin, 8)

        def fresh(c, line, parity, e, s):
            q = (e + parity + c) % 2
            near = neighbours(u[1 - c], line, e, s, q, 2, closed)
            flow = neighbours(v[1 - c], line, e, s, q, 2, closed)
            return fs[c, line, e, s] + g[c, line, e, s] * (k[c, line, e, s] * near + flow)

        def relax(c):
            def visit(line, parity):
                for e in range(2):
                    for s in range(2):
                        value = fresh(c, line, parity, e, s)
                        u[c][line, e, s] = value
                        v[c][line, e, s] = k[c, line, e, s] * value

            over_lines(0, height - 1, 1, visit, 8)

        relax(1)
        relax(0)
        relax(1)

        def restrict(line, parity):
            i = (line - 1) // 2
            for s in range(2):
                value = None
                for j in range(2):
                    for e in range(2):
                        at = 1 + 2 * i + j
                        part = half[at, e, s] * (fresh(0, at, j, e, s) - ur[at, e, s])
                        value = part if value is None else value + part
                f2[s, i] = value * 0.125

        def restrict_pairs(i, carry):
            for j in range(2):
                restrict(1 + 2 * (2 * i + j), 0)
            return carry

        lax.fori_loop(0, height2 // 2, restrict_pairs, 0)

        for c in range(2):
            for line in (0, height2 + 1):
                uc[c, line] = blank
                vc[c, line] = blank
            for y in range(height2):
                right = jnp.where(grid.zero(c, y), f2[0, y], f2[1, y])
                start = 32.0 * right * gc[c, y]
                sc[c, y] = start
                if c == 0:
                    uc[0, 1 + y] = start
                    vc[0, 1 + y] = kc[0, 1 + y] * start

        def fresh2(c, y):
            flow = kc[c, 1 + y] * grid.around(uc.at[1 - c], c, y) + grid.around(vc.at[1 - c], c, y)
            return sc[c, y] + gc[c, y] * flow

        def relax2(c):
            for y in range(height2):
                value = fresh2(c, y)
                uc[c, 1 + y] = value
                vc[c, 1 + y] = kc[c, 1 + y] * value

        relax2(1)
        relax2(0)
        relax2(1)

        for y in range(height3):
            parts = [hc[2 * y + j] * (fresh2(0, 2 * y + j) - uc[0, 1 + 2 * y + j]) for j in range(2)]
            f3[y] = 128.0 * grid.paired(*parts) * g3[y]
        mixed = (iota(0, depth) // 2 + iota(1, depth)) % 2

        def relax3(c, field):
            result = []
            for y in range(height3):
                mid = field[y]
                value = f3[y]
                for i, (step, axis) in enumerate(MOVES):
                    value = value + w3[y, i] * pltpu.roll(mid, -step % mid.shape[axis], axis=axis)
                if y:
                    value = value + w3[y, 4] * field[y - 1]
                if y + 1 < height3:
                    value = value + w3[y, 5] * field[y + 1]
                result.append(jnp.where(mixed == (y + c) % 2, value, mid))
            return result

        def two_colours(_, field):
            return tuple(relax3(1, relax3(0, list(field))))

        field = lax.fori_loop(0, 12, two_colours, (blank,) * height3)

        for y in range(height2):
            coarse = field[y // 2]
            value = uc[1, 1 + y] + (coarse + pltpu.roll(coarse, 1, axis=0))
            uc[1, 1 + y] = value
            vc[1, 1 + y] = kc[1, 1 + y] * value
        for c in (0, 1, 0, 1):
            relax2(c)

        for y in range(height2):
            zero = grid.zero(0, y)
            red, black = uc[0, 1 + y], uc[1, 1 + y]
            f2[0, y] = jnp.where(zero, red, black)
            f2[1, y] = jnp.where(zero, black, red)

        def add(line, parity):
            for e in range(2):
                for s in range(2):
                    value = ub[line, e, s] + f2[s, (line - 1) // 2]
                    ub[line, e, s] = value
                    vb[line, e, s] = k[1, line, e, s] * value

        over_lines(0, height - 1, 1, add, 8)
        for c in (0, 1, 0, 1):
            relax(c)

        for j in range(-3, 7):
            line = 1 + jnp.clip(4 * yplace + j, 0, height - 1)
            for t in range(-3, 7):
                e = t % 2
                at = pl.ds(jnp.clip(2 * zplace + t // 2, 0, depth - 1), 1)
                for s in range(4):
                    row = u[(s + e + j) % 2][line, e, s // 2, at, :]
                    if -2 <= t <= 5:
                        error[j + 3, s, t % 8 : t % 8 + 1, :] = row
                    elif 0 <= j < 8 // 2:
                        errorx[1 if t < 0 else 0, j, s : s + 1, :] = row

    lines, lines2, flat2 = grid.lines, grid.lines2, grid.flat2
    scratch = [(2, *lines), (2, *lines), *[lines] * 4, flat2, flat2, flat2, (2, *lines2), (2, *lines2)]
    return body, scratch + [(height3, depth, LANES)]


def swap_steps(nz, ny, first=None):
    ybits, zbits = ny.bit_length() - 1, nz.bit_length() - 1
    along_y = list(range(ybits - 1, -1, -1))
    if first is not None:
        along_y = [first, *(bit for bit in along_y if bit != first)]
    return [*along_y, *range(ybits + zbits - 1, ybits - 1, -1)]


def swap(block, step, nz, ny):
    return lax.ppermute(block, ("gz", "gy"), [(i, i ^ (1 << step)) for i in range(nz * ny)])


def swapped(block, step, nz, ny):
    return jnp.concatenate([block, swap(block, step, nz, ny)])


def solve_coarse(fmine, ftheirs, ready, nz, ny):
    body, scratch = coarse_kernel(nz, ny)
    outs = ((10, 4, 8, LANES), (2, 4, 4, LANES))
    return call(body, 8, outs, scratch, fmine, ftheirs, *ready)


def extended(array, sides, width):
    for axis, dim in sides:
        size, length = (lax.axis_size(axis), array.shape[dim])
        up = [(i, (i + 1) % size) for i in range(size - 1)]
        down = [(j, i) for i, j in up]
        last = lax.slice_in_dim(array, length - width, length, axis=dim)
        initial = lax.slice_in_dim(array, 0, width, axis=dim)
        before = lax.ppermute(last, axis, up)
        after = lax.ppermute(initial, axis, down)
        array = jnp.concatenate([before, array, after], axis=dim)
    return array


def coarsen(field):
    total = field[0::2, 0::2, 0::2] + field[0::2, 0::2, 1::2]
    total = total + field[0::2, 1::2, 0::2] + field[0::2, 1::2, 1::2]
    total = total + field[1::2, 0::2, 0::2] + field[1::2, 0::2, 1::2]
    total = total + field[1::2, 1::2, 0::2] + field[1::2, 1::2, 1::2]
    return total * 0.125


def prolong(field):
    return jnp.repeat(jnp.repeat(jnp.repeat(field, 2, axis=0), 2, axis=1), 2, axis=2)


def face_terms(kpad):
    center = kpad[1:-1, 1:-1, 1:-1]
    z_minus = 0.5 * (center + kpad[:-2, 1:-1, 1:-1])
    z_plus = 0.5 * (center + kpad[2:, 1:-1, 1:-1])
    y_minus = 0.5 * (center + kpad[1:-1, :-2, 1:-1])
    y_plus = 0.5 * (center + kpad[1:-1, 2:, 1:-1])
    x_minus = 0.5 * (center + kpad[1:-1, 1:-1, :-2])
    x_plus = 0.5 * (center + kpad[1:-1, 1:-1, 2:])
    total = z_minus + z_plus + y_minus + y_plus + x_minus + x_plus
    return ((z_minus, z_plus, y_minus, y_plus, x_minus, x_plus), total)


def neighbour_sum(weights, upad):
    z_minus, z_plus, y_minus, y_plus, x_minus, x_plus = weights
    acc = z_minus * upad[:-2, 1:-1, 1:-1] + z_plus * upad[2:, 1:-1, 1:-1]
    acc = acc + y_minus * upad[1:-1, :-2, 1:-1] + y_plus * upad[1:-1, 2:, 1:-1]
    acc = acc + x_minus * upad[1:-1, 1:-1, :-2] + x_plus * upad[1:-1, 1:-1, 2:]
    return acc


def extend(field, layout):
    if layout == "column":
        wider = extended(field, (("gy", 1),), 1)
        wider = jnp.pad(wider, ((1, 1), (0, 0), (0, 0)))
    else:
        wider = extended(field, (("gz", 0), ("gy", 1)), 1)
    return jnp.pad(wider, ((0, 0), (0, 0), (1, 1)))


def region_masks(shape, z_start, y_start):
    zpos = lax.broadcasted_iota(jnp.int32, shape, 0) + z_start
    ypos = lax.broadcasted_iota(jnp.int32, shape, 1) + y_start
    xpos = lax.broadcasted_iota(jnp.int32, shape, 2)
    return (zpos + ypos + xpos + 4) % 2


def cycle(rhs, conduct, level, layout, z_start, y_start, z_total, y_total):
    scale = 4.0**level
    weights, total = face_terms(extend(conduct, layout))
    parity = region_masks(rhs.shape, z_start, y_start)
    first = parity == 0
    second = parity == 1

    def relax(field, colour):
        fresh = (scale * rhs + neighbour_sum(weights, extend(field, layout))) / total
        return jnp.where(colour, fresh, field)

    def smooth(field, sweeps):
        for sweep in range(sweeps):
            for colour in (first, second):
                field = relax(field, colour)
        return field

    def remainder(field):
        return rhs - (total * field - neighbour_sum(weights, extend(field, layout))) / scale

    field = jnp.zeros(rhs.shape, jnp.float32)
    if level == LEVELS - 1:
        return (smooth(field, 12), None)
    field = smooth(field, 2)
    rhs_next = coarsen(remainder(field))
    conduct_next = coarsen(conduct)
    joined = layout == "split" and level == 1
    if joined:
        local_depth = rhs_next.shape[0]
        rhs_next, conduct_next = (
            lax.all_gather(rhs_next, "gz", axis=0, tiled=True),
            lax.all_gather(conduct_next, "gz", axis=0, tiled=True),
        )
        error, unused = cycle(
            rhs_next, conduct_next, level + 1, "column", 0, y_start // 2, z_total // 2, y_total // 2
        )
        error = lax.dynamic_slice_in_dim(error, lax.axis_index("gz") * local_depth, local_depth, 0)
    else:
        error, unused = cycle(
            rhs_next,
            conduct_next,
            level + 1,
            layout,
            z_start // 2,
            y_start // 2,
            z_total // 2,
            y_total // 2,
        )
    field = field + prolong(error)
    field = smooth(field, 2)
    return (field, remainder(field))


def natural_coarse(message):
    packed = message.reshape(2, 2, 2, 4, 2, LANES)
    parity = (jnp.arange(2)[:, None, None, None, None] + jnp.arange(4)[None, None, :, None, None]) % 2 == 0
    even = jnp.where(parity, packed[0], packed[1])
    odd = jnp.where(parity, packed[1], packed[0])
    both = jnp.stack([even, odd])
    return both.transpose(4, 1, 3, 5, 2, 0).reshape(4, 4, 4 * LANES)


def solve_coarse_spread(message, kmessage, nz, ny):
    z_start, y_start = 4 * lax.axis_index("gz"), 4 * lax.axis_index("gy")
    field, unused = cycle(
        natural_coarse(message), natural_coarse(kmessage), 1, "split", z_start, y_start, 4 * nz, 4 * ny
    )
    wide = extended(field, (("gz", 0), ("gy", 1)), 3).reshape(10, 10, LANES, 4).transpose(1, 3, 0, 2)
    error = jnp.concatenate([wide[:, :, 3:9], wide[:, :, 1:3]], axis=2)
    return error, jnp.stack([wide[3:7, :, 9], wide[3:7, :, 0]])


def exchange(first, second, axis):
    size = lax.axis_size(axis)
    results = []
    for message, start in ((first, 0), (second, 1)):
        pairs = [(i, i + 1) for i in range(start, size - 1, 2)]
        results.append(lax.ppermute(message, axis, pairs + [(j, i) for i, j in pairs]))
    return results


def on_device(right_side, coefficient):
    nz, ny = lax.axis_size("gz"), lax.axis_size("gy")
    assert right_side.shape == (8, 8, 8 * LANES)
    cells = (2, 2, 8, 2, 4, 4, LANES)
    yface, zface = (16, 2, 4, 4, LANES), (8, 4, 16, LANES)
    coarse = (8, 8, LANES)
    packed = call(pack_kernel, 3, (cells, yface, yface), [(2, 8, 64, LANES)], right_side, coefficient)
    local, ya, yb = packed
    ya, yb = exchange(ya, yb, "gy")
    za, zb, kmessage = call(zpack_kernel, 2, (zface, zface, coarse), [], local)
    za, zb = exchange(za, zb, "gz")
    coarse_cells = 8 * 8 * LANES
    whole = nz * ny * coarse_cells <= WHOLE_COARSE_CELLS and nz & (nz - 1) == 0 and ny & (ny - 1) == 0
    swaps, kswaps = swap_steps(nz, ny, 0), swap_steps(nz, ny)
    kall = kmessage[None]
    if whole:
        kall = swapped(kall, kswaps[0], nz, ny)
        ya, yb, kall = lax.optimization_barrier((ya, yb, kall))
    relayed, sems = (8 * CORNER_ROWS, LANES), pltpu.SemaphoreType.DMA((2,))
    corners = call(relay_kernel, 2, (relayed, relayed), [(2, *yface), sems], ya, yb, specs=[FAR] * 2)
    ca, cb = exchange(*corners, "gz")
    if whole:
        for step in kswaps[1:-3]:
            kall = swapped(kall, step, nz, ny)
    lines, face = (LINES, 2, 4, 8, LANES), (FACE_ROWS, LANES)
    outs = ((2, *lines), (2, *lines), (2, *lines), (8, *lines[1:]), lines, (2, 8, 4, LANES))
    outs += ((FACE_ROWS + 64, LANES), face, coarse)
    scratch = [(2, *lines), lines, lines, lines, relayed, relayed, sems]
    k, g, fs, half, ub, kx, yc, yd, message = call(
        down_kernel, 6, outs, scratch, local, ya, yb, za, zb, ca, cb, specs=[VMEM] * 5 + [FAR] * 2
    )
    if whole:
        yc, kall = lax.optimization_barrier((yc, kall))
    yc, yd = exchange(yc, yd, "gy")
    if whole:
        fall = jnp.stack([message, yc[FACE_ROWS:].reshape(message.shape)])
        kall = swapped(kall, kswaps[-3], nz, ny)
        fall = swapped(fall, swaps[1], nz, ny)
        fall, kall, yc, yd = lax.optimization_barrier((fall, kall, yc, yd))
        kall = swapped(kall, kswaps[-2], nz, ny)
        for step in swaps[2:-2]:
            fall = swapped(fall, step, nz, ny)
    zface = (ZROWS, LANES)
    zc, zd = call(widen_kernel, 1, (zface, zface), [(2, *face), sems], ub, yc, yd, specs=[VMEM, FAR, FAR])
    if whole:
        fall, zc, zd = lax.optimization_barrier((fall, zc, zd))
    zc, zd = exchange(zc, zd, "gz")
    if whole:
        fall = swapped(fall, swaps[-2], nz, ny)
        ktheirs = swap(kall, kswaps[-1], nz, ny)
        ready = prepare_coarse(kall, ktheirs, nz, ny)
        fall, zc, zd, *ready = lax.optimization_barrier((fall, zc, zd, *ready))
        ftheirs = swap(fall, swaps[-1], nz, ny)
        error, errorx = solve_coarse(fall, ftheirs, ready, nz, ny)
    else:
        error, errorx = solve_coarse_spread(message, kmessage, nz, ny)
    block = (8, 8, 8 * LANES)
    scratch = [lines] * 4 + [(2, 8, 4, LANES)] * 2 + [(2, 8, 64, LANES)]
    return call(up_kernel, 6, (block, block), scratch, k, g, fs, half, ub, kx, yc, yd, zc, zd, error, errorx)


def solution(mesh):
    spec = P("gz", "gy", None)
    return jax.shard_map(
        on_device, mesh=mesh, in_specs=(spec, spec), out_specs=(spec, spec), check_vma=False
    )
```
